32 devices in a mesh: dp: 8 (over z, x), seq: 4 (over y, core).
Axes of the slice: x: 2, y: 2, z: 4, core: 2. Of those that a mesh axis runs over, the one named last changes fastest.
Arguments:
- tokens: bfloat16 [16, 1024, 768], P('dp', 'seq'), may hold values from -6 to 6
- gain_one: float32 [768], replicated, may hold values from 0.25 to 1.75
- shift_one: float32 [768], replicated, may hold values from -3 to 3
- w_query: bfloat16 [768, 768], replicated, may hold values from -0.3125 to 0.3125
- w_key: bfloat16 [768, 768], replicated, may hold values from -0.3125 to 0.3125
- w_value: bfloat16 [768, 768], replicated, may hold values from -0.21875 to 0.21875
- w_out: bfloat16 [768, 768], replicated, may hold values from -0.875 to 0.875
- gain_two: float32 [768], replicated, may hold values from 0.25 to 1.75
- shift_two: float32 [768], replicated, may hold values from -3 to 3
- w_up: bfloat16 [768, 3072], replicated, may hold values from -0.21875 to 0.21875
- w_down: bfloat16 [3072, 768], replicated, may hold values from -0.15625 to 0.15625
- cotangent: bfloat16 [16, 1024, 768], P('dp', 'seq'), may hold values from -6 to 6
- lengths: int32 [16], P('dp'), may hold values from 102 to 1024, as said below
Outputs:
- output: bfloat16 [16, 1024, 768], P('dp', 'seq')
- grad_tokens: bfloat16 [16, 1024, 768], P('dp', 'seq')
- grad_gain_one: float32 [768], replicated
- grad_shift_one: float32 [768], replicated
- grad_w_query: float32 [768, 768], P('dp', 'seq')
- grad_w_key: float32 [768, 768], P('dp', 'seq')
- grad_w_value: float32 [768, 768], P('dp', 'seq')
- grad_w_out: float32 [768, 768], P('dp', 'seq')
- grad_gain_two: float32 [768], replicated
- grad_shift_two: float32 [768], replicated
- grad_w_up: float32 [768, 3072], P('dp', 'seq')
- grad_w_down: float32 [3072, 768], P('dp', 'seq')
The draws below stay inside these ranges and needn't reach their ends.
Inputs may be any that keep to these rules, and one draw needn't show every extreme that they name: `lengths`: in every aligned block of 4 rows one row, at a place drawn from the seed, has length 1024; the others lean toward short rows.
All inputs are finite; a program needn't handle non-finite values.
Results may differ from the reference program's by a relative error of at most 0.017.
Values may be sent and summed in bfloat16 or wider, within the bound.
No kernel may reach another device: no remote copies, remote signals or barrier semaphores. Data moves between devices by JAX's collectives and lax.ppermute only.
A program may use at most 128 MiB of HBM per device.

```python
import jax
import jax.numpy as jnp
from jax import lax

D = 768
HD = 64
FF = 3072
L = 1024
ROWS_DEV = 2
ROWS = 16
N_DP = 8


def draw_lengths(key, part):
    key = jax.random.fold_in(key, 7)
    first_key, second_key, third_key, place_key = jax.random.split(key, 4)
    lowest = max(L // 10, 1)
    draw_one = jax.random.randint(first_key, (ROWS,), lowest, L + 1)
    draw_two = jax.random.randint(second_key, (ROWS,), lowest, L + 1)
    draw_three = jax.random.randint(third_key, (ROWS,), lowest, L + 1)
    shortest = jnp.minimum(jnp.minimum(draw_one, draw_two), draw_three)
    chosen = jax.random.randint(place_key, (ROWS // 4,), 0, 4)
    slots = jnp.arange(ROWS, dtype=jnp.int32).reshape(ROWS // 4, 4)
    longest = (slots % 4 == chosen[:, None]).reshape(ROWS)
    return jnp.where(longest, L, shortest).astype(jnp.int32)


def steps_of(rng, dims, cuts, least, top_value):
    def one(axis_at, parts):
        heights = jax.random.uniform(jax.random.fold_in(jax.random.fold_in(rng, 6), axis_at), (parts,), jnp.float32, least / len(cuts), top_value / len(cuts))
        return jnp.repeat(jnp.exp(heights), dims[axis_at] // parts).reshape((-1,) + (1,) * (len(dims) - axis_at - 1))

    loudness = one(*cuts[0])
    for cut in cuts[1:]:
        loudness = loudness * one(*cut)
    return loudness


def normal_values(rng, dims, deviation, limit, cuts=(), kind=jnp.bfloat16):
    values = deviation * jax.random.normal(rng, dims, jnp.float32)
    if cuts:
        values = values * steps_of(rng, dims, cuts, -0.22, 0.18)
    return jnp.clip(values, -limit, limit).astype(kind)


def setup_inputs(seed: int = 0) -> dict:
    arg_keys = jax.random.split(jax.random.key(seed), 14)
    tokens = normal_values(arg_keys[0], (ROWS, L, D), 1.0, 6.0, ((0, 8), (1, 4)))
    gain_one = jnp.clip(1.0 + 0.15 * jax.random.normal(arg_keys[1], (D,), jnp.float32), 0.25, 1.75)
    shift_one = normal_values(arg_keys[2], (D,), 0.5, 3.0, (), jnp.float32)
    w_query = normal_values(arg_keys[3], (D, D), (D // 2) ** -0.5, 0.3125)
    w_key = normal_values(arg_keys[4], (D, D), (D // 2) ** -0.5, 0.3125)
    w_value = normal_values(arg_keys[5], (D, D), D ** -0.5, 0.21875)
    w_out = normal_values(arg_keys[6], (D, D), (D // 16) ** -0.5, 0.875)
    gain_two = jnp.clip(1.0 + 0.15 * jax.random.normal(arg_keys[7], (D,), jnp.float32), 0.25, 1.75)
    shift_two = normal_values(arg_keys[8], (D,), 0.5, 3.0, (), jnp.float32)
    w_up = normal_values(arg_keys[9], (D, FF), D ** -0.5, 0.21875)
    w_down = normal_values(arg_keys[10], (FF, D), (FF // 2) ** -0.5, 0.15625)
    cotangent = normal_values(arg_keys[11], (ROWS, L, D), 1.0, 6.0, ((0, 8), (1, 4)))
    lengths = draw_lengths(jax.random.fold_in(arg_keys[13], 71), 0)
    return dict(tokens=tokens, gain_one=gain_one, shift_one=shift_one, w_query=w_query, w_key=w_key, w_value=w_value, w_out=w_out, gain_two=gain_two, shift_two=shift_two, w_up=w_up, w_down=w_down, cotangent=cotangent, lengths=lengths)


@jax.custom_vjp
def low(v):
    return lax.optimization_barrier(v.astype(jnp.bfloat16)).astype(jnp.float32)

@jax.custom_vjp
def low_back(v):
    return v

def low_keep(v):
    return (low(v), None)

def low_pass(kept, grad):
    return (grad,)

def back_keep(v):
    return (v, None)

def back_low(kept, grad):
    return (low(grad),)
low.defvjp(low_keep, low_pass)
low_back.defvjp(back_keep, back_low)
EPSILON = 1e-05
MASKED = -1000000000.0

def layer_norm(values, gain, shift):
    average = lax.optimization_barrier(jnp.mean(values, axis=-1, keepdims=True))
    centred = values - average
    variance = lax.optimization_barrier(jnp.mean(centred * centred, axis=-1, keepdims=True))
    return centred * lax.rsqrt(variance + EPSILON) * gain + shift

def rotary_tables(offset, number, head_dim):
    halfway = head_dim // 2
    frequency = 10000.0 ** (-2.0 * jnp.arange(halfway, dtype=jnp.float32) / head_dim)
    places = (offset + jnp.arange(number, dtype=jnp.int32)).astype(jnp.float32)
    angles = places[:, None] * frequency[None, :]
    return (jnp.cos(angles), jnp.sin(angles))

def rotate(values, cosine, sine_table):
    halfway = values.shape[-1] // 2
    leading = values[..., :halfway]
    trailing = values[..., halfway:]
    cosine = cosine[:, None, :]
    sine_table = sine_table[:, None, :]
    return jnp.concatenate([leading * cosine - trailing * sine_table, trailing * cosine + leading * sine_table], axis=-1)

def matmul(left, right):
    return jnp.dot(left, right, precision=lax.Precision.HIGHEST)

def layer_block(params, inputs, keeping):
    gain_one, shift_one, w_query, w_key, w_value, w_out, gain_two, shift_two, w_up, w_down = params
    row_count, length, model_width = inputs.shape
    head_count = model_width // HD
    score_scale = HD ** (-0.5)
    flattened = inputs.reshape(row_count * length, model_width)
    normed = low(layer_norm(flattened, gain_one, shift_one))
    cosine, sine_table = rotary_tables(0, length, HD)
    shaped = (row_count, length, head_count, HD)
    queries = rotate(low_back(matmul(normed, w_query)).reshape(shaped), cosine, sine_table)
    key_all = rotate(low_back(matmul(normed, w_key)).reshape(shaped), cosine, sine_table)
    queries = low(low_back(queries))
    key_all = low(low_back(key_all))
    value_all = low(low_back(matmul(normed, w_value))).reshape(shaped)

    def attend(pieces):
        query_row, key_row, value_row, keep_row = pieces
        scores = low_back(jnp.einsum('qhd,khd->hqk', query_row, key_row, precision=lax.Precision.HIGHEST) * score_scale)
        scores = jnp.where(keep_row[None, None, :], scores, MASKED)
        attn_weights = jax.nn.softmax(scores, axis=-1)
        return jnp.einsum('hqk,khd->qhd', low(attn_weights), value_row, precision=lax.Precision.HIGHEST)
    context = lax.map(jax.checkpoint(attend), (queries, key_all, value_all, keeping))
    context = low(low_back(context.reshape(row_count * length, model_width)))
    residual = flattened + low_back(matmul(context, w_out))
    normed_two = low(layer_norm(residual, gain_two, shift_two))
    hidden = low_back(matmul(normed_two, w_up))
    active = low(jax.nn.gelu(hidden, approximate=True))
    row_mask = keeping.reshape(row_count * length, 1).astype(jnp.float32)
    result = (residual + low_back(matmul(active, w_down))) * row_mask
    return result.reshape(row_count, length, model_width)

def reference(tokens, gain_one, shift_one, w_query, w_key, w_value, w_out, gain_two, shift_two, w_up, w_down, cotangent, lengths):
    params = tuple((element.astype(jnp.float32) for element in (gain_one, shift_one, w_query, w_key, w_value, w_out, gain_two, shift_two, w_up, w_down)))
    shaped = (N_DP, ROWS_DEV, L, D)
    inputs = tokens.astype(jnp.float32).reshape(shaped)
    places = jnp.arange(L, dtype=jnp.int32)
    keeping = (places[None, :] < lengths[:, None]).reshape(N_DP, ROWS_DEV, L)

    def whole_layer(params, inputs):

        def by_group(carried, pieces):
            return (carried, jax.checkpoint(layer_block)(params, pieces[0], pieces[1]))
        unused, stacked = lax.scan(by_group, jnp.zeros((), jnp.float32), (inputs, keeping))
        return stacked
    output, pullback = jax.vjp(whole_layer, params, inputs)
    grad_params, grad_inputs = pullback(cotangent.astype(jnp.float32).reshape(shaped))
    g_gain_one, g_shift_one, g_query, g_key, g_value, g_out, g_gain_two, g_shift_two, g_up, g_down = grad_params
    return (output.reshape(ROWS, L, D).astype(jnp.bfloat16), grad_inputs.reshape(ROWS, L, D).astype(jnp.bfloat16), g_gain_one, g_shift_one, g_query, g_key, g_value, g_out, g_gain_two, g_shift_two, g_up, g_down)
```

```python
import functools

import jax
import jax.numpy as jnp
from jax import lax
from jax.experimental import pallas as pl
from jax.experimental.pallas import tpu as pltpu
from jax.sharding import PartitionSpec as P

HD = 64
EPSILON = 1e-05
MASKED = -1000000000.0
LANES = 128
BF16 = jnp.bfloat16
F32 = jnp.float32
VMEM_BYTES = 56 * 1024 * 1024


def swap(values, axis, bit):
    count = lax.axis_size(axis)
    return lax.ppermute(values, axis, [(i, i ^ bit) for i in range(count)])


def pick(values, index, axis=0):
    return lax.dynamic_index_in_dim(values, index, axis, keepdims=False)


def dot(left, right):
    return jnp.dot(left, right, preferred_element_type=F32)


def dot_back(left, right):
    return lax.dot_general(left, right, (((1,), (1,)), ((), ())), preferred_element_type=F32)


def outer_sum(left, right):
    return lax.dot_general(left, right, (((0,), (0,)), ((), ())), preferred_element_type=F32)


def normalize(values):
    average = jnp.mean(values, axis=-1, keepdims=True)
    centred = values - average
    variance = jnp.mean(centred * centred, axis=-1, keepdims=True)
    inverse = lax.rsqrt(variance + EPSILON)
    return centred * inverse, inverse


def norm_back(grad, gain, normal, inverse):
    scaled = grad * gain
    first = jnp.mean(scaled, axis=-1, keepdims=True)
    second = jnp.mean(scaled * normal, axis=-1, keepdims=True)
    return (scaled - first - normal * second) * inverse


def swap_halves(values):
    lane = lax.broadcasted_iota(jnp.int32, values.shape, 1)
    up = pltpu.roll(values, LANES - HD // 2, 1)
    down = pltpu.roll(values, HD // 2, 1)
    return jnp.where(lane % HD < HD // 2, up, down)


def params(**kinds):
    return pltpu.CompilerParams(vmem_limit_bytes=VMEM_BYTES, **kinds)


def cost(flops, bytes_accessed, transcendentals=0):
    return pl.CostEstimate(
        flops=int(flops), bytes_accessed=int(bytes_accessed), transcendentals=int(transcendentals)
    )


def whole(shape):
    return pl.BlockSpec(shape, lambda *_: (0,) * len(shape))


def project_kernel(
    mine_ref, other_ref, gain_ref, shift_ref, weight_ref, cos_ref, sin_ref, *rest, score_scale
):
    qkv_ref, normed_ref = rest[-2:]
    step = pl.program_id(0)
    values = jnp.where(step == 0, mine_ref[...], other_ref[...]).astype(F32)
    normal, _ = normalize(values)
    normed = (normal * gain_ref[...] + shift_ref[...]).astype(BF16)
    normed_ref[...] = normed
    width = weight_ref.shape[1] // 3
    cosine, sine = cos_ref[...], sin_ref[...]
    for part in range(3):
        out = dot(normed, weight_ref[:, part * width : (part + 1) * width])
        for pair in range(width // LANES):
            piece = out[:, pair * LANES : (pair + 1) * LANES]
            if part < 2:
                piece = piece * cosine + swap_halves(piece) * sine
                if part == 0:
                    piece = piece * score_scale
            start = part * width + pair * LANES
            qkv_ref[:, start : start + LANES] = piece.astype(BF16)


def project_call(call, mine, other, gain, shift, weight, cosine, sine, previous):
    rows, width = mine.shape
    out_width = weight.shape[1]
    total = 4 * rows
    row_block = lambda i: (2 * i + call, 0)
    in_specs = [
        whole((rows, width)),
        whole((rows, width)),
        whole((1, width)),
        whole((1, width)),
        whole((width, out_width)),
        pl.BlockSpec((rows, LANES), row_block),
        pl.BlockSpec((rows, LANES), row_block),
    ]
    aliases = {}
    if previous:
        in_specs += [pl.BlockSpec(memory_space=pl.ANY)] * 2
        aliases = {7: 0, 8: 1}
    return pl.pallas_call(
        functools.partial(project_kernel, score_scale=HD ** (-0.5)),
        grid=(2,),
        in_specs=in_specs,
        out_specs=[
            pl.BlockSpec((rows, out_width), row_block),
            pl.BlockSpec((rows, width), row_block),
        ],
        out_shape=[
            jax.ShapeDtypeStruct((total, out_width), BF16),
            jax.ShapeDtypeStruct((total, width), BF16),
        ],
        input_output_aliases=aliases,
        compiler_params=params(),
        cost_estimate=cost(4 * rows * width * out_width, 6e6),
    )(mine, other, gain, shift, weight, cosine, sine, *previous)


def augment(lane, head, keys, bias):
    return jnp.where(lane == (HD if head == 0 else 0), bias, keys)


def only_head(lane, head, values):
    return jnp.where(lane // HD == head, values, jnp.zeros_like(values))


def with_one(lane, head, values):
    return jnp.where(
        lane == (HD if head == 0 else 0),
        jnp.ones_like(values),
        only_head(lane, head, values),
    )


def attend_kernel(query_ref, key_ref, value_ref, bias_ref, mine_ref, other_ref, lse_ref, ctx_ref, *, tile):
    total = query_ref.shape[0]
    lane = lax.broadcasted_iota(jnp.int32, (1, LANES), 1)
    keys = key_ref[...]
    values_t = value_ref[...].T
    for head in range(2):
        key_aug = augment(lane, head, keys, bias_ref[...])
        for start in range(0, total, tile):
            queries = with_one(lane, head, query_ref[start : start + tile, :])
            scores = dot_back(key_aug, queries)
            highest = jnp.max(scores, axis=0, keepdims=True)
            weights = jnp.exp(scores - highest)
            sums = jnp.sum(weights, axis=0, keepdims=True)
            context = dot(values_t[head * HD : (head + 1) * HD, :], weights.astype(BF16))
            ctx_ref[head * HD : (head + 1) * HD, start : start + tile] = context / sums
            lse_ref[0, head : head + 1, start : start + tile] = highest + jnp.log(sums)
    contexts = ctx_ref[...].T.astype(BF16)
    mine_ref[...] = contexts[: total // 2]
    other_ref[...] = contexts[total // 2 :]


def attend_call(qkv, bias):
    total, width = qkv.shape
    width //= 3
    pairs = width // LANES
    half = total // 2
    column = lambda part: pl.BlockSpec((total, LANES), lambda p: (0, part * pairs + p))
    return pl.pallas_call(
        functools.partial(attend_kernel, tile=256),
        grid=(pairs,),
        in_specs=[column(0), column(1), column(2), whole((total, LANES))],
        out_specs=[
            pl.BlockSpec((half, LANES), lambda p: (0, p)),
            pl.BlockSpec((half, LANES), lambda p: (0, p)),
            pl.BlockSpec((1, 8, total), lambda p: (p, 0, 0)),
        ],
        out_shape=[
            jax.ShapeDtypeStruct((half, width), BF16),
            jax.ShapeDtypeStruct((half, width), BF16),
            jax.ShapeDtypeStruct((pairs, 8, total), F32),
        ],
        scratch_shapes=[pltpu.VMEM((LANES, total), F32)],
        compiler_params=params(),
        cost_estimate=cost(16 * total * total * LANES * pairs, 4e6, 2 * pairs * total * total),
    )(qkv, qkv, qkv, bias)


def residual_kernel(
    keep_ref, recv_ref, mine_ref, got_ref, wmine_ref, wgot_ref, gain_ref, shift_ref, res_ref, normed_ref
):
    step = pl.program_id(0)
    values = jnp.where(step == 0, keep_ref[...], recv_ref[...]).astype(F32)
    residual = values + (dot(mine_ref[...], wmine_ref[...]) + dot(got_ref[...], wgot_ref[...]))
    res_ref[...] = residual
    normal, _ = normalize(residual)
    normed_ref[...] = (normal * gain_ref[...] + shift_ref[...]).astype(BF16)


def residual_call(keep, recv, ctx_mine, ctx_got, w_mine, w_got, gain, shift):
    rows, width = keep.shape
    heads = ctx_mine.shape[1]
    row_block = lambda i: (i, 0)
    return pl.pallas_call(
        residual_kernel,
        grid=(2,),
        in_specs=[
            whole((rows, width)),
            whole((rows, width)),
            pl.BlockSpec((rows, heads), row_block),
            pl.BlockSpec((rows, heads), row_block),
            whole((heads, width)),
            whole((heads, width)),
            whole((1, width)),
            whole((1, width)),
        ],
        out_specs=[pl.BlockSpec((rows, width), row_block)] * 2,
        out_shape=[
            jax.ShapeDtypeStruct((2 * rows, width), F32),
            jax.ShapeDtypeStruct((2 * rows, width), BF16),
        ],
        compiler_params=params(),
        cost_estimate=cost(8 * rows * width * heads, 6e6),
    )(keep, recv, ctx_mine, ctx_got, w_mine, w_got, gain, shift)


def gelu_both(values):
    root = 0.7978845608028654
    cubic = 0.044715
    square = values * values
    bent = jnp.tanh(root * values * (1.0 + cubic * square))
    half = 0.5 * (1.0 + bent)
    slope = half + 0.5 * values * (1.0 - bent * bent) * (root * (1.0 + 3.0 * cubic * square))
    return values * half, slope


def feed_kernel(
    where_ref,
    normed_m_ref, normed_o_ref, grad_m_ref, grad_o_ref, up_ref, down_ref,
    up_send_ref, up_keep_ref, down_send_ref, down_keep_ref,
    out_m_ref, out_o_ref, back_m_ref, back_o_ref,
    normed_ref, grad_ref, normed_t_ref, grad_t_ref, active_ref, hidden_ref, out_ref, back_ref,
    *, tile,
):
    step = pl.program_id(0)
    x_half = where_ref[2]
    half = normed_m_ref.shape[0]
    block = up_ref.shape[1]

    @pl.when(step == 0)
    def _():
        normed_ref[:half, :] = normed_m_ref[...]
        normed_ref[half:, :] = normed_o_ref[...]
        grad_ref[:half, :] = grad_m_ref[...]
        grad_ref[half:, :] = grad_o_ref[...]
        normed_t_ref[...] = normed_ref[...].T
        grad_t_ref[...] = grad_ref[...].T

    up_out = []
    for start in range(0, block, tile):
        span = slice(start, start + tile)
        hidden = dot(normed_ref[...], up_ref[:, span])
        active, slope = gelu_both(hidden)
        active_ref[:, span] = active.astype(BF16)
        grad_active = dot_back(grad_ref[...], down_ref[span, :])
        hidden_ref[:, span] = (grad_active * slope).astype(BF16)
    out = dot(active_ref[...], down_ref[...])
    back = dot_back(hidden_ref[...], up_ref[...])
    up_grad = dot(normed_t_ref[...], hidden_ref[...]).astype(BF16)
    down_grad = dot(grad_t_ref[...], active_ref[...]).astype(BF16)
    part = block // 2
    for side in range(2):
        piece = down_grad[:, side * part : (side + 1) * part]

        @pl.when(x_half == side)
        def _():
            down_keep_ref[0] = piece

        @pl.when(x_half != side)
        def _():
            down_send_ref[0] = piece

    @pl.when(step == 0)
    def _():
        up_send_ref[...] = up_grad
        out_ref[...] = out
        back_ref[...] = back

    @pl.when(step == 1)
    def _():
        up_keep_ref[...] = up_grad
        out_m_ref[...] = out_ref[:half, :] + out[:half]
        out_o_ref[...] = (out_ref[half:, :] + out[half:]).astype(BF16)
        back_m_ref[...] = back_ref[:half, :] + back[:half]
        back_o_ref[...] = (back_ref[half:, :] + back[half:]).astype(BF16)


def feed_call(where, normed_m, normed_o, grad_m, grad_o, w_up, w_down):
    half, width = normed_m.shape
    total = 2 * half
    block = w_up.shape[1] // 4
    part = block // 2
    token = whole((half, width))

    def high(j, where_ref):
        return jnp.where(j == 0, 1 - where_ref[1], where_ref[1])

    def at(j, where_ref):
        return 2 * high(j, where_ref) + where_ref[0]

    return pl.pallas_call(
        functools.partial(feed_kernel, tile=256),
        grid_spec=pltpu.PrefetchScalarGridSpec(
            num_scalar_prefetch=1,
            grid=(2,),
            in_specs=[
                token, token, token, token,
                pl.BlockSpec((width, block), lambda j, w: (0, at(j, w))),
                pl.BlockSpec((block, width), lambda j, w: (at(j, w), 0)),
            ],
            out_specs=[
                whole((width, block)),
                whole((width, block)),
                pl.BlockSpec((1, width, part), lambda j, w: (high(j, w), 0, 0)),
                pl.BlockSpec((1, width, part), lambda j, w: (high(j, w), 0, 0)),
                token, token, token, token,
            ],
            scratch_shapes=[
                pltpu.VMEM((total, width), BF16),
                pltpu.VMEM((total, width), BF16),
                pltpu.VMEM((width, total), BF16),
                pltpu.VMEM((width, total), BF16),
                pltpu.VMEM((total, block), BF16),
                pltpu.VMEM((total, block), BF16),
                pltpu.VMEM((total, width), F32),
                pltpu.VMEM((total, width), F32),
            ],
        ),
        out_shape=[
            jax.ShapeDtypeStruct((width, block), BF16),
            jax.ShapeDtypeStruct((width, block), BF16),
            jax.ShapeDtypeStruct((2, width, part), BF16),
            jax.ShapeDtypeStruct((2, width, part), BF16),
            jax.ShapeDtypeStruct((half, width), F32),
            jax.ShapeDtypeStruct((half, width), BF16),
            jax.ShapeDtypeStruct((half, width), F32),
            jax.ShapeDtypeStruct((half, width), BF16),
        ],
        compiler_params=params(),
        cost_estimate=cost(24 * total * width * block, 2e7, total * 2 * block),
    )(where, normed_m, normed_o, grad_m, grad_o, w_up, w_down)


def middle_kernel(
    res_ref, out_ref, out_got_ref, back_ref, back_got_ref, grad_ref, mask_ref, gain_ref,
    keep_ref, send_ref, grad_res_ref, grad_low_ref, sums_ref,
):
    step = pl.program_id(0)
    residual = res_ref[...]
    output = ((residual + out_ref[...] + out_got_ref[...].astype(F32)) * mask_ref[...]).astype(BF16)

    @pl.when(step == 0)
    def _():
        keep_ref[...] = output

    @pl.when(step == 1)
    def _():
        send_ref[...] = output

    normal, inverse = normalize(residual)
    back = back_ref[...] + back_got_ref[...].astype(F32)
    gains = jnp.sum(back * normal, axis=0, keepdims=True)
    shifts = jnp.sum(back, axis=0, keepdims=True)

    @pl.when(step == 0)
    def _():
        sums_ref[0:1, :] = gains
        sums_ref[1:2, :] = shifts

    @pl.when(step == 1)
    def _():
        sums_ref[0:1, :] += gains
        sums_ref[1:2, :] += shifts

    grad = grad_ref[...].astype(F32) + norm_back(back, gain_ref[...], normal, inverse)
    grad_res_ref[...] = grad
    grad_low_ref[...] = grad.astype(BF16)


def middle_call(residual, out_m, out_got, back_m, back_got, grad_m, mask, gain):
    half, width = residual.shape
    rows = half // 2
    row = pl.BlockSpec((rows, width), lambda i: (i, 0))
    return pl.pallas_call(
        middle_kernel,
        grid=(2,),
        in_specs=[row, row, row, row, row, row, pl.BlockSpec((rows, 1), lambda i: (i, 0)), whole((1, width))],
        out_specs=[whole((rows, width)), whole((rows, width)), row, row, whole((8, width))],
        out_shape=[
            jax.ShapeDtypeStruct((rows, width), BF16),
            jax.ShapeDtypeStruct((rows, width), BF16),
            jax.ShapeDtypeStruct((half, width), F32),
            jax.ShapeDtypeStruct((half, width), BF16),
            jax.ShapeDtypeStruct((8, width), F32),
        ],
        compiler_params=params(),
        cost_estimate=cost(half * width * 30, 1e7),
    )(residual, out_m, out_got, back_m, back_got, grad_m, mask, gain)


def attend_back_kernel(
    query_ref, key_ref, value_ref, bias_ref, ctx_m_ref, ctx_o_ref, grad_m_ref, grad_o_ref,
    wout_ref, lse_ref, cos_ref, sin_ref,
    dq_ref, dk_ref, dv_ref, dwout_ref,
    grad_ref, gctx_ref, dqt_ref, dk_acc, dv_acc,
    *, tile, score_scale,
):
    total = query_ref.shape[0]
    half = total // 2
    lane = lax.broadcasted_iota(jnp.int32, (1, LANES), 1)

    @pl.when(pl.program_id(0) == 0)
    def _():
        grad_ref[:half, :] = grad_m_ref[...]
        grad_ref[half:, :] = grad_o_ref[...]

    gctx = dot_back(grad_ref[...], wout_ref[...]).astype(BF16)
    gctx_ref[...] = gctx
    context = jnp.concatenate([ctx_m_ref[...], ctx_o_ref[...]], axis=0)
    dwout_ref[...] = dot(context.T, grad_ref[...]).astype(BF16)
    products = (gctx.astype(F32) * context.astype(F32)).T
    keys = key_ref[...]
    keys_t = keys.T
    values = value_ref[...]
    for head in range(2):
        key_aug = augment(lane, head, keys, bias_ref[...])
        delta = jnp.sum(products[head * HD : (head + 1) * HD, :], axis=0, keepdims=True)
        for start in range(0, total, tile):
            span = slice(start, start + tile)
            queries = query_ref[span, :]
            scores = dot_back(key_aug, with_one(lane, head, queries))
            weights = jnp.exp(scores - lse_ref[0, head : head + 1, span])
            grads = only_head(lane, head, gctx_ref[span, :])
            grad_weights = dot_back(values, grads)
            grad_scores = (weights * (grad_weights - delta[:, span])).astype(BF16)
            dv = dot(weights.astype(BF16), grads)
            dk = dot(grad_scores, only_head(lane, head, queries))
            dqt_ref[head * HD : (head + 1) * HD, span] = dot(
                keys_t[head * HD : (head + 1) * HD, :], grad_scores
            )
            if head == 0 and start == 0:
                dv_acc[...] = dv
                dk_acc[...] = dk
            else:
                dv_acc[...] += dv
                dk_acc[...] += dk
    cosine, sine = cos_ref[...], sin_ref[...]
    dq = dqt_ref[...].T * score_scale
    dk = dk_acc[...]
    dq_ref[...] = (dq * cosine - swap_halves(dq) * sine).astype(BF16)
    dk_ref[...] = (dk * cosine - swap_halves(dk) * sine).astype(BF16)
    dv_ref[...] = dv_acc[...].astype(BF16)


def attend_back_call(qkv, bias, ctx_m, ctx_o, grad_m, grad_o, w_out, lse, cosine, sine):
    total, width = qkv.shape
    width //= 3
    pairs = width // LANES
    half, model = grad_m.shape
    column = lambda part: pl.BlockSpec((total, LANES), lambda p: (0, part * pairs + p))
    out_column = pl.BlockSpec((total, LANES), lambda p: (0, p))
    ctx_column = pl.BlockSpec((half, LANES), lambda p: (0, p))
    weight_rows = pl.BlockSpec((LANES, model), lambda p: (p, 0))
    return pl.pallas_call(
        functools.partial(attend_back_kernel, tile=256, score_scale=HD ** (-0.5)),
        grid=(pairs,),
        in_specs=[
            column(0), column(1), column(2), whole((total, LANES)),
            ctx_column, ctx_column, whole((half, model)), whole((half, model)),
            weight_rows,
            pl.BlockSpec((1, 8, total), lambda p: (p, 0, 0)),
            whole((total, LANES)), whole((total, LANES)),
        ],
        out_specs=[out_column, out_column, out_column, weight_rows],
        out_shape=[
            jax.ShapeDtypeStruct((total, width), BF16),
            jax.ShapeDtypeStruct((total, width), BF16),
            jax.ShapeDtypeStruct((total, width), BF16),
            jax.ShapeDtypeStruct((width, model), BF16),
        ],
        scratch_shapes=[
            pltpu.VMEM((total, model), BF16),
            pltpu.VMEM((total, LANES), BF16),
            pltpu.VMEM((LANES, total), F32),
            pltpu.VMEM((total, LANES), F32),
            pltpu.VMEM((total, LANES), F32),
        ],
        compiler_params=params(),
        cost_estimate=cost(40 * total * total * LANES * pairs, 1e7, 2 * pairs * total * total),
    )(qkv, qkv, qkv, bias, ctx_m, ctx_o, grad_m, grad_o, w_out, lse, cosine, sine)


def qkv_grad_kernel(normed_ref, dq_ref, dk_ref, dv_ref, out_ref, normed_t_ref):
    step = pl.program_id(0)

    @pl.when(step == 0)
    def _():
        normed_t_ref[...] = normed_ref[...].T

    for part, ref in enumerate((dq_ref, dk_ref, dv_ref)):

        @pl.when(step == part)
        def _():
            out_ref[0] = dot(normed_t_ref[...], ref[...]).astype(BF16)


def qkv_grad_call(normed, dq, dk, dv):
    total, width = normed.shape
    heads = dq.shape[1]
    return pl.pallas_call(
        qkv_grad_kernel,
        grid=(3,),
        in_specs=[whole((total, width))] + [whole((total, heads))] * 3,
        out_specs=pl.BlockSpec((1, width, heads), lambda j: (j, 0, 0)),
        out_shape=jax.ShapeDtypeStruct((3, width, heads), BF16),
        scratch_shapes=[pltpu.VMEM((width, total), BF16)],
        compiler_params=params(),
        cost_estimate=cost(6 * total * width * heads, 6e6),
    )(normed, dq, dk, dv)


def normed_grad_kernel(dq_ref, dk_ref, dv_ref, weight_ref, mine_ref, other_ref):
    step = pl.program_id(0)
    heads = dq_ref.shape[1]
    out = dot_back(dq_ref[...], weight_ref[:, :heads])
    out += dot_back(dk_ref[...], weight_ref[:, heads : 2 * heads])
    out += dot_back(dv_ref[...], weight_ref[:, 2 * heads :])

    @pl.when(step == 0)
    def _():
        other_ref[...] = out.astype(BF16)

    @pl.when(step == 1)
    def _():
        mine_ref[...] = out


def normed_grad_call(dq, dk, dv, weight):
    total, heads = dq.shape
    width = weight.shape[0]
    half = total // 2
    row = pl.BlockSpec((half, heads), lambda i: (1 - i, 0))
    return pl.pallas_call(
        normed_grad_kernel,
        grid=(2,),
        in_specs=[row, row, row, whole(weight.shape)],
        out_specs=[whole((half, width)), whole((half, width))],
        out_shape=[
            jax.ShapeDtypeStruct((half, width), F32),
            jax.ShapeDtypeStruct((half, width), BF16),
        ],
        compiler_params=params(),
        cost_estimate=cost(6 * total * width * heads, 6e6),
    )(dq, dk, dv, weight)


def tokens_grad_kernel(
    keep_ref, recv_ref, back_ref, got_ref, grad_res_ref, gain_ref, keep_out_ref, send_out_ref, sums_ref
):
    step = pl.program_id(0)
    values = jnp.where(step == 0, recv_ref[...], keep_ref[...]).astype(F32)
    normal, inverse = normalize(values)
    back = back_ref[...] + got_ref[...].astype(F32)
    gains = jnp.sum(back * normal, axis=0, keepdims=True)
    shifts = jnp.sum(back, axis=0, keepdims=True)
    grad = (grad_res_ref[...] + norm_back(back, gain_ref[...], normal, inverse)).astype(BF16)

    @pl.when(step == 0)
    def _():
        sums_ref[0:1, :] = gains
        sums_ref[1:2, :] = shifts
        send_out_ref[...] = grad

    @pl.when(step == 1)
    def _():
        sums_ref[0:1, :] += gains
        sums_ref[1:2, :] += shifts
        keep_out_ref[...] = grad


def tokens_grad_call(keep, recv, back, got, grad_res, gain):
    rows, width = keep.shape
    row = pl.BlockSpec((rows, width), lambda i: (1 - i, 0))
    return pl.pallas_call(
        tokens_grad_kernel,
        grid=(2,),
        in_specs=[whole((rows, width)), whole((rows, width)), row, row, row, whole((1, width))],
        out_specs=[whole((rows, width)), whole((rows, width)), whole((8, width))],
        out_shape=[
            jax.ShapeDtypeStruct((rows, width), BF16),
            jax.ShapeDtypeStruct((rows, width), BF16),
            jax.ShapeDtypeStruct((8, width), F32),
        ],
        compiler_params=params(),
        cost_estimate=cost(2 * rows * width * 30, 6e6),
    )(keep, recv, back, got, grad_res, gain)


def low_bits(values, axis, index, count):
    bit = 1
    while bit < count:
        shape = values.shape[:axis] + (values.shape[axis] // 2, 2) + values.shape[axis + 1 :]
        paired = values.reshape(shape)
        side = (index // bit) % 2
        sent = pick(paired, 1 - side, axis + 1).astype(BF16)
        values = pick(paired, side, axis + 1).astype(F32) + swap(sent, "dp", bit).astype(F32)
        bit *= 2
    return values


def last_four(chunks, own, bit):
    total = chunks(0).astype(F32)
    got = [swap(chunks(k).astype(BF16), "dp", bit * k) for k in (1, 2, 3)]
    for one in got:
        total = total + one.astype(F32)
    return total


def local(
    tokens, gain_one, shift_one, w_query, w_key, w_value, w_out, gain_two, shift_two, w_up, w_down,
    cotangent, lengths,
):
    row_count, piece, width = tokens.shape
    n_dp = lax.axis_size("dp")
    n_seq = lax.axis_size("seq")
    count = n_dp // 4
    place = lax.axis_index("seq")
    core, row = place % 2, place // 2
    data = lax.axis_index("dp")
    high = data // count
    total = n_seq * piece
    half = total // 2
    group = width // n_seq

    tok_keep = pick(tokens, row)
    tok_recv = swap(pick(tokens, 1 - row), "seq", 2)
    cot_keep = pick(cotangent, row)
    cot_recv = swap(pick(cotangent, 1 - row), "seq", 2)
    tok_keep_o = swap(tok_keep, "seq", 1)
    tok_recv_o = swap(tok_recv, "seq", 1)

    starts = jnp.stack(
        [2 * row + core, 2 * (1 - row) + core, 2 * row + 1 - core, 2 * (1 - row) + 1 - core]
    )
    spots = (starts[:, None] * piece + jnp.arange(piece, dtype=jnp.int32)[None, :]).reshape(total)
    valid = (spots < pick(lengths, row))[:, None]
    mask = valid.astype(F32)
    bias = jnp.broadcast_to(jnp.where(valid, 0.0, MASKED).astype(BF16), (total, LANES))
    lane = jnp.arange(LANES, dtype=jnp.int32)
    steps = (lane % (HD // 2)).astype(F32)
    frequency = 10000.0 ** (-2.0 * steps / HD)
    angles = spots.astype(F32)[:, None] * frequency[None, :]
    cosine = jnp.cos(angles)
    sine = jnp.where(lane % HD < HD // 2, -1.0, 1.0) * jnp.sin(angles)

    def my_columns(weight):
        return pick(weight.reshape(width, 2, 2, group), core, 2).reshape(width, 2 * group)

    w_qkv = jnp.concatenate([my_columns(w_query), my_columns(w_key), my_columns(w_value)], axis=1)
    out_rows = w_out.reshape(2, 2, group, width)
    w_out_m = pick(out_rows, core, 1).reshape(2 * group, width)
    w_out_o = pick(out_rows, 1 - core, 1).reshape(2 * group, width)

    gain1, shift1 = gain_one.reshape(1, width), shift_one.reshape(1, width)
    gain2, shift2 = gain_two.reshape(1, width), shift_two.reshape(1, width)

    first = project_call(0, tok_keep, tok_keep_o, gain1, shift1, w_qkv, cosine, sine, ())
    qkv, normed = project_call(1, tok_recv, tok_recv_o, gain1, shift1, w_qkv, cosine, sine, first)
    ctx_m, ctx_o, lse = attend_call(qkv, bias)
    ctx_got = swap(ctx_o, "seq", 1)

    grad_m = jnp.concatenate([cot_keep, cot_recv], axis=0)
    grad_m = jnp.where(valid[:half], grad_m, jnp.zeros_like(grad_m))
    grad_o = swap(grad_m, "seq", 1)

    residual, normed_two = residual_call(
        tok_keep, tok_recv, ctx_m, ctx_got, w_out_m, w_out_o, gain2, shift2
    )
    normed_two_o = swap(normed_two, "seq", 1)
    side = (data // (count // 2)) % 2
    where = jnp.stack([core, row, side]).astype(jnp.int32)
    up_send, up_keep, down_send, down_keep, out_m, out_o, back_m, back_o = feed_call(
        where, normed_two, normed_two_o, grad_m, grad_o, w_up, w_down
    )
    back_got = swap(back_o, "seq", 1)
    out_got = swap(out_o, "seq", 1)
    out_keep, out_send, grad_res, grad_low, sums_two = middle_call(
        residual, out_m, out_got, back_m, back_got, grad_m, mask[:half], gain2
    )
    grad_low_o = swap(grad_low, "seq", 1)
    out_back = swap(out_send, "seq", 2)
    dq, dk, dv, dw_out = attend_back_call(
        qkv, bias, ctx_m, ctx_o, grad_low, grad_low_o, w_out_m, lse, cosine, sine
    )
    normed_m, normed_o = normed_grad_call(dq, dk, dv, w_qkv)
    normed_got = swap(normed_o, "seq", 1)
    dw_qkv = qkv_grad_call(normed, dq, dk, dv)
    tok_out_keep, tok_out_send, sums_one = tokens_grad_call(
        tok_keep, tok_recv, normed_m, normed_got, grad_res, gain1
    )
    tok_back = swap(tok_out_send, "seq", 2)

    up = up_keep.astype(F32) + swap(up_send, "seq", 2).astype(F32)
    block_rows = width // n_dp
    up = low_bits(up.reshape(n_dp, block_rows, -1), 0, data, count)
    grad_up = last_four(lambda k: pick(up, high ^ k), high, count)

    down = down_keep.astype(F32) + swap(down_send, "dp", count // 2).astype(F32)
    halves = down.reshape(2, 2, 2 * group, -1)
    down = pick(halves, row, 1).astype(F32) + swap(pick(halves, 1 - row, 1).astype(BF16), "seq", 2)
    down = down.reshape(2, 2, group, -1)
    bit = count // 4
    while bit > 0:
        side = (data // bit) % 2
        size = down.shape[-1] // 2
        sent = lax.dynamic_slice_in_dim(down, (1 - side) * size, size, 3).astype(BF16)
        down = lax.dynamic_slice_in_dim(down, side * size, size, 3) + swap(sent, "dp", bit)
        bit //= 2

    def down_chunk(k):
        target = high ^ k
        return pick(pick(down, target // 2), target % 2)

    grad_down = last_four(down_chunk, high, count)

    out = low_bits(dw_out.reshape(2 * count, width // n_dp, width), 0, data, count)
    out = out.astype(F32).reshape(2, width // n_dp, 2, 2 * group)
    out = pick(out, row, 2) + swap(pick(out, 1 - row, 2).astype(BF16), "seq", 2)
    out = out.reshape(2, width // n_dp, 2, group)

    def out_chunk(k):
        target = high ^ k
        return pick(pick(out, target // 2), target % 2, 1)

    grad_out = last_four(out_chunk, high, count)

    exchange = []
    for d in range(n_dp):
        for s in range(n_seq):
            second = (d // count) % 2
            to_d = d + (s % 2 - second) * count
            to_s = s - s % 2 + second
            exchange.append((d * n_seq + s, to_d * n_seq + to_s))
    grad_down, grad_out = (
        lax.ppermute(one, ("dp", "seq"), exchange) for one in (grad_down, grad_out)
    )
    grad_down = grad_down.T

    parts = dw_qkv.reshape(3, width, 2, group)
    qkv_sum = pick(parts, row, 2).astype(F32) + swap(pick(parts, 1 - row, 2), "seq", 2)
    qkv_sum = low_bits(qkv_sum.reshape(3, n_dp, width // n_dp, group), 1, data, count)
    grad_qkv = last_four(lambda k: pick(qkv_sum, high ^ k, 1), high, count)

    sums = jnp.concatenate([sums_one[:2], sums_two[:2]], axis=0)
    for axis in ("seq", "dp"):
        bit = 1
        while bit < lax.axis_size(axis):
            sums = sums + swap(sums, axis, bit)
            bit *= 2

    def rows_of(kept, back):
        return jnp.where(row == 0, jnp.stack([kept, back]), jnp.stack([back, kept]))

    return (
        rows_of(out_keep, out_back),
        rows_of(tok_out_keep, tok_back),
        sums[0],
        sums[1],
        grad_qkv[0],
        grad_qkv[1],
        grad_qkv[2],
        grad_out,
        sums[2],
        sums[3],
        grad_up,
        grad_down,
    )


def solution(mesh):
    tokens = P("dp", "seq", None)
    weights = P("dp", "seq")
    return jax.shard_map(
        local,
        mesh=mesh,
        in_specs=(tokens,) + (P(),) * 10 + (tokens, P("dp")),
        out_specs=(tokens, tokens, P(), P(), weights, weights, weights, weights, P(), P(), weights, weights),
        check_vma=False,
    )
```

```python
import functools

import jax
import jax.numpy as jnp
import numpy as np
from jax import lax
from jax.experimental import pallas as pl
from jax.experimental.pallas import tpu as pltpu
from jax.sharding import PartitionSpec as P

HD = 64
EPSILON = 1e-05
MASKED = -1000000000.0
LANES = 128
BF16 = jnp.bfloat16
F32 = jnp.float32
VMEM_BYTES = 56 * 1024 * 1024
CORE, ROW, SIDE, LENGTH, SPOT = 0, 1, 2, 3, 4


def swap(values, axis, bit):
    count = lax.axis_size(axis)
    return lax.ppermute(values, axis, [(i, i ^ bit) for i in range(count)])


def together(*values):
    return lax.optimization_barrier(values)


def pick(values, index, axis=0):
    return lax.dynamic_index_in_dim(values, index, axis, keepdims=False)


def dot(left, right):
    return jnp.dot(left, right, preferred_element_type=F32)


def dot_back(left, right):
    return lax.dot_general(left, right, (((1,), (1,)), ((), ())), preferred_element_type=F32)


def normalize(values):
    average = jnp.mean(values, axis=-1, keepdims=True)
    centred = values - average
    variance = jnp.mean(centred * centred, axis=-1, keepdims=True)
    inverse = lax.rsqrt(variance + EPSILON)
    return centred * inverse, inverse


def norm_back(grad, gain, normal, inverse):
    scaled = grad * gain
    first = jnp.mean(scaled, axis=-1, keepdims=True)
    second = jnp.mean(scaled * normal, axis=-1, keepdims=True)
    return (scaled - first - normal * second) * inverse


def row_vector(ref):
    return ref[...].reshape(1, ref.shape[0])


def swap_halves(values):
    lane = lax.broadcasted_iota(jnp.int32, values.shape, 1)
    up = pltpu.roll(values, LANES - HD // 2, 1)
    down = pltpu.roll(values, HD // 2, 1)
    return jnp.where(lane % HD < HD // 2, up, down)


def rotary_tables(length):
    lane = np.arange(LANES)
    frequency = 10000.0 ** (-2.0 * (lane % (HD // 2)) / HD)
    angles = np.arange(length)[:, None] * frequency[None, :]
    sign = np.where(lane % HD < HD // 2, -1.0, 1.0)
    return np.cos(angles).astype(np.float32), (sign * np.sin(angles)).astype(np.float32)


def kept_rows(where_ref, block, rows, lanes):
    spot = lax.broadcasted_iota(jnp.int32, (rows, lanes), 0) + where_ref[SPOT + block] * rows
    return spot < where_ref[LENGTH]


def params(**kinds):
    return pltpu.CompilerParams(vmem_limit_bytes=VMEM_BYTES, **kinds)


SMALL = pl.CostEstimate(flops=1, bytes_accessed=1, transcendentals=0)


def whole(shape):
    return pl.BlockSpec(shape, lambda *_: (0,) * len(shape))


def call(kernel, grid, in_specs, out_specs, out_shape, scratch, estimate, aliases=None):
    return pl.pallas_call(
        kernel,
        grid_spec=pltpu.PrefetchScalarGridSpec(
            num_scalar_prefetch=1,
            grid=grid,
            in_specs=in_specs,
            out_specs=out_specs,
            scratch_shapes=scratch,
        ),
        out_shape=[jax.ShapeDtypeStruct(shape, kind) for shape, kind in out_shape],
        input_output_aliases=aliases or {},
        compiler_params=params(),
        cost_estimate=estimate,
    )


def pair_columns(ref, core, pair):
    group = ref.shape[1] // 4
    pieces = []
    start, end = pair * LANES, (pair + 1) * LANES
    if start < group:
        pieces.append(ref[:, core * group + start : core * group + min(end, group)])
    if end > group:
        begin = max(start, group)
        pieces.append(ref[:, (1 + core) * group + begin : (1 + core) * group + end])
    return pieces[0] if len(pieces) == 1 else jnp.concatenate(pieces, axis=1)


def project_kernel(where_ref, mine_ref, other_ref, gain_ref, shift_ref, *rest, first, pairs):
    step = pl.program_id(0)
    if first:
        wq_ref, wk_ref, wv_ref, cos_ref, sin_ref, qkv_ref, normed_t_ref, weight_ref = rest

        @pl.when(step == 0)
        def _():
            for core in range(2):

                @pl.when(where_ref[CORE] == core)
                def _():
                    for part, ref in enumerate((wq_ref, wk_ref, wv_ref)):
                        for pair in range(pairs):
                            start = (3 * pair + part) * LANES
                            weight_ref[:, start : start + LANES] = pair_columns(ref, core, pair)
    else:
        weight_ref, cos_ref, sin_ref, _, _, qkv_ref, normed_t_ref = rest
    values = jnp.where(step == 0, mine_ref[...], other_ref[...]).astype(F32)
    normal, _ = normalize(values)
    normed = (normal * row_vector(gain_ref) + row_vector(shift_ref)).astype(BF16)
    normed_t_ref[...] = normed.T
    cosine, sine = cos_ref[...], sin_ref[...]
    width = 3 * LANES
    for pair in range(pairs):
        out = dot(normed, weight_ref[:, pair * width : (pair + 1) * width])
        for part in range(3):
            piece = out[:, part * LANES : (part + 1) * LANES]
            if part < 2:
                piece = piece * cosine + swap_halves(piece) * sine
                if part == 0:
                    piece = piece * (HD ** (-0.5))
            start = pair * width + part * LANES
            qkv_ref[:, start : start + LANES] = piece.astype(BF16)


def project_call(turn, where, mine, other, gain, shift, weights, tables, previous):
    rows, width = mine.shape
    out_width = 3 * width // 2
    total = 4 * rows
    block = lambda i, w: (2 * i + turn, 0)
    table = pl.BlockSpec((rows, LANES), lambda i, w: (w[SPOT + 2 * i + turn], 0))
    in_specs = [whole((rows, width))] * 2 + [whole((width,))] * 2
    in_specs += [whole(weight.shape) for weight in weights] + [table, table]
    out_specs = [
        pl.BlockSpec((rows, out_width), block),
        pl.BlockSpec((width, rows), lambda i, w: (0, 2 * i + turn)),
    ]
    out_shape = [((total, out_width), BF16), ((width, total), BF16)]
    aliases = {}
    if previous:
        aliases = {1 + len(in_specs): 0, 2 + len(in_specs): 1}
        in_specs += [pl.BlockSpec(memory_space=pl.ANY)] * 2
    else:
        out_specs.append(whole((width, out_width)))
        out_shape.append(((width, out_width), BF16))
    return call(
        functools.partial(project_kernel, first=not previous, pairs=out_width // (3 * LANES)),
        (2,), in_specs, out_specs, out_shape, [],
        SMALL, aliases,
    )(where, mine, other, gain, shift, *weights, *tables, *previous)


def mask_lane(lane, head, keys, bias):
    return jnp.where(lane == (HD if head == 0 else 0), bias, keys)


def only_head(lane, head, values):
    return jnp.where(lane // HD == head, values, jnp.zeros_like(values))


def with_one(lane, head, values):
    one = lane == (HD if head == 0 else 0)
    return jnp.where(one, jnp.ones_like(values), only_head(lane, head, values))


def fill_bias(where_ref, bias_ref):
    rows = bias_ref.shape[0] // 4
    for block in range(4):
        kept = kept_rows(where_ref, block, rows, LANES)
        bias_ref[block * rows : (block + 1) * rows, :] = jnp.where(kept, 0.0, MASKED).astype(BF16)


def attend_kernel(
    where_ref, query_ref, key_ref, value_ref, mine_ref, other_ref, ctx_t_ref, lse_ref, bias_ref, ctx_ref,
    *, tile,
):
    total = query_ref.shape[0]
    lane = lax.broadcasted_iota(jnp.int32, (1, LANES), 1)

    @pl.when(pl.program_id(0) == 0)
    def _():
        fill_bias(where_ref, bias_ref)

    keys = key_ref[...]
    values_t = value_ref[...].T
    for head in range(2):
        key_aug = mask_lane(lane, head, keys, bias_ref[...])
        for start in range(0, total, tile):
            queries = with_one(lane, head, query_ref[start : start + tile, :])
            scores = dot_back(key_aug, queries)
            highest = jnp.max(scores, axis=0, keepdims=True)
            weights = jnp.exp(scores - highest)
            sums = jnp.sum(weights, axis=0, keepdims=True)
            context = dot(values_t[head * HD : (head + 1) * HD, :], weights.astype(BF16))
            ctx_ref[head * HD : (head + 1) * HD, start : start + tile] = context / sums
            lse_ref[0, head : head + 1, start : start + tile] = highest + jnp.log(sums)
    ctx_t_ref[...] = ctx_ref[...].astype(BF16)
    contexts = ctx_ref[...].T.astype(BF16)
    mine_ref[...] = contexts[: total // 2]
    other_ref[...] = contexts[total // 2 :]


def attend_call(where, qkv):
    total, width = qkv.shape
    pairs = width // (3 * LANES)
    width //= 3
    half = total // 2
    column = lambda part: pl.BlockSpec((total, LANES), lambda p, w: (0, 3 * p + part))
    out_column = pl.BlockSpec((half, LANES), lambda p, w: (0, p))
    return call(
        functools.partial(attend_kernel, tile=256),
        (pairs,),
        [column(0), column(1), column(2)],
        [
            out_column, out_column,
            pl.BlockSpec((LANES, total), lambda p, w: (p, 0)),
            pl.BlockSpec((1, 8, total), lambda p, w: (p, 0, 0)),
        ],
        [((half, width), BF16), ((half, width), BF16), ((width, total), BF16), ((pairs, 8, total), F32)],
        [pltpu.VMEM((total, LANES), BF16), pltpu.VMEM((LANES, total), F32)],
        SMALL,
    )(where, qkv, qkv, qkv)


def stack_rows(refs):
    return jnp.concatenate([ref[0] for ref in refs], axis=0)


def residual_kernel(
    where_ref, keep_ref, recv_ref, mine_ref, got_ref, w0_ref, w1_ref, w2_ref, w3_ref,
    gain_ref, shift_ref, res_ref, normed_ref,
):
    step = pl.program_id(0)
    values = jnp.where(step == 0, keep_ref[...], recv_ref[...]).astype(F32)
    attended = dot(mine_ref[...], stack_rows((w0_ref, w1_ref)))
    attended += dot(got_ref[...], stack_rows((w2_ref, w3_ref)))
    residual = values + attended
    res_ref[...] = residual
    normal, _ = normalize(residual)
    normed_ref[...] = (normal * row_vector(gain_ref) + row_vector(shift_ref)).astype(BF16)


def out_weight_specs(group, width):
    places = (
        lambda w: w[CORE],
        lambda w: 2 + w[CORE],
        lambda w: 1 - w[CORE],
        lambda w: 3 - w[CORE],
    )
    return [pl.BlockSpec((1, group, width), lambda i, w, at=at: (at(w), 0, 0)) for at in places]


def residual_call(where, keep, recv, ctx_mine, ctx_got, w_out, gain, shift):
    rows, width = keep.shape
    heads = ctx_mine.shape[1]
    row = lambda lanes: pl.BlockSpec((rows, lanes), lambda i, w: (i, 0))
    return call(
        residual_kernel,
        (2,),
        [whole((rows, width))] * 2 + [row(heads)] * 2
        + out_weight_specs(heads // 2, width) + [whole((width,))] * 2,
        [row(width)] * 2,
        [((2 * rows, width), F32), ((2 * rows, width), BF16)],
        [],
        SMALL,
    )(where, keep, recv, ctx_mine, ctx_got, w_out, w_out, w_out, w_out, gain, shift)


def gelu_both(values):
    root = 0.7978845608028654
    cubic = 0.044715
    square = values * values
    bent = jnp.tanh(root * values * (1.0 + cubic * square))
    half = 0.5 * (1.0 + bent)
    slope = half + 0.5 * values * (1.0 - bent * bent) * (root * (1.0 + 3.0 * cubic * square))
    return values * half, slope


def feed_kernel(
    where_ref,
    normed_m_ref, normed_o_ref, cot0_ref, cot1_ref, cot2_ref, cot3_ref, up_ref, down_ref,
    up_send_ref, up_keep_ref, down_send_ref, down_keep_ref,
    out_m_ref, out_o_ref, back_m_ref, back_o_ref,
    normed_ref, grad_ref, normed_t_ref, grad_t_ref, active_ref, hidden_ref, out_ref, back_ref,
    *, tile,
):
    step = pl.program_id(0)
    half, width = normed_m_ref.shape
    block = up_ref.shape[1]

    @pl.when(step == 0)
    def _():
        normed_ref[:half, :] = normed_m_ref[...]
        normed_ref[half:, :] = normed_o_ref[...]
        rows = half // 2
        for place, ref in enumerate((cot0_ref, cot1_ref, cot2_ref, cot3_ref)):
            kept = kept_rows(where_ref, place, rows, width)
            grad_ref[place * rows : (place + 1) * rows, :] = jnp.where(
                kept, ref[...], jnp.zeros_like(ref)
            )
        normed_t_ref[...] = normed_ref[...].T
        grad_t_ref[...] = grad_ref[...].T

    for start in range(0, block, tile):
        span = slice(start, start + tile)
        hidden = dot(normed_ref[...], up_ref[:, span])
        active, slope = gelu_both(hidden)
        active_ref[:, span] = active.astype(BF16)
        grad_active = dot_back(grad_ref[...], down_ref[span, :])
        hidden_ref[:, span] = (grad_active * slope).astype(BF16)
    out = dot(active_ref[...], down_ref[...])
    back = dot_back(hidden_ref[...], up_ref[...])
    up_grad = dot(normed_t_ref[...], hidden_ref[...]).astype(BF16)
    down_grad = dot(grad_t_ref[...], active_ref[...]).astype(BF16)
    part = block // 2
    for side in range(2):
        piece = down_grad[:, side * part : (side + 1) * part]

        @pl.when(where_ref[SIDE] == side)
        def _():
            down_keep_ref[0] = piece

        @pl.when(where_ref[SIDE] != side)
        def _():
            down_send_ref[0] = piece

    @pl.when(step == 0)
    def _():
        up_send_ref[...] = up_grad
        out_ref[...] = out
        back_ref[...] = back

    @pl.when(step == 1)
    def _():
        up_keep_ref[...] = up_grad
        out_m_ref[...] = out_ref[:half, :] + out[:half]
        out_o_ref[...] = (out_ref[half:, :] + out[half:]).astype(BF16)
        back_m_ref[...] = back_ref[:half, :] + back[:half]
        back_o_ref[...] = (back_ref[half:, :] + back[half:]).astype(BF16)


def feed_call(where, normed_m, normed_o, cotangents, w_up, w_down):
    half, width = normed_m.shape
    total = 2 * half
    block = w_up.shape[1] // 4
    part = block // 2
    token = whole((half, width))

    def high(j, w):
        return jnp.where(j == 0, 1 - w[ROW], w[ROW])

    def at(j, w):
        return 2 * high(j, w) + w[CORE]

    down_piece = pl.BlockSpec((1, width, part), lambda j, w: (high(j, w), 0, 0))
    return call(
        functools.partial(feed_kernel, tile=256),
        (2,),
        [token, token] + [whole((half // 2, width))] * 4
        + [
            pl.BlockSpec((width, block), lambda j, w: (0, at(j, w))),
            pl.BlockSpec((block, width), lambda j, w: (at(j, w), 0)),
        ],
        [whole((width, block)), whole((width, block)), down_piece, down_piece, token, token, token, token],
        [
            ((width, block), BF16),
            ((width, block), BF16),
            ((2, width, part), BF16),
            ((2, width, part), BF16),
            ((half, width), F32),
            ((half, width), BF16),
            ((half, width), F32),
            ((half, width), BF16),
        ],
        [
            pltpu.VMEM((total, width), BF16),
            pltpu.VMEM((total, width), BF16),
            pltpu.VMEM((width, total), BF16),
            pltpu.VMEM((width, total), BF16),
            pltpu.VMEM((total, block), BF16),
            pltpu.VMEM((total, block), BF16),
            pltpu.VMEM((total, width), F32),
            pltpu.VMEM((total, width), F32),
        ],
        SMALL,
    )(where, normed_m, normed_o, *cotangents, w_up, w_down)


def middle_kernel(
    where_ref,
    res_ref, out_ref, out_got_ref, back_ref, back_got_ref, cot0_ref, cot1_ref, gain_ref,
    keep_ref, send_ref, grad_res_ref, grad_low_ref, sums_ref,
):
    step = pl.program_id(0)
    residual = res_ref[...]
    kept = kept_rows(where_ref, step, *residual.shape)
    output = residual + out_ref[...] + out_got_ref[...].astype(F32)
    output = jnp.where(kept, output, jnp.zeros_like(output)).astype(BF16)

    @pl.when(step == 0)
    def _():
        keep_ref[0] = output

    @pl.when(step == 1)
    def _():
        send_ref[...] = output

    normal, inverse = normalize(residual)
    back = back_ref[...] + back_got_ref[...].astype(F32)
    gains = jnp.sum(back * normal, axis=0, keepdims=True)
    shifts = jnp.sum(back, axis=0, keepdims=True)

    @pl.when(step == 0)
    def _():
        sums_ref[0:1, :] = gains
        sums_ref[1:2, :] = shifts

    @pl.when(step == 1)
    def _():
        sums_ref[0:1, :] += gains
        sums_ref[1:2, :] += shifts

    cotangent = jnp.where(step == 0, cot0_ref[...], cot1_ref[...]).astype(F32)
    cotangent = jnp.where(kept, cotangent, jnp.zeros_like(cotangent))
    grad = cotangent + norm_back(back, row_vector(gain_ref), normal, inverse)
    grad_res_ref[...] = grad
    grad_low_ref[...] = grad.astype(BF16)


def middle_call(where, residual, out_m, out_got, back_m, back_got, cot_keep, cot_recv, gain):
    half, width = residual.shape
    rows = half // 2
    row = pl.BlockSpec((rows, width), lambda i, w: (i, 0))
    return call(
        middle_kernel,
        (2,),
        [row] * 5 + [whole((rows, width))] * 2 + [whole((width,))],
        [
            pl.BlockSpec((1, rows, width), lambda i, w: (w[ROW], 0, 0)),
            whole((rows, width)),
            row,
            row,
            whole((8, width)),
        ],
        [
            ((2, rows, width), BF16),
            ((rows, width), BF16),
            ((half, width), F32),
            ((half, width), BF16),
            ((8, width), F32),
        ],
        [],
        SMALL,
    )(where, residual, out_m, out_got, back_m, back_got, cot_keep, cot_recv, gain)


def piece_order(where_ref):
    side, row = where_ref[SIDE], where_ref[ROW]
    order = []
    for kept in (0, 1):
        mine = side if kept else 1 - side
        order += [8 * high + 2 * mine + half for high in (0, 1) for half in (0, 1)]
    for kept in (0, 1):
        mine = row if kept else 1 - row
        order += [8 * high + 4 + 2 * one + mine for high in (0, 1) for one in (0, 1)]
    return order


def attend_back_kernel(
    where_ref,
    query_ref, key_ref, value_ref, ctx_mine_ref, ctx_got_ref, grad_m_ref, grad_o_ref,
    w0_ref, w1_ref, lse_ref, cos_ref, sin_ref, normed_t_ref, *rest,
    tile, score_scale, pair, pairs,
):
    if pair < pairs - 1:
        rest = rest[4 if pair else 0 :]
        out_refs, grads_ref = rest[:4], rest[4]
        rest = rest[5:]
    else:
        early_refs, weight_ref = rest[: pairs - 1], rest[pairs - 1]
        rest = rest[pairs + 4 :]
        out_refs, back_m_ref, back_o_ref = rest[:4], rest[4], rest[5]
        rest = rest[6:]
    bias_ref, grad_ref, columns_ref, gctx_ref, dqt_ref, dk_acc, dv_acc, qkv_ref, own_ref = rest
    total = query_ref.shape[0]
    half = total // 2
    model = grad_m_ref.shape[1]
    lane = lax.broadcasted_iota(jnp.int32, (1, LANES), 1)
    unit = model // 16
    group = model // 4
    fill_bias(where_ref, bias_ref)
    grad_ref[:half, :] = grad_m_ref[...]
    grad_ref[half:, :] = grad_o_ref[...]
    for core in range(2):

        @pl.when(where_ref[CORE] == core)
        def _():
            columns_ref[...] = pair_columns(grad_ref, core, pair)

    wout = jnp.concatenate([w0_ref[0], w1_ref[0]], axis=0)[pair * LANES : (pair + 1) * LANES]
    gctx = dot_back(grad_ref[...], wout).astype(BF16)
    gctx_ref[...] = gctx
    ctx_t = ctx_mine_ref[pair * LANES : (pair + 1) * LANES, :]
    products = gctx.astype(F32).T * ctx_t.astype(F32)
    keys = key_ref[...]
    keys_t = keys.T
    values = value_ref[...]
    for head in range(2):
        key_aug = mask_lane(lane, head, keys, bias_ref[...])
        delta = jnp.sum(products[head * HD : (head + 1) * HD, :], axis=0, keepdims=True)
        for start in range(0, total, tile):
            span = slice(start, start + tile)
            queries = query_ref[span, :]
            scores = dot_back(key_aug, with_one(lane, head, queries))
            weights = jnp.exp(scores - lse_ref[0, head : head + 1, span])
            grads = only_head(lane, head, gctx_ref[span, :])
            grad_weights = dot_back(values, grads)
            grad_scores = (weights * (grad_weights - delta[:, span])).astype(BF16)
            dv = dot(weights.astype(BF16), grads)
            dk = dot(grad_scores, only_head(lane, head, queries))
            dqt_ref[head * HD : (head + 1) * HD, span] = dot(
                keys_t[head * HD : (head + 1) * HD, :], grad_scores
            )
            if head == 0 and start == 0:
                dv_acc[...] = dv
                dk_acc[...] = dk
            else:
                dv_acc[...] += dv
                dk_acc[...] += dk
    rows = total // 4
    tables = []
    for ref in (cos_ref, sin_ref):
        tables.append(
            jnp.concatenate(
                [
                    ref[pl.ds(pl.multiple_of(where_ref[SPOT + block] * rows, rows), rows), :]
                    for block in range(4)
                ],
                axis=0,
            )
        )
    cosine, sine = tables
    dq = dqt_ref[...].T * score_scale
    dk = dk_acc[...]
    dq = (dq * cosine - swap_halves(dq) * sine).astype(BF16)
    dk = (dk * cosine - swap_halves(dk) * sine).astype(BF16)
    grads = jnp.concatenate([dq, dk, dv_acc[...].astype(BF16)], axis=1)
    qkv_ref[...] = dot(normed_t_ref[...], grads).astype(BF16)
    columns = columns_ref[...]
    turned = jnp.concatenate([columns[half:], columns[:half]], axis=0)
    own_ref[0] = dot(ctx_mine_ref[...], columns).astype(BF16)
    own_ref[1] = dot(ctx_got_ref[...], turned).astype(BF16)
    for place, source in enumerate(piece_order(where_ref)):
        ref = out_refs[place // 4]
        span = slice(place % 4 * unit, (place % 4 + 1) * unit)
        ref[span, : 3 * LANES] = qkv_ref[pl.ds(pl.multiple_of(source * unit, unit), unit), :]
        block = source // 4
        other = jnp.where(block % 2 == where_ref[CORE], 0, 1)
        inside = pl.multiple_of((block // 2) * group + (source % 4) * unit, unit)
        ref[span, 3 * LANES :] = own_ref[other, pl.ds(inside, unit), :]
    if pair < pairs - 1:
        grads_ref[...] = grads
    else:
        width = 3 * LANES
        back = dot_back(grads, weight_ref[:, pair * width :])
        for early, ref in enumerate(early_refs):
            back += dot_back(ref[...], weight_ref[:, early * width : (early + 1) * width])
        back_m_ref[...] = back[:half]
        back_o_ref[...] = back[half:].astype(BF16)


def attend_back_call(
    pair, where, qkv, ctx_t, ctx_got_t, grad_m, grad_o, w_out, lse, tables, normed_t, early, weight, pieces
):
    total, width = qkv.shape
    pairs = width // (3 * LANES)
    width //= 3
    half, model = grad_m.shape
    quarter = model // 4
    column = lambda part: pl.BlockSpec((total, LANES), lambda i, w: (0, 3 * pair + part))
    piece = pl.BlockSpec((quarter, 4 * LANES), lambda i, w: (0, pair))
    in_specs = [
        column(0), column(1), column(2),
        whole((width, total)), whole((width, total)),
        whole((half, model)), whole((half, model)),
    ]
    in_specs += out_weight_specs(width // 2, model)[:2]
    in_specs += [
        pl.BlockSpec((1, 8, total), lambda i, w: (pair, 0, 0)),
        whole((total, LANES)), whole((total, LANES)),
        whole((model, total)),
    ]
    args = [
        qkv, qkv, qkv, ctx_t, ctx_got_t, grad_m, grad_o, w_out, w_out, lse, *tables, normed_t,
    ]
    last = pair == pairs - 1
    out_specs = [piece] * 4
    out_shape = [((quarter, 4 * width), BF16)] * 4
    if last:
        in_specs += [whole((total, 3 * LANES))] * (pairs - 1) + [whole(weight.shape)]
        args += [*early, weight]
        out_specs += [whole((half, model))] * 2
        out_shape += [((half, model), F32), ((half, model), BF16)]
    else:
        out_specs.append(whole((total, 3 * LANES)))
        out_shape.append(((total, 3 * LANES), BF16))
    aliases = {}
    if pieces:
        aliases = {1 + len(args) + k: k for k in range(4)}
        in_specs += [pl.BlockSpec(memory_space=pl.ANY)] * 4
        args += list(pieces)
    return call(
        functools.partial(
            attend_back_kernel, tile=256, score_scale=HD ** (-0.5), pair=pair, pairs=pairs
        ),
        (1,), in_specs, out_specs, out_shape,
        [
            pltpu.VMEM((total, LANES), BF16),
            pltpu.VMEM((total, model), BF16),
            pltpu.VMEM((total, LANES), BF16),
            pltpu.VMEM((total, LANES), BF16),
            pltpu.VMEM((LANES, total), F32),
            pltpu.VMEM((total, LANES), F32),
            pltpu.VMEM((total, LANES), F32),
            pltpu.VMEM((model, 3 * LANES), BF16),
            pltpu.VMEM((2, width, LANES), BF16),
        ],
        SMALL, aliases,
    )(where, *args)


def tokens_grad_kernel(
    where_ref,
    keep_ref, recv_ref, back_ref, got_ref, grad_res_ref, gain_ref, keep_out_ref, send_out_ref, sums_ref,
):
    step = pl.program_id(0)
    values = jnp.where(step == 0, recv_ref[...], keep_ref[...]).astype(F32)
    normal, inverse = normalize(values)
    back = back_ref[...] + got_ref[...].astype(F32)
    gains = jnp.sum(back * normal, axis=0, keepdims=True)
    shifts = jnp.sum(back, axis=0, keepdims=True)
    grad = (grad_res_ref[...] + norm_back(back, row_vector(gain_ref), normal, inverse)).astype(BF16)

    @pl.when(step == 0)
    def _():
        sums_ref[0:1, :] = gains
        sums_ref[1:2, :] = shifts
        send_out_ref[...] = grad

    @pl.when(step == 1)
    def _():
        sums_ref[0:1, :] += gains
        sums_ref[1:2, :] += shifts
        keep_out_ref[0] = grad


def tokens_grad_call(where, keep, recv, back, got, grad_res, gain):
    rows, width = keep.shape
    row = pl.BlockSpec((rows, width), lambda i, w: (1 - i, 0))
    return call(
        tokens_grad_kernel,
        (2,),
        [whole((rows, width))] * 2 + [row] * 3 + [whole((width,))],
        [
            pl.BlockSpec((1, rows, width), lambda i, w: (w[ROW], 0, 0)),
            whole((rows, width)),
            whole((8, width)),
        ],
        [((2, rows, width), BF16), ((rows, width), BF16), ((8, width), F32)],
        [],
        SMALL,
    )(where, keep, recv, back, got, grad_res, gain)


def local(
    tokens, gain_one, shift_one, w_query, w_key, w_value, w_out, gain_two, shift_two, w_up, w_down,
    cotangent, lengths,
):
    row_count, piece, width = tokens.shape
    n_dp = lax.axis_size("dp")
    n_seq = lax.axis_size("seq")
    count = n_dp // 4
    place = lax.axis_index("seq")
    core, row = place % 2, place // 2
    data = lax.axis_index("dp")
    high = data // count
    side = (data // (count // 2)) % 2
    total = n_seq * piece
    group = width // n_seq

    tok_recv = swap(pick(tokens, 1 - row), "seq", 2)
    tok_keep = pick(tokens, row)
    tok_keep_o = swap(tok_keep, "seq", 1)
    cot_keep = pick(cotangent, row)
    cot_recv = swap(pick(cotangent, 1 - row), "seq", 2)

    where = jnp.stack(
        [
            core, row, side, pick(lengths, row),
            2 * row + core, 2 * (1 - row) + core, 2 * row + 1 - core, 2 * (1 - row) + 1 - core,
        ]
    ).astype(jnp.int32)
    tables = tuple(jnp.asarray(table) for table in rotary_tables(total))
    out_blocks = w_out.reshape(n_seq, group, width)

    qkv, normed_t, w_qkv = project_call(
        0, where, tok_keep, tok_keep_o, gain_one, shift_one, (w_query, w_key, w_value), tables, ()
    )
    tok_recv, qkv, normed_t = together(tok_recv, qkv, normed_t)
    tok_recv_o = swap(tok_recv, "seq", 1)
    qkv, normed_t = project_call(
        1, where, tok_recv, tok_recv_o, gain_one, shift_one, (w_qkv,), tables, (qkv, normed_t)
    )
    ctx_m, ctx_o, ctx_t, lse = attend_call(where, qkv)
    ctx_m, ctx_o, ctx_t, cot_keep, cot_recv = together(ctx_m, ctx_o, ctx_t, cot_keep, cot_recv)
    ctx_got = swap(ctx_o, "seq", 1)
    residual, normed_two = residual_call(
        where, tok_keep, tok_recv, ctx_m, ctx_got, out_blocks, gain_two, shift_two
    )
    normed_two_o = swap(normed_two, "seq", 1)
    cotangents = (cot_keep, cot_recv, swap(cot_keep, "seq", 1), swap(cot_recv, "seq", 1))
    ctx_got_t = swap(ctx_t, "seq", 1)
    up_send, up_keep, down_send, down_keep, out_m, out_o, back_m, back_o = feed_call(
        where, normed_two, normed_two_o, cotangents, w_up, w_down
    )
    back_got = swap(back_o, "seq", 1)
    out_got = swap(out_o, "seq", 1)
    out_buf, out_send, grad_res, grad_low, sums_two = middle_call(
        where, residual, out_m, out_got, back_m, back_got, cot_keep, cot_recv, gain_two
    )
    grad_low_o = swap(grad_low, "seq", 1)

    up_got = swap(up_send, "seq", 2)
    down_got = swap(down_send, "dp", count // 2)
    block_rows = width // n_dp

    pairs = qkv.shape[1] // (3 * LANES)
    early, pieces = [], ()
    def up_part(index):
        shape = (4, 2, count // 2 * block_rows, width)
        kept = pick(up_keep.reshape(shape), index, 1).astype(F32)
        return kept + pick(up_got.reshape(shape), index, 1).astype(F32)

    def down_part(index):
        shape = (2, 2, 2 * group, -1)
        kept = pick(down_keep.reshape(shape), index, 1).astype(F32)
        return kept + pick(down_got.reshape(shape), index, 1).astype(F32)

    groups = [[k * count + j for k in range(4)] for j in range(count)]

    def scatter(values):
        return lax.psum_scatter(
            values.reshape(-1, values.shape[2]), "dp", scatter_dimension=0,
            axis_index_groups=groups, tiled=True,
        )

    def upper(up_got2, down_got2):
        up = up_part(side) + up_got2.astype(F32)
        down = (down_part(row) + down_got2.astype(F32)).reshape(4, group, -1)
        if count > 2:
            up = up.reshape(4, count // 2, block_rows, width)
            bit = count // 4
            while bit > 0:
                mine = (data // bit) % 2
                size, lanes = up.shape[1] // 2, down.shape[2] // 2
                sent = lax.dynamic_slice_in_dim(up, (1 - mine) * size, size, 1).astype(BF16)
                up = lax.dynamic_slice_in_dim(up, mine * size, size, 1) + swap(sent, "dp", bit)
                sent = lax.dynamic_slice_in_dim(down, (1 - mine) * lanes, lanes, 2).astype(BF16)
                down = lax.dynamic_slice_in_dim(down, mine * lanes, lanes, 2) + swap(sent, "dp", bit)
                bit //= 2
            up = up.reshape(4, block_rows, width)
        lanes = down.shape[2]
        folds = width // lanes
        size = group // folds
        down = jnp.concatenate([down[:, k * size : (k + 1) * size] for k in range(folds)], axis=2)
        return jnp.concatenate([up.astype(BF16), down.astype(BF16)], axis=1)

    for pair in range(pairs):
        if pair == pairs - 2:
            up_got, down_got, *early = together(up_got, down_got, *early)
            up_sent, down_sent = up_part(1 - side).astype(BF16), down_part(1 - row).astype(BF16)
            up_sent, down_sent, out_send, *early = together(up_sent, down_sent, out_send, *early)
            up_got2 = swap(up_sent, "dp", count // 2)
            down_got2 = swap(down_sent, "seq", 2)
            out_back = swap(out_send, "seq", 2)
        if pair == pairs - 1:
            up_got2, down_got2, *early = together(up_got2, down_got2, *early)
            both = upper(up_got2, down_got2)
            both, *early = together(both, *early)
            feed_grads = scatter(both)
        pieces = list(attend_back_call(
            pair, where, qkv, ctx_t, ctx_got_t, grad_low, grad_low_o, out_blocks, lse, tables,
            normed_t, early, w_qkv, pieces,
        ))
        if pair < pairs - 1:
            early.append(pieces.pop())
    *pieces, out_back = together(*pieces, out_back)
    piece0, piece1, piece2, piece3, normed_m, normed_o = pieces
    normed_got = swap(normed_o, "seq", 1)
    tok_buf, tok_send, sums_one = tokens_grad_call(
        where, tok_keep, tok_recv, normed_m, normed_got, grad_res, gain_one
    )

    sums = jnp.concatenate([sums_one[:2], sums_two[:2]], axis=0)
    sums = sums + swap(sums, "seq", 1)
    inner = count // 2
    shape = (2, 2, width // 16, -1)
    if count == 2:
        got0, got2 = swap(piece0, "dp", inner), swap(piece2, "seq", 2)
        got0, got2, tok_send = together(got0, got2, tok_send)
        lanes = piece0.shape[1]

        def packed(values, sums):
            values = values.astype(BF16)
            values = values.reshape(-1, values.shape[-1])
            top = sums.astype(BF16)
            rest = (sums - top.astype(F32)).astype(BF16)
            return jnp.concatenate([values, jnp.concatenate([top, rest]).reshape(-1, values.shape[1])])

        def unpacked(got):
            size = 2 * sums.size // got.shape[1]
            ends = got[-size:].astype(F32).reshape(2, 4, width)
            return got[:-size].astype(F32), ends[0] + ends[1]

        def first(index):
            kept = pick(piece1.reshape(shape), index, 1).astype(F32)
            return kept + pick(got0.reshape(shape), index, 1).astype(F32)

        def second(index):
            kept = pick(piece3.reshape(shape), index, 1).astype(F32)
            return kept + pick(got2.reshape(shape), index, 1).astype(F32)

        got_first = swap(first(1 - row).astype(BF16), "seq", 2)
        got_second = swap(packed(second(1 - side), sums), "dp", inner)
        got_second, more = unpacked(got_second)
        sums = sums + more
        tok_send, got_first = together(tok_send, got_first)
        tok_back = swap(tok_send, "seq", 2)
        both = (
            first(row) + got_first.astype(F32),
            second(side) + got_second.reshape(2, width // 16, lanes),
        )
        both = jnp.stack(both, axis=1).reshape(4, width // 16, lanes)
        got = [swap(packed(pick(both, high ^ k), sums), "dp", count * k) for k in (1, 2, 3)]
        tok_back, feed_grads, *got = together(tok_back, feed_grads, *got)
        summed = pick(both, high)
        for one in got:
            values, more = unpacked(one)
            summed, sums = summed + values, sums + more
        summed = summed.reshape(-1, pairs, 4, LANES).transpose(0, 2, 1, 3)
        summed = summed.reshape(-1, 4, 2, group)
        other = swap(packed(pick(summed, 1 - row, 2).reshape(-1, width), sums), "seq", 2)
        other, more = unpacked(other)
        sums = sums + more
        mine = pick(summed, row, 2).reshape(-1, width)
        ordered = jnp.where(row == 0, jnp.concatenate([mine, other]), jnp.concatenate([other, mine]))
    else:
        sides = jnp.stack([piece0, piece1]).reshape((2,) + shape)
        sides = jnp.stack([pick(sides, jnp.where(side == k, 1, 0)) for k in (0, 1)], 1)
        halves = jnp.stack([piece2, piece3]).reshape((2,) + shape)
        halves = jnp.stack([pick(halves, jnp.where(row == k, 1, 0)) for k in (0, 1)], 2)
        summed = jnp.stack([sides, halves], 1).reshape(width, pairs, 4, LANES).transpose(0, 2, 1, 3)
        summed = summed.reshape(width, 4, 2, group)
        other = swap(pick(summed, 1 - row, 2), "seq", 2).astype(F32)
        summed = (pick(summed, row, 2).astype(F32) + other).astype(BF16).reshape(width, -1)
        ordered = lax.psum_scatter(summed, "dp", scatter_dimension=0, tiled=True).astype(F32)
        tok_back = swap(tok_send, "seq", 2)
        sums = sums + swap(sums, "seq", 2)
        bit = 1
        while bit < n_dp:
            sums = sums + swap(sums, "dp", bit)
            bit *= 2
    ordered = [ordered[:, k * group : (k + 1) * group] for k in range(4)]

    exchange = []
    for d in range(n_dp):
        for s in range(n_seq):
            second_bit = (d // count) % 2
            to_d = d + (s % 2 - second_bit) * count
            to_s = s - s % 2 + second_bit
            exchange.append((d * n_seq + s, to_d * n_seq + to_s))
    grad_up, grad_down = feed_grads[:block_rows].astype(F32), feed_grads[block_rows:]
    grad_down = lax.ppermute(grad_down, ("dp", "seq"), exchange).astype(F32)
    lanes = w_down.shape[0] // n_dp
    grad_down = jnp.concatenate(
        [grad_down[:, k * lanes : (k + 1) * lanes] for k in range(width // lanes)], axis=0
    ).T

    output = lax.dynamic_update_slice(out_buf, out_back[None], (1 - row, 0, 0))
    grad_tokens = lax.dynamic_update_slice(tok_buf, tok_back[None], (1 - row, 0, 0))
    return (
        output,
        grad_tokens,
        sums[0],
        sums[1],
        ordered[0],
        ordered[1],
        ordered[2],
        ordered[3],
        sums[2],
        sums[3],
        grad_up,
        grad_down,
    )


def solution(mesh):
    tokens = P("dp", "seq", None)
    weights = P("dp", "seq")
    return jax.shard_map(
        local,
        mesh=mesh,
        in_specs=(tokens,) + (P(),) * 10 + (tokens, P("dp")),
        out_specs=(tokens, tokens, P(), P(), weights, weights, weights, weights, P(), P(), weights, weights),
        check_vma=False,
    )
```

```python
import functools

import jax
import jax.numpy as jnp
import numpy as np
from jax import lax
from jax.experimental import pallas as pl
from jax.experimental.pallas import tpu as pltpu
from jax.sharding import PartitionSpec as P

HD = 64
EPSILON = 1e-05
MASKED = -1000000000.0
LANES = 128
BF16 = jnp.bfloat16
F32 = jnp.float32
CORE, ROW, SIDE, LENGTH, SPOT = 0, 1, 2, 3, 4


def swap(values, axis, bit):
    count = lax.axis_size(axis)
    return lax.ppermute(values, axis, [(i, i ^ bit) for i in range(count)])


def together(*values):
    return lax.optimization_barrier(values)


def pick(values, index, axis=0):
    return lax.dynamic_index_in_dim(values, index, axis, keepdims=False)


def dot(left, right):
    return jnp.dot(left, right, preferred_element_type=F32)


def dot_back(left, right):
    return lax.dot_general(left, right, (((1,), (1,)), ((), ())), preferred_element_type=F32)


def normalize(values):
    average = jnp.mean(values, axis=-1, keepdims=True)
    centred = values - average
    variance = jnp.mean(centred * centred, axis=-1, keepdims=True)
    inverse = lax.rsqrt(variance + EPSILON)
    return centred * inverse, inverse


def norm_back(grad, gain, normal, inverse):
    scaled = grad * gain
    first = jnp.mean(scaled, axis=-1, keepdims=True)
    second = jnp.mean(scaled * normal, axis=-1, keepdims=True)
    return (scaled - first - normal * second) * inverse


def row_vector(ref):
    return ref[...].reshape(1, ref.shape[0])


def swap_halves(values):
    lane = lax.broadcasted_iota(jnp.int32, values.shape, 1)
    up = pltpu.roll(values, LANES - HD // 2, 1)
    down = pltpu.roll(values, HD // 2, 1)
    return jnp.where(lane % HD < HD // 2, up, down)


def rotary_tables(length):
    lane = np.arange(LANES)
    frequency = 10000.0 ** (-2.0 * (lane % (HD // 2)) / HD)
    angles = np.arange(length)[:, None] * frequency[None, :]
    sign = np.where(lane % HD < HD // 2, -1.0, 1.0)
    return np.cos(angles).astype(np.float32), (sign * np.sin(angles)).astype(np.float32)


def kept_rows(where_ref, block, rows, lanes):
    spot = lax.broadcasted_iota(jnp.int32, (rows, lanes), 0) + where_ref[SPOT + block] * rows
    return spot < where_ref[LENGTH]


SMALL = pl.CostEstimate(flops=1, bytes_accessed=1, transcendentals=0)


def whole(shape):
    return pl.BlockSpec(shape, lambda *_: (0,) * len(shape))


def call(kernel, grid, in_specs, out_specs, out_shape, scratch, estimate, aliases=None, mib=16):
    return pl.pallas_call(
        kernel,
        grid_spec=pltpu.PrefetchScalarGridSpec(
            num_scalar_prefetch=1,
            grid=grid,
            in_specs=in_specs,
            out_specs=out_specs,
            scratch_shapes=scratch,
        ),
        out_shape=[jax.ShapeDtypeStruct(shape, kind) for shape, kind in out_shape],
        input_output_aliases=aliases or {},
        compiler_params=pltpu.CompilerParams(vmem_limit_bytes=mib * 1024 * 1024),
        cost_estimate=estimate,
    )


def pair_columns(ref, core, pair):
    group = ref.shape[1] // 4
    pieces = []
    start, end = pair * LANES, (pair + 1) * LANES
    if start < group:
        pieces.append(ref[:, core * group + start : core * group + min(end, group)])
    if end > group:
        begin = max(start, group)
        pieces.append(ref[:, (1 + core) * group + begin : (1 + core) * group + end])
    return pieces[0] if len(pieces) == 1 else jnp.concatenate(pieces, axis=1)


def project_kernel(where_ref, mine_ref, other_ref, gain_ref, shift_ref, *rest, first, pairs):
    step = pl.program_id(0)
    if first:
        wq_ref, wk_ref, wv_ref, cos_ref, sin_ref, qkv_ref, normed_t_ref, weight_ref = rest

        @pl.when(step == 0)
        def _():
            for core in range(2):

                @pl.when(where_ref[CORE] == core)
                def _():
                    for part, ref in enumerate((wq_ref, wk_ref, wv_ref)):
                        for pair in range(pairs):
                            start = (3 * pair + part) * LANES
                            weight_ref[:, start : start + LANES] = pair_columns(ref, core, pair)
    else:
        weight_ref, cos_ref, sin_ref, _, _, qkv_ref, normed_t_ref = rest
    values = jnp.where(step == 0, mine_ref[...], other_ref[...]).astype(F32)
    normal, _ = normalize(values)
    normed = (normal * row_vector(gain_ref) + row_vector(shift_ref)).astype(BF16)
    normed_t_ref[...] = normed.T
    cosine, sine = cos_ref[...], sin_ref[...]
    width = 3 * LANES
    for pair in range(pairs):
        out = dot(normed, weight_ref[:, pair * width : (pair + 1) * width])
        for part in range(3):
            piece = out[:, part * LANES : (part + 1) * LANES]
            if part < 2:
                piece = piece * cosine + swap_halves(piece) * sine
                if part == 0:
                    piece = piece * (HD ** (-0.5))
            start = pair * width + part * LANES
            qkv_ref[:, start : start + LANES] = piece.astype(BF16)


def project_call(turn, where, mine, other, gain, shift, weights, tables, previous):
    rows, width = mine.shape
    out_width = 3 * width // 2
    total = 4 * rows
    block = lambda i, w: (2 * i + turn, 0)
    table = pl.BlockSpec((rows, LANES), lambda i, w: (w[SPOT + 2 * i + turn], 0))
    in_specs = [whole((rows, width))] * 2 + [whole((width,))] * 2
    in_specs += [whole(weight.shape) for weight in weights] + [table, table]
    out_specs = [
        pl.BlockSpec((rows, out_width), block),
        pl.BlockSpec((width, rows), lambda i, w: (0, 2 * i + turn)),
    ]
    out_shape = [((total, out_width), BF16), ((width, total), BF16)]
    aliases = {}
    if previous:
        aliases = {1 + len(in_specs): 0, 2 + len(in_specs): 1}
        in_specs += [pl.BlockSpec(memory_space=pl.ANY)] * 2
    else:
        out_specs.append(whole((width, out_width)))
        out_shape.append(((width, out_width), BF16))
    return call(
        functools.partial(project_kernel, first=not previous, pairs=out_width // (3 * LANES)),
        (2,), in_specs, out_specs, out_shape, [],
        SMALL, aliases, 20,
    )(where, mine, other, gain, shift, *weights, *tables, *previous)


def mask_lane(lane, head, keys, bias):
    return jnp.where(lane == (HD if head == 0 else 0), bias, keys)


def only_head(lane, head, values):
    return jnp.where(lane // HD == head, values, jnp.zeros_like(values))


def with_one(lane, head, values):
    one = lane == (HD if head == 0 else 0)
    return jnp.where(one, jnp.ones_like(values), only_head(lane, head, values))


def fill_bias(where_ref, bias_ref):
    rows = bias_ref.shape[0] // 4
    for block in range(4):
        kept = kept_rows(where_ref, block, rows, LANES)
        bias_ref[block * rows : (block + 1) * rows, :] = jnp.where(kept, 0.0, MASKED).astype(BF16)


def attend_kernel(
    where_ref, query_ref, key_ref, value_ref, mine_ref, other_ref, ctx_t_ref, lse_ref, bias_ref, ctx_ref,
    *, tile,
):
    total = query_ref.shape[0]
    lane = lax.broadcasted_iota(jnp.int32, (1, LANES), 1)

    @pl.when(pl.program_id(0) == 0)
    def _():
        fill_bias(where_ref, bias_ref)

    keys = key_ref[...]
    values_t = value_ref[...].T
    for head in range(2):
        key_aug = mask_lane(lane, head, keys, bias_ref[...])
        for start in range(0, total, tile):
            queries = with_one(lane, head, query_ref[start : start + tile, :])
            scores = dot_back(key_aug, queries)
            highest = jnp.max(scores, axis=0, keepdims=True)
            weights = jnp.exp(scores - highest)
            sums = jnp.sum(weights, axis=0, keepdims=True)
            context = dot(values_t[head * HD : (head + 1) * HD, :], weights.astype(BF16))
            ctx_ref[head * HD : (head + 1) * HD, start : start + tile] = context / sums
            lse_ref[0, head : head + 1, start : start + tile] = highest + jnp.log(sums)
    ctx_t_ref[...] = ctx_ref[...].astype(BF16)
    contexts = ctx_ref[...].T.astype(BF16)
    mine_ref[...] = contexts[: total // 2]
    other_ref[...] = contexts[total // 2 :]


def attend_call(where, qkv):
    total, width = qkv.shape
    pairs = width // (3 * LANES)
    width //= 3
    half = total // 2
    column = lambda part: pl.BlockSpec((total, LANES), lambda p, w: (0, 3 * p + part))
    out_column = pl.BlockSpec((half, LANES), lambda p, w: (0, p))
    return call(
        functools.partial(attend_kernel, tile=total),
        (pairs,),
        [column(0), column(1), column(2)],
        [
            out_column, out_column,
            pl.BlockSpec((LANES, total), lambda p, w: (p, 0)),
            pl.BlockSpec((1, 8, total), lambda p, w: (p, 0, 0)),
        ],
        [((half, width), BF16), ((half, width), BF16), ((width, total), BF16), ((pairs, 8, total), F32)],
        [pltpu.VMEM((total, LANES), BF16), pltpu.VMEM((LANES, total), F32)],
        SMALL, mib=32,
    )(where, qkv, qkv, qkv)


def stack_rows(refs):
    return jnp.concatenate([ref[0] for ref in refs], axis=0)


def residual_kernel(
    where_ref, keep_ref, recv_ref, mine_ref, got_ref, w0_ref, w1_ref, w2_ref, w3_ref,
    gain_ref, shift_ref, res_ref, normed_ref,
):
    step = pl.program_id(0)
    values = jnp.where(step == 0, keep_ref[...], recv_ref[...]).astype(F32)
    attended = dot(mine_ref[...], stack_rows((w0_ref, w1_ref)))
    attended += dot(got_ref[...], stack_rows((w2_ref, w3_ref)))
    residual = values + attended
    res_ref[...] = residual
    normal, _ = normalize(residual)
    normed_ref[...] = (normal * row_vector(gain_ref) + row_vector(shift_ref)).astype(BF16)


def out_weight_specs(group, width):
    places = (
        lambda w: w[CORE],
        lambda w: 2 + w[CORE],
        lambda w: 1 - w[CORE],
        lambda w: 3 - w[CORE],
    )
    return [pl.BlockSpec((1, group, width), lambda i, w, at=at: (at(w), 0, 0)) for at in places]


def residual_call(where, keep, recv, ctx_mine, ctx_got, w_out, gain, shift):
    rows, width = keep.shape
    heads = ctx_mine.shape[1]
    row = lambda lanes: pl.BlockSpec((rows, lanes), lambda i, w: (i, 0))
    return call(
        residual_kernel,
        (2,),
        [whole((rows, width))] * 2 + [row(heads)] * 2
        + out_weight_specs(heads // 2, width) + [whole((width,))] * 2,
        [row(width)] * 2,
        [((2 * rows, width), F32), ((2 * rows, width), BF16)],
        [],
        SMALL, mib=16,
    )(where, keep, recv, ctx_mine, ctx_got, w_out, w_out, w_out, w_out, gain, shift)


def gelu_both(values):
    root = 0.7978845608028654
    bend = (root * 0.044715) * (values * values)
    half = 0.5 * jnp.tanh(values * (root + bend)) + 0.5
    steep = values * (2.0 * root + 6.0 * bend)
    return values * half, half * ((1.0 - half) * steep + 1.0)


def fill_cotangent(where_ref, refs, grad_ref):
    rows, width = refs[0].shape
    for place, ref in enumerate(refs):
        kept = kept_rows(where_ref, place, rows, width)
        grad_ref[place * rows : (place + 1) * rows, :] = jnp.where(kept, ref[...], jnp.zeros_like(ref))


def feed_kernel(
    where_ref,
    normed_m_ref, normed_o_ref, cot0_ref, cot1_ref, cot2_ref, cot3_ref, up_ref, down_ref,
    *rest, tile, last,
):
    if last:
        before_ref, up_before_ref, *rest = rest
        up0_ref, up1_ref, send_ref, keep_ref, active_ref, back_m_ref, back_o_ref = rest[:7]
        normed_ref, grad_ref, normed_t_ref, grad_t_ref, hidden_ref = rest[7:]
    else:
        up0_ref, up1_ref, send_ref, keep_ref, active_ref, hidden_ref = rest[:6]
        normed_ref, grad_ref, normed_t_ref, grad_t_ref = rest[6:]
    half, width = normed_m_ref.shape
    block = up_ref.shape[1]
    normed_ref[:half, :] = normed_m_ref[...]
    normed_ref[half:, :] = normed_o_ref[...]
    fill_cotangent(where_ref, (cot0_ref, cot1_ref, cot2_ref, cot3_ref), grad_ref)
    normed_t_ref[...] = normed_ref[...].T
    grad_t_ref[...] = grad_ref[...].T
    for start in range(0, block, tile):
        span = slice(start, start + tile)
        hidden = dot(normed_ref[...], up_ref[:, span])
        active, slope = gelu_both(hidden)
        active_ref[:, span] = active.astype(BF16)
        grad_active = dot_back(grad_ref[...], down_ref[span, :])
        hidden_ref[:, span] = (grad_active * slope).astype(BF16)
    up_grad = dot(normed_t_ref[...], hidden_ref[...]).astype(BF16)
    up0_ref[...] = up_grad[: width // 2]
    up1_ref[...] = up_grad[width // 2 :]
    down_grad = dot(grad_t_ref[...], active_ref[...]).astype(BF16)
    part = block // 2
    for side in range(2):
        piece = down_grad[:, side * part : (side + 1) * part]

        @pl.when(where_ref[SIDE] == side)
        def _():
            keep_ref[...] = piece

        @pl.when(where_ref[SIDE] != side)
        def _():
            send_ref[...] = piece

    if last:
        back = dot_back(before_ref[...], up_before_ref[...]) + dot_back(hidden_ref[...], up_ref[...])
        back_m_ref[...] = back[:half]
        back_o_ref[...] = back[half:].astype(BF16)


def feed_high(last, w):
    return w[ROW] if last else 1 - w[ROW]


def feed_call(last, where, normed_m, normed_o, cotangents, w_up, w_down, before=()):
    half, width = normed_m.shape
    total = 2 * half
    block = w_up.shape[1] // 4
    part = block // 2
    token = whole((half, width))
    up_block = lambda last: pl.BlockSpec(
        (width, block), lambda i, w: (0, 2 * feed_high(last, w) + w[CORE])
    )
    down_block = pl.BlockSpec((block, width), lambda i, w: (2 * feed_high(last, w) + w[CORE], 0))
    in_specs = [token, token] + [whole((half // 2, width))] * 4 + [up_block(last), down_block]
    args = [normed_m, normed_o, *cotangents, w_up, w_down]
    out_shape = [
        ((width // 2, block), BF16),
        ((width // 2, block), BF16),
        ((width, part), BF16),
        ((width, part), BF16),
        ((total, block), BF16),
    ]
    scratch = [
        pltpu.VMEM((total, width), BF16),
        pltpu.VMEM((total, width), BF16),
        pltpu.VMEM((width, total), BF16),
        pltpu.VMEM((width, total), BF16),
    ]
    if last:
        in_specs += [whole((total, block)), up_block(False)]
        args += [*before, w_up]
        out_shape += [((half, width), F32), ((half, width), BF16)]
        scratch.append(pltpu.VMEM((total, block), BF16))
    else:
        out_shape.append(((total, block), BF16))
    return call(
        functools.partial(feed_kernel, tile=256, last=last),
        (1,), in_specs, [whole(shape) for shape, _ in out_shape], out_shape, scratch, SMALL, mib=36,
    )(where, *args)


def feed_out_kernel(where_ref, first_ref, last_ref, down0_ref, down1_ref, mine_ref, other_ref):
    out = dot(first_ref[...], down0_ref[...]) + dot(last_ref[...], down1_ref[...])

    @pl.when(pl.program_id(0) == 0)
    def _():
        other_ref[...] = out.astype(BF16)

    @pl.when(pl.program_id(0) == 1)
    def _():
        mine_ref[...] = out


def feed_out_call(where, first, last, w_down):
    total, block = first.shape
    width = w_down.shape[1]
    half = total // 2
    row = pl.BlockSpec((half, block), lambda i, w: (1 - i, 0))
    down = [
        pl.BlockSpec((block, width), lambda i, w, last=last: (2 * feed_high(last, w) + w[CORE], 0))
        for last in (False, True)
    ]
    return call(
        feed_out_kernel,
        (2,),
        [row, row, *down],
        [whole((half, width))] * 2,
        [((half, width), F32), ((half, width), BF16)],
        [], SMALL, mib=20,
    )(where, first, last, w_down, w_down)


def output_kernel(where_ref, res_ref, out_ref, got_ref, send_ref, keep_ref):
    step = pl.program_id(0)
    output = res_ref[...] + out_ref[...] + got_ref[...].astype(F32)
    kept = kept_rows(where_ref, 1 - step, *output.shape)
    output = jnp.where(kept, output, jnp.zeros_like(output)).astype(BF16)

    @pl.when(step == 0)
    def _():
        send_ref[...] = output

    @pl.when(step == 1)
    def _():
        keep_ref[0] = output


def output_call(where, residual, out, got):
    half, width = residual.shape
    rows = half // 2
    row = pl.BlockSpec((rows, width), lambda i, w: (1 - i, 0))
    return call(
        output_kernel,
        (2,),
        [row] * 3,
        [whole((rows, width)), pl.BlockSpec((1, rows, width), lambda i, w: (w[ROW], 0, 0))],
        [((rows, width), BF16), ((2, rows, width), BF16)],
        [], SMALL, mib=12,
    )(where, residual, out, got)


def add_sums(sums_ref, step, row, gains, shifts):
    @pl.when(step == 0)
    def _():
        sums_ref[...] = jnp.zeros_like(sums_ref)

    sums_ref[row : row + 1, :] += gains
    sums_ref[row + 1 : row + 2, :] += shifts


def middle_kernel(
    where_ref,
    res_ref, back_ref, back_got_ref, cot0_ref, cot1_ref, gain_ref, grad_low_ref, sums_ref,
):
    step = pl.program_id(0)
    residual = res_ref[...]
    kept = kept_rows(where_ref, step, *residual.shape)
    normal, inverse = normalize(residual)
    back = back_ref[...] + back_got_ref[...].astype(F32)
    gains = jnp.sum(back * normal, axis=0, keepdims=True)
    shifts = jnp.sum(back, axis=0, keepdims=True)

    add_sums(sums_ref, step, 2, gains, shifts)
    cotangent = jnp.where(step == 0, cot0_ref[...], cot1_ref[...]).astype(F32)
    cotangent = jnp.where(kept, cotangent, jnp.zeros_like(cotangent))
    grad = cotangent + norm_back(back, row_vector(gain_ref), normal, inverse)
    grad_low_ref[...] = grad.astype(BF16)


def middle_call(where, residual, back_m, back_got, cot_keep, cot_recv, gain):
    half, width = residual.shape
    rows = half // 2
    row = pl.BlockSpec((rows, width), lambda i, w: (i, 0))
    return call(
        middle_kernel,
        (2,),
        [row] * 3 + [whole((rows, width))] * 2 + [whole((width,))],
        [row, whole((8, width))],
        [((half, width), BF16), ((8, width), F32)],
        [], SMALL, mib=12,
    )(where, residual, back_m, back_got, cot_keep, cot_recv, gain)


def piece_order(where_ref):
    side, row = where_ref[SIDE], where_ref[ROW]
    order = []
    for kept in (0, 1):
        mine = side if kept else 1 - side
        order += [8 * high + 2 * mine + half for high in (0, 1) for half in (0, 1)]
    for kept in (0, 1):
        mine = row if kept else 1 - row
        order += [8 * high + 4 + 2 * one + mine for high in (0, 1) for one in (0, 1)]
    return order


def attend_back_kernel(
    where_ref,
    query_ref, key_ref, value_ref, ctx_mine_ref, ctx_got_ref, grad_m_ref, grad_o_ref,
    w0_ref, w1_ref, lse_ref, cos_ref, sin_ref, normed_t_ref, *rest,
    tile, score_scale, pair, pairs,
):
    if pair < pairs - 1:
        rest = rest[4 if pair else 0 :]
        out_refs, grads_ref = rest[:4], rest[4]
        rest = rest[5:]
    else:
        early_refs, weight_ref = rest[: pairs - 1], rest[pairs - 1]
        rest = rest[pairs + 4 :]
        out_refs, back_m_ref, back_o_ref = rest[:4], rest[4], rest[5]
        rest = rest[6:]
    bias_ref, grad_ref, columns_ref, gctx_ref, dqt_ref, dk_acc, dv_acc, qkv_ref, own_ref = rest
    total = query_ref.shape[0]
    half = total // 2
    model = grad_m_ref.shape[1]
    lane = lax.broadcasted_iota(jnp.int32, (1, LANES), 1)
    unit = model // 16
    group = model // 4
    fill_bias(where_ref, bias_ref)
    grad_ref[:half, :] = grad_m_ref[...]
    grad_ref[half:, :] = grad_o_ref[...]
    for core in range(2):

        @pl.when(where_ref[CORE] == core)
        def _():
            columns_ref[...] = pair_columns(grad_ref, core, pair)

    wout = jnp.concatenate([w0_ref[0], w1_ref[0]], axis=0)[pair * LANES : (pair + 1) * LANES]
    gctx = dot_back(grad_ref[...], wout).astype(BF16)
    gctx_ref[...] = gctx
    ctx_t = ctx_mine_ref[pair * LANES : (pair + 1) * LANES, :]
    products = gctx.astype(F32).T * ctx_t.astype(F32)
    keys = key_ref[...]
    keys_t = keys.T
    values = value_ref[...]
    for head in range(2):
        key_aug = mask_lane(lane, head, keys, bias_ref[...])
        delta = jnp.sum(products[head * HD : (head + 1) * HD, :], axis=0, keepdims=True)
        for start in range(0, total, tile):
            span = slice(start, start + tile)
            queries = query_ref[span, :]
            scores = dot_back(key_aug, with_one(lane, head, queries))
            weights = jnp.exp(scores - lse_ref[0, head : head + 1, span])
            grads = only_head(lane, head, gctx_ref[span, :])
            grad_weights = dot_back(values, grads)
            grad_scores = (weights * (grad_weights - delta[:, span])).astype(BF16)
            dv = dot(weights.astype(BF16), grads)
            dk = dot(grad_scores, only_head(lane, head, queries))
            dqt_ref[head * HD : (head + 1) * HD, span] = dot(
                keys_t[head * HD : (head + 1) * HD, :], grad_scores
            )
            if head == 0 and start == 0:
                dv_acc[...] = dv
                dk_acc[...] = dk
            else:
                dv_acc[...] += dv
                dk_acc[...] += dk
    rows = total // 4
    tables = []
    for ref in (cos_ref, sin_ref):
        tables.append(
            jnp.concatenate(
                [
                    ref[pl.ds(pl.multiple_of(where_ref[SPOT + block] * rows, rows), rows), :]
                    for block in range(4)
                ],
                axis=0,
            )
        )
    cosine, sine = tables
    dq = dqt_ref[...].T * score_scale
    dk = dk_acc[...]
    dq = (dq * cosine - swap_halves(dq) * sine).astype(BF16)
    dk = (dk * cosine - swap_halves(dk) * sine).astype(BF16)
    grads = jnp.concatenate([dq, dk, dv_acc[...].astype(BF16)], axis=1)
    qkv_ref[...] = dot(normed_t_ref[...], grads).astype(BF16)
    columns = columns_ref[...]
    turned = jnp.concatenate([columns[half:], columns[:half]], axis=0)
    own_ref[0] = dot(ctx_mine_ref[...], columns).astype(BF16)
    own_ref[1] = dot(ctx_got_ref[...], turned).astype(BF16)
    for place, source in enumerate(piece_order(where_ref)):
        ref = out_refs[place // 4]
        span = slice(place % 4 * unit, (place % 4 + 1) * unit)
        ref[span, : 3 * LANES] = qkv_ref[pl.ds(pl.multiple_of(source * unit, unit), unit), :]
        block = source // 4
        other = jnp.where(block % 2 == where_ref[CORE], 0, 1)
        inside = pl.multiple_of((block // 2) * group + (source % 4) * unit, unit)
        ref[span, 3 * LANES :] = own_ref[other, pl.ds(inside, unit), :]
    if pair < pairs - 1:
        grads_ref[...] = grads
    else:
        width = 3 * LANES
        back = dot_back(grads, weight_ref[:, pair * width :])
        for early, ref in enumerate(early_refs):
            back += dot_back(ref[...], weight_ref[:, early * width : (early + 1) * width])
        back_m_ref[...] = back[:half]
        back_o_ref[...] = back[half:].astype(BF16)


def attend_back_call(
    pair, where, qkv, ctx_t, ctx_got_t, grad_m, grad_o, w_out, lse, tables, normed_t, early, weight, pieces
):
    total, width = qkv.shape
    pairs = width // (3 * LANES)
    width //= 3
    half, model = grad_m.shape
    quarter = model // 4
    column = lambda part: pl.BlockSpec((total, LANES), lambda i, w: (0, 3 * pair + part))
    piece = pl.BlockSpec((quarter, 4 * LANES), lambda i, w: (0, pair))
    in_specs = [
        column(0), column(1), column(2),
        whole((width, total)), whole((width, total)),
        whole((half, model)), whole((half, model)),
    ]
    in_specs += out_weight_specs(width // 2, model)[:2]
    in_specs += [
        pl.BlockSpec((1, 8, total), lambda i, w: (pair, 0, 0)),
        whole((total, LANES)), whole((total, LANES)),
        whole((model, total)),
    ]
    args = [
        qkv, qkv, qkv, ctx_t, ctx_got_t, grad_m, grad_o, w_out, w_out, lse, *tables, normed_t,
    ]
    last = pair == pairs - 1
    out_specs = [piece] * 4
    out_shape = [((quarter, 4 * width), BF16)] * 4
    if last:
        in_specs += [whole((total, 3 * LANES))] * (pairs - 1) + [whole(weight.shape)]
        args += [*early, weight]
        out_specs += [whole((half, model))] * 2
        out_shape += [((half, model), F32), ((half, model), BF16)]
    else:
        out_specs.append(whole((total, 3 * LANES)))
        out_shape.append(((total, 3 * LANES), BF16))
    aliases = {}
    if pieces:
        aliases = {1 + len(args) + k: k for k in range(4)}
        in_specs += [pl.BlockSpec(memory_space=pl.ANY)] * 4
        args += list(pieces)
    return call(
        functools.partial(
            attend_back_kernel, tile=total, score_scale=HD ** (-0.5), pair=pair, pairs=pairs
        ),
        (1,), in_specs, out_specs, out_shape,
        [
            pltpu.VMEM((total, LANES), BF16),
            pltpu.VMEM((total, model), BF16),
            pltpu.VMEM((total, LANES), BF16),
            pltpu.VMEM((total, LANES), BF16),
            pltpu.VMEM((LANES, total), F32),
            pltpu.VMEM((total, LANES), F32),
            pltpu.VMEM((total, LANES), F32),
            pltpu.VMEM((model, 3 * LANES), BF16),
            pltpu.VMEM((2, width, LANES), BF16),
        ],
        SMALL, aliases, 44,
    )(where, *args)


def tokens_grad_kernel(
    where_ref,
    keep_ref, recv_ref, back_ref, got_ref, grad_res_ref, gain_ref, keep_out_ref, send_out_ref, sums_ref,
):
    step = pl.program_id(0)
    values = jnp.where(step == 0, recv_ref[...], keep_ref[...]).astype(F32)
    normal, inverse = normalize(values)
    back = back_ref[...] + got_ref[...].astype(F32)
    gains = jnp.sum(back * normal, axis=0, keepdims=True)
    shifts = jnp.sum(back, axis=0, keepdims=True)
    grad = (grad_res_ref[...].astype(F32) + norm_back(back, row_vector(gain_ref), normal, inverse)).astype(BF16)

    add_sums(sums_ref, step, 0, gains, shifts)

    @pl.when(step == 0)
    def _():
        send_out_ref[...] = grad

    @pl.when(step == 1)
    def _():
        keep_out_ref[0] = grad


def tokens_grad_call(where, keep, recv, back, got, grad_res, gain):
    rows, width = keep.shape
    row = pl.BlockSpec((rows, width), lambda i, w: (1 - i, 0))
    return call(
        tokens_grad_kernel,
        (2,),
        [whole((rows, width))] * 2 + [row] * 3 + [whole((width,))],
        [
            pl.BlockSpec((1, rows, width), lambda i, w: (w[ROW], 0, 0)),
            whole((rows, width)),
            whole((8, width)),
        ],
        [((2, rows, width), BF16), ((rows, width), BF16), ((8, width), F32)],
        [],
        SMALL, mib=12,
    )(where, keep, recv, back, got, grad_res, gain)


def local(
    tokens, gain_one, shift_one, w_query, w_key, w_value, w_out, gain_two, shift_two, w_up, w_down,
    cotangent, lengths,
):
    row_count, piece, width = tokens.shape
    n_dp = lax.axis_size("dp")
    n_seq = lax.axis_size("seq")
    count = n_dp // 4
    place = lax.axis_index("seq")
    core, row = place % 2, place // 2
    data = lax.axis_index("dp")
    high = data // count
    side = (data // (count // 2)) % 2
    total = n_seq * piece
    group = width // n_seq

    tok_recv = swap(pick(tokens, 1 - row), "seq", 2)
    tok_keep = pick(tokens, row)
    tok_keep_o = swap(tok_keep, "seq", 1)
    cot_keep = pick(cotangent, row)
    cot_recv = swap(pick(cotangent, 1 - row), "seq", 2)

    where = jnp.stack(
        [
            core, row, side, pick(lengths, row),
            2 * row + core, 2 * (1 - row) + core, 2 * row + 1 - core, 2 * (1 - row) + 1 - core,
        ]
    ).astype(jnp.int32)
    tables = tuple(jnp.asarray(table) for table in rotary_tables(total))
    out_blocks = w_out.reshape(n_seq, group, width)

    qkv, normed_t, w_qkv = project_call(
        0, where, tok_keep, tok_keep_o, gain_one, shift_one, (w_query, w_key, w_value), tables, ()
    )
    tok_recv, qkv, normed_t = together(tok_recv, qkv, normed_t)
    tok_recv_o = swap(tok_recv, "seq", 1)
    qkv, normed_t = project_call(
        1, where, tok_recv, tok_recv_o, gain_one, shift_one, (w_qkv,), tables, (qkv, normed_t)
    )
    ctx_m, ctx_o, ctx_t, lse = attend_call(where, qkv)
    cot_keep_o = swap(cot_keep, "seq", 1)
    ctx_m, ctx_o, ctx_t, cot_recv, cot_keep_o = together(ctx_m, ctx_o, ctx_t, cot_recv, cot_keep_o)
    cotangents = (cot_keep, cot_recv, cot_keep_o, swap(cot_recv, "seq", 1))
    ctx_got = swap(ctx_o, "seq", 1)
    residual, normed_two = residual_call(
        where, tok_keep, tok_recv, ctx_m, ctx_got, out_blocks, gain_two, shift_two
    )
    normed_two_o = swap(normed_two, "seq", 1)
    ctx_got_t = swap(ctx_t, "seq", 1)
    up_send0, up_send1, down_send0, down_keep0, active0, hidden0 = feed_call(
        False, where, normed_two, normed_two_o, cotangents, w_up, w_down
    )
    up_got0, up_got1 = swap(up_send0, "seq", 2), swap(up_send1, "seq", 2)
    down_got0 = swap(down_send0, "dp", count // 2)
    up_keep0, up_keep1, down_send1, down_keep1, active1, back_m, back_o = feed_call(
        True, where, normed_two, normed_two_o, cotangents, w_up, w_down, (hidden0,)
    )
    back_o, up_got0, down_got0 = together(back_o, up_got0, down_got0)
    back_got = swap(back_o, "seq", 1)
    down_got1 = swap(down_send1, "dp", count // 2)
    grad_low, sums_two = middle_call(where, residual, back_m, back_got, cot_keep, cot_recv, gain_two)
    grad_low_o = swap(grad_low, "seq", 1)

    block_rows = width // n_dp

    pairs = qkv.shape[1] // (3 * LANES)
    early, pieces = [], ()
    def up_part(index):
        shape = (2, 2, count // 2 * block_rows, width)
        parts = []
        for kept, got in ((up_keep0, up_got0), (up_keep1, up_got1)):
            kept = pick(kept.reshape(shape), index, 1).astype(F32)
            parts.append(kept + pick(got.reshape(shape), index, 1).astype(F32))
        return jnp.concatenate(parts)

    def down_part(index):
        shape = (2, 2 * group, -1)
        parts = []
        for kept, got in ((down_keep0, down_got0), (down_keep1, down_got1)):
            kept = pick(kept.reshape(shape), index).astype(F32)
            parts.append(kept + pick(got.reshape(shape), index).astype(F32))
        return jnp.where(row == 0, jnp.stack(parts[::-1]), jnp.stack(parts))

    def upper(up_got2, down_got2):
        up = up_part(side) + up_got2.astype(F32)
        down = (down_part(row) + down_got2.astype(F32)).reshape(4, group, -1)
        if count > 2:
            up = up.reshape(4, count // 2, block_rows, width)
            bit = count // 4
            while bit > 0:
                mine = (data // bit) % 2
                size, lanes = up.shape[1] // 2, down.shape[2] // 2
                sent = lax.dynamic_slice_in_dim(up, (1 - mine) * size, size, 1).astype(BF16)
                up = lax.dynamic_slice_in_dim(up, mine * size, size, 1) + swap(sent, "dp", bit)
                sent = lax.dynamic_slice_in_dim(down, (1 - mine) * lanes, lanes, 2).astype(BF16)
                down = lax.dynamic_slice_in_dim(down, mine * lanes, lanes, 2) + swap(sent, "dp", bit)
                bit //= 2
            up = up.reshape(4, block_rows, width)
        lanes = down.shape[2]
        folds = width // lanes
        size = group // folds
        down = jnp.concatenate([down[:, k * size : (k + 1) * size] for k in range(folds)], axis=2)
        return jnp.concatenate([up.astype(BF16), down.astype(BF16)], axis=1)

    def feed_sums(feed_got):
        up, down = feed_own[:block_rows].astype(F32), feed_own[block_rows:].astype(F32)
        for one_up, one_down in zip(*feed_got):
            up, down = up + one_up.astype(F32), down + one_down.astype(F32)
        return up, down.astype(BF16)

    def exchanged(values):
        perm = []
        for d in range(n_dp):
            for s in range(n_seq):
                second_bit = (d // count) % 2
                to_d = d + (s % 2 - second_bit) * count
                to_s = s - s % 2 + second_bit
                perm.append((d * n_seq + s, to_d * n_seq + to_s))
        return lax.ppermute(values, ("dp", "seq"), perm)

    for pair in range(pairs):
        if pair == pairs - 2:
            up_got1, down_got1, *early = together(up_got1, down_got1, *early)
            up_sent, down_sent = up_part(1 - side).astype(BF16), down_part(1 - row).astype(BF16)
            up_sent, down_sent, *early = together(up_sent, down_sent, *early)
            up_got2 = swap(up_sent, "dp", count // 2)
            down_got2 = swap(down_sent, "seq", 2)
        if pair == pairs - 1:
            up_got2, down_got2, *early = together(up_got2, down_got2, *early)
            both = upper(up_got2, down_got2)
            both, *early = together(both, *early)
            feed_own = pick(both, high)
            feed_got = [
                [swap(pick(one, high ^ k), "dp", count * k) for k in (1, 2, 3)]
                for one in (both[:, :block_rows], both[:, block_rows:])
            ]
        pieces = list(attend_back_call(
            pair, where, qkv, ctx_t, ctx_got_t, grad_low, grad_low_o, out_blocks, lse, tables,
            normed_t, early, w_qkv, pieces,
        ))
        if pair < pairs - 1:
            early.append(pieces.pop())
    pieces, feed_got[0] = together(pieces, feed_got[0])
    piece0, piece1, piece2, piece3, normed_m, normed_o = pieces
    normed_got = swap(normed_o, "seq", 1)
    out_m, out_o = feed_out_call(where, active0, active1, w_down)
    tok_buf, tok_send, sums_one = tokens_grad_call(
        where, tok_keep, tok_recv, normed_m, normed_got, grad_low, gain_one
    )


    sums = sums_one + sums_two
    sums = sums + swap(sums, "seq", 1)
    inner = count // 2
    shape = (2, 2, width // 16, -1)
    if count == 2:
        got0, got2 = swap(piece0, "dp", inner), swap(piece2, "seq", 2)
        got0, got2, tok_send, out_o, feed_got = together(got0, got2, tok_send, out_o, feed_got)
        lanes = piece0.shape[1]
        unit = width // 16
        more = sums.shape[0]

        def first(index):
            kept = pick(piece1.reshape(shape), index, 1).astype(F32)
            return kept + pick(got0.reshape(shape), index, 1).astype(F32)

        def second(index):
            kept = pick(piece3.reshape(shape), index, 1).astype(F32)
            kept = kept + pick(got2.reshape(shape), index, 1).astype(F32)
            wide = jnp.pad(sums, ((0, 0), (0, lanes - width)))
            return jnp.concatenate([kept.reshape(2 * unit, lanes), wide])

        sent_first, sent_second = first(1 - row).astype(BF16), second(1 - side).astype(BF16)
        sent_first, sent_second, tok_send, out_o, feed_got = together(
            sent_first, sent_second, tok_send, out_o, feed_got
        )
        got_first = swap(sent_first, "seq", 2)
        got_second = swap(sent_second, "dp", inner)
        tok_back = swap(tok_send, "seq", 2)
        out_send, out_buf = output_call(where, residual, out_m, swap(out_o, "seq", 1))
        grad_up, grad_down = feed_sums(feed_got)
        got_first, got_second, out_send, grad_down = together(got_first, got_second, out_send, grad_down)
        firsts = first(row) + got_first.astype(F32)
        seconds = second(side) + got_second.astype(F32)

        def chunk(k):
            target = high ^ k
            values = jnp.where(
                target % 2 == 0,
                pick(firsts, target // 2),
                pick(seconds[: 2 * unit].reshape(2, unit, lanes), target // 2),
            )
            return jnp.concatenate([values, seconds[2 * unit :]])

        *sent, out_send, grad_down = together(
            *(chunk(k).astype(BF16) for k in (1, 2, 3)), out_send, grad_down
        )
        got = [swap(one, "dp", count * k) for k, one in zip((1, 2, 3), sent)]
        out_back = swap(out_send, "seq", 2)
        grad_down = exchanged(grad_down)
        tok_back, grad_down, *got = together(tok_back, grad_down, *got)
        summed = chunk(0)
        for one in got:
            summed = summed + one.astype(F32)
        sums = summed[unit:, :width]
        summed = summed[:unit].reshape(unit, pairs, 4, LANES).transpose(0, 2, 1, 3)
        summed = summed.reshape(unit, 4, 2, group)
        sent = jnp.concatenate([pick(summed, 1 - row, 2).reshape(unit, width), sums])
        other = swap(sent.astype(BF16), "seq", 2).astype(F32)
        sums = sums + other[unit:]
        mine, other = pick(summed, row, 2).reshape(unit, width), other[:unit]
        ordered = jnp.where(row == 0, jnp.concatenate([mine, other]), jnp.concatenate([other, mine]))
    else:
        sides = jnp.stack([piece0, piece1]).reshape((2,) + shape)
        sides = jnp.stack([pick(sides, jnp.where(side == k, 1, 0)) for k in (0, 1)], 1)
        halves = jnp.stack([piece2, piece3]).reshape((2,) + shape)
        halves = jnp.stack([pick(halves, jnp.where(row == k, 1, 0)) for k in (0, 1)], 2)
        summed = jnp.stack([sides, halves], 1).reshape(width, pairs, 4, LANES).transpose(0, 2, 1, 3)
        summed = summed.reshape(width, 4, 2, group)
        other = swap(pick(summed, 1 - row, 2), "seq", 2).astype(F32)
        summed = (pick(summed, row, 2).astype(F32) + other).astype(BF16).reshape(width, -1)
        ordered = lax.psum_scatter(summed, "dp", scatter_dimension=0, tiled=True).astype(F32)
        tok_back = swap(tok_send, "seq", 2)
        out_send, out_buf = output_call(where, residual, out_m, swap(out_o, "seq", 1))
        out_back = swap(out_send, "seq", 2)
        grad_up, grad_down = feed_sums(feed_got)
        grad_down = exchanged(grad_down)
        sums = sums + swap(sums, "seq", 2)
        bit = 1
        while bit < n_dp:
            sums = sums + swap(sums, "dp", bit)
            bit *= 2
    ordered = [ordered[:, k * group : (k + 1) * group] for k in range(4)]

    lanes = w_down.shape[0] // n_dp
    grad_down = grad_down.astype(F32)
    grad_down = jnp.concatenate(
        [grad_down[:, k * lanes : (k + 1) * lanes] for k in range(width // lanes)], axis=0
    ).T

    output = lax.dynamic_update_slice(out_buf, out_back[None], (1 - row, 0, 0))
    grad_tokens = lax.dynamic_update_slice(tok_buf, tok_back[None], (1 - row, 0, 0))
    return (
        output,
        grad_tokens,
        sums[0],
        sums[1],
        ordered[0],
        ordered[1],
        ordered[2],
        ordered[3],
        sums[2],
        sums[3],
        grad_up,
        grad_down,
    )


def solution(mesh):
    tokens = P("dp", "seq", None)
    weights = P("dp", "seq")
    return jax.shard_map(
        local,
        mesh=mesh,
        in_specs=(tokens,) + (P(),) * 10 + (tokens, P("dp")),
        out_specs=(tokens, tokens, P(), P(), weights, weights, weights, weights, P(), P(), weights, weights),
        check_vma=False,
    )
```

```python
import functools

import jax
import jax.numpy as jnp
import numpy as np
from jax import lax
from jax.experimental import pallas as pl
from jax.experimental.pallas import tpu as pltpu
from jax.sharding import PartitionSpec as P

HD = 64
EPSILON = 1e-05
MASKED = -1000000000.0
LANES = 128
BF16 = jnp.bfloat16
F32 = jnp.float32
CORE, ROW, SIDE, LENGTH, SPOT, HIGH = 0, 1, 2, 3, 4, 8


def swap(values, axis, bit):
    count = lax.axis_size(axis)
    return lax.ppermute(values, axis, [(i, i ^ bit) for i in range(count)])


def together(*values):
    return lax.optimization_barrier(values)


def pick(values, index, axis=0):
    return lax.dynamic_index_in_dim(values, index, axis, keepdims=False)


def dot(left, right):
    return jnp.dot(left, right, preferred_element_type=F32)


def dot_back(left, right):
    return lax.dot_general(left, right, (((1,), (1,)), ((), ())), preferred_element_type=F32)


def normalize(values):
    average = jnp.mean(values, axis=-1, keepdims=True)
    centred = values - average
    variance = jnp.mean(centred * centred, axis=-1, keepdims=True)
    inverse = lax.rsqrt(variance + EPSILON)
    return centred * inverse, inverse


def norm_back(grad, gain, normal, inverse):
    scaled = grad * gain
    first = jnp.mean(scaled, axis=-1, keepdims=True)
    second = jnp.mean(scaled * normal, axis=-1, keepdims=True)
    return (scaled - first - normal * second) * inverse


def row_vector(ref):
    return ref[...].reshape(1, ref.shape[0])


def swap_halves(values):
    lane = lax.broadcasted_iota(jnp.int32, values.shape, 1)
    up = pltpu.roll(values, LANES - HD // 2, 1)
    down = pltpu.roll(values, HD // 2, 1)
    return jnp.where(lane % HD < HD // 2, up, down)


def rotary_tables(length):
    lane = np.arange(LANES)
    frequency = 10000.0 ** (-2.0 * (lane % (HD // 2)) / HD)
    angles = np.arange(length)[:, None] * frequency[None, :]
    sign = np.where(lane % HD < HD // 2, -1.0, 1.0)
    return np.cos(angles).astype(np.float32), (sign * np.sin(angles)).astype(np.float32)


def kept_rows(where_ref, block, rows, lanes):
    spot = lax.broadcasted_iota(jnp.int32, (rows, lanes), 0) + where_ref[SPOT + block] * rows
    return spot < where_ref[LENGTH]


SMALL = pl.CostEstimate(flops=1, bytes_accessed=1, transcendentals=0)


def whole(shape):
    return pl.BlockSpec(shape, lambda *_: (0,) * len(shape))


def call(kernel, grid, in_specs, out_specs, out_shape, scratch, estimate, aliases=None, mib=16):
    return pl.pallas_call(
        kernel,
        grid_spec=pltpu.PrefetchScalarGridSpec(
            num_scalar_prefetch=1,
            grid=grid,
            in_specs=in_specs,
            out_specs=out_specs,
            scratch_shapes=scratch,
        ),
        out_shape=[jax.ShapeDtypeStruct(shape, kind) for shape, kind in out_shape],
        input_output_aliases=aliases or {},
        compiler_params=pltpu.CompilerParams(vmem_limit_bytes=mib * 1024 * 1024),
        cost_estimate=estimate,
    )


def pair_columns(ref, core, pair):
    group = ref.shape[1] // 4
    pieces = []
    start, end = pair * LANES, (pair + 1) * LANES
    if start < group:
        pieces.append(ref[:, core * group + start : core * group + min(end, group)])
    if end > group:
        begin = max(start, group)
        pieces.append(ref[:, (1 + core) * group + begin : (1 + core) * group + end])
    return pieces[0] if len(pieces) == 1 else jnp.concatenate(pieces, axis=1)


def project_kernel(where_ref, mine_ref, other_ref, gain_ref, shift_ref, *rest, first, pairs):
    step = pl.program_id(0)
    if first:
        wq_ref, wk_ref, wv_ref, cos_ref, sin_ref, qkv_ref, normed_t_ref, weight_ref = rest

        @pl.when(step == 0)
        def _():
            for core in range(2):

                @pl.when(where_ref[CORE] == core)
                def _():
                    for part, ref in enumerate((wq_ref, wk_ref, wv_ref)):
                        for pair in range(pairs):
                            start = (3 * pair + part) * LANES
                            weight_ref[:, start : start + LANES] = pair_columns(ref, core, pair)
    else:
        weight_ref, cos_ref, sin_ref, _, _, qkv_ref, normed_t_ref = rest
    values = jnp.where(step == 0, mine_ref[...], other_ref[...]).astype(F32)
    normal, _ = normalize(values)
    normed = (normal * row_vector(gain_ref) + row_vector(shift_ref)).astype(BF16)
    normed_t_ref[...] = normed.T
    cosine, sine = cos_ref[...], sin_ref[...]
    width = 3 * LANES
    for pair in range(pairs):
        out = dot(normed, weight_ref[:, pair * width : (pair + 1) * width])
        for part in range(3):
            piece = out[:, part * LANES : (part + 1) * LANES]
            if part < 2:
                piece = piece * cosine + swap_halves(piece) * sine
                if part == 0:
                    piece = piece * (HD ** (-0.5))
            start = pair * width + part * LANES
            qkv_ref[:, start : start + LANES] = piece.astype(BF16)


def project_call(turn, where, mine, other, gain, shift, weights, tables, previous):
    rows, width = mine.shape
    out_width = 3 * width // 2
    total = 4 * rows
    block = lambda i, w: (2 * i + turn, 0)
    table = pl.BlockSpec((rows, LANES), lambda i, w: (w[SPOT + 2 * i + turn], 0))
    in_specs = [whole((rows, width))] * 2 + [whole((width,))] * 2
    in_specs += [whole(weight.shape) for weight in weights] + [table, table]
    out_specs = [
        pl.BlockSpec((rows, out_width), block),
        pl.BlockSpec((width, rows), lambda i, w: (0, 2 * i + turn)),
    ]
    out_shape = [((total, out_width), BF16), ((width, total), BF16)]
    aliases = {}
    if previous:
        aliases = {1 + len(in_specs): 0, 2 + len(in_specs): 1}
        in_specs += [pl.BlockSpec(memory_space=pl.ANY)] * 2
    else:
        out_specs.append(whole((width, out_width)))
        out_shape.append(((width, out_width), BF16))
    return call(
        functools.partial(project_kernel, first=not previous, pairs=out_width // (3 * LANES)),
        (2,), in_specs, out_specs, out_shape, [],
        SMALL, aliases, 12,
    )(where, mine, other, gain, shift, *weights, *tables, *previous)


def mask_lane(lane, head, keys, bias):
    return jnp.where(lane == (HD if head == 0 else 0), bias, keys)


def only_head(lane, head, values):
    return jnp.where(lane // HD == head, values, jnp.zeros_like(values))


def with_one(lane, head, values):
    one = lane == (HD if head == 0 else 0)
    return jnp.where(one, jnp.ones_like(values), only_head(lane, head, values))


def fill_bias(where_ref, bias_ref):
    rows = bias_ref.shape[0] // 4
    for block in range(4):
        kept = kept_rows(where_ref, block, rows, LANES)
        bias_ref[block * rows : (block + 1) * rows, :] = jnp.where(kept, 0.0, MASKED).astype(BF16)


def attend_kernel(
    where_ref, query_ref, key_ref, value_ref, mine_ref, other_ref, ctx_t_ref, lse_ref, bias_ref, ctx_ref,
    *, tile,
):
    total = query_ref.shape[0]
    lane = lax.broadcasted_iota(jnp.int32, (1, LANES), 1)

    @pl.when(pl.program_id(0) == 0)
    def _():
        fill_bias(where_ref, bias_ref)

    keys = key_ref[...]
    values_t = value_ref[...].T
    for head in range(2):
        key_aug = mask_lane(lane, head, keys, bias_ref[...])
        for start in range(0, total, tile):
            queries = with_one(lane, head, query_ref[start : start + tile, :])
            scores = dot_back(key_aug, queries)
            highest = jnp.max(scores, axis=0, keepdims=True)
            weights = jnp.exp(scores - highest)
            sums = jnp.sum(weights, axis=0, keepdims=True)
            context = dot(values_t[head * HD : (head + 1) * HD, :], weights.astype(BF16))
            ctx_ref[head * HD : (head + 1) * HD, start : start + tile] = context / sums
            lse_ref[0, head : head + 1, start : start + tile] = highest + jnp.log(sums)
    ctx_t_ref[...] = ctx_ref[...].astype(BF16)
    contexts = ctx_ref[...].T.astype(BF16)
    mine_ref[...] = contexts[: total // 2]
    other_ref[...] = contexts[total // 2 :]


def attend_call(where, qkv):
    total, width = qkv.shape
    pairs = width // (3 * LANES)
    width //= 3
    half = total // 2
    column = lambda part: pl.BlockSpec((total, LANES), lambda p, w: (0, 3 * p + part))
    out_column = pl.BlockSpec((half, LANES), lambda p, w: (0, p))
    return call(
        functools.partial(attend_kernel, tile=total),
        (pairs,),
        [column(0), column(1), column(2)],
        [
            out_column, out_column,
            pl.BlockSpec((LANES, total), lambda p, w: (p, 0)),
            pl.BlockSpec((1, 8, total), lambda p, w: (p, 0, 0)),
        ],
        [((half, width), BF16), ((half, width), BF16), ((width, total), BF16), ((pairs, 8, total), F32)],
        [pltpu.VMEM((total, LANES), BF16), pltpu.VMEM((LANES, total), F32)],
        SMALL, mib=16,
    )(where, qkv, qkv, qkv)


def stack_rows(refs):
    return jnp.concatenate([ref[0] for ref in refs], axis=0)


def residual_kernel(
    where_ref, keep_ref, recv_ref, mine_ref, got_ref, w0_ref, w1_ref, w2_ref, w3_ref,
    gain_ref, shift_ref, res_ref, normed_ref,
):
    step = pl.program_id(0)
    values = jnp.where(step == 0, keep_ref[...], recv_ref[...]).astype(F32)
    attended = dot(mine_ref[...], stack_rows((w0_ref, w1_ref)))
    attended += dot(got_ref[...], stack_rows((w2_ref, w3_ref)))
    residual = values + attended
    res_ref[...] = residual
    normal, _ = normalize(residual)
    normed_ref[...] = (normal * row_vector(gain_ref) + row_vector(shift_ref)).astype(BF16)


def out_weight_specs(group, width):
    places = (
        lambda w: w[CORE],
        lambda w: 2 + w[CORE],
        lambda w: 1 - w[CORE],
        lambda w: 3 - w[CORE],
    )
    return [pl.BlockSpec((1, group, width), lambda i, w, at=at: (at(w), 0, 0)) for at in places]


def residual_call(where, keep, recv, ctx_mine, ctx_got, w_out, gain, shift):
    rows, width = keep.shape
    heads = ctx_mine.shape[1]
    row = lambda lanes: pl.BlockSpec((rows, lanes), lambda i, w: (i, 0))
    return call(
        residual_kernel,
        (2,),
        [whole((rows, width))] * 2 + [row(heads)] * 2
        + out_weight_specs(heads // 2, width) + [whole((width,))] * 2,
        [row(width)] * 2,
        [((2 * rows, width), F32), ((2 * rows, width), BF16)],
        [],
        SMALL, mib=10,
    )(where, keep, recv, ctx_mine, ctx_got, w_out, w_out, w_out, w_out, gain, shift)


def gelu_both(values):
    root = 0.7978845608028654
    bend = (root * 0.044715) * (values * values)
    half = 0.5 * jnp.tanh(values * (root + bend)) + 0.5
    steep = values * (2.0 * root + 6.0 * bend)
    return values * half, half * ((1.0 - half) * steep + 1.0)


def fill_cotangent(where_ref, refs, grad_ref):
    rows, width = refs[0].shape
    for place, ref in enumerate(refs):
        kept = kept_rows(where_ref, place, rows, width)
        grad_ref[place * rows : (place + 1) * rows, :] = jnp.where(kept, ref[...], jnp.zeros_like(ref))


def feed_kernel(
    where_ref,
    normed_m_ref, normed_o_ref, cot0_ref, cot1_ref, cot2_ref, cot3_ref, up_ref, down_ref,
    *rest, tile, last,
):
    if last:
        before_ref, up_before_ref, *rest = rest
        up0_ref, up1_ref, send_ref, keep_ref, active_ref, back_m_ref, back_o_ref = rest[:7]
        normed_ref, grad_ref, normed_t_ref, grad_t_ref, hidden_ref = rest[7:]
    else:
        up0_ref, up1_ref, send_ref, keep_ref, active_ref, hidden_ref = rest[:6]
        normed_ref, grad_ref, normed_t_ref, grad_t_ref = rest[6:]
    half, width = normed_m_ref.shape
    block = up_ref.shape[1]
    normed_ref[:half, :] = normed_m_ref[...]
    normed_ref[half:, :] = normed_o_ref[...]
    fill_cotangent(where_ref, (cot0_ref, cot1_ref, cot2_ref, cot3_ref), grad_ref)
    normed_t_ref[...] = normed_ref[...].T
    grad_t_ref[...] = grad_ref[...].T
    for start in range(0, block, tile):
        span = slice(start, start + tile)
        hidden = dot(normed_ref[...], up_ref[:, span])
        active, slope = gelu_both(hidden)
        active_ref[:, span] = active.astype(BF16)
        grad_active = dot_back(grad_ref[...], down_ref[span, :])
        hidden_ref[:, span] = (grad_active * slope).astype(BF16)
    up_grad = dot(normed_t_ref[...], hidden_ref[...]).astype(BF16)
    up0_ref[...] = up_grad[: width // 2]
    up1_ref[...] = up_grad[width // 2 :]
    down_grad = dot(grad_t_ref[...], active_ref[...]).astype(BF16)
    part = block // 2
    for side in range(2):
        piece = down_grad[:, side * part : (side + 1) * part]

        @pl.when(where_ref[SIDE] == side)
        def _():
            keep_ref[...] = piece

        @pl.when(where_ref[SIDE] != side)
        def _():
            send_ref[...] = piece

    if last:
        back = dot_back(before_ref[...], up_before_ref[...]) + dot_back(hidden_ref[...], up_ref[...])
        back_m_ref[...] = back[:half]
        back_o_ref[...] = back[half:].astype(BF16)


def feed_high(last, w):
    return w[ROW] if last else 1 - w[ROW]


def feed_call(last, where, normed_m, normed_o, cotangents, w_up, w_down, before=()):
    half, width = normed_m.shape
    total = 2 * half
    block = w_up.shape[1] // 4
    part = block // 2
    token = whole((half, width))
    up_block = lambda last: pl.BlockSpec(
        (width, block), lambda i, w: (0, 2 * feed_high(last, w) + w[CORE])
    )
    down_block = pl.BlockSpec((block, width), lambda i, w: (2 * feed_high(last, w) + w[CORE], 0))
    in_specs = [token, token] + [whole((half // 2, width))] * 4 + [up_block(last), down_block]
    args = [normed_m, normed_o, *cotangents, w_up, w_down]
    out_shape = [
        ((width // 2, block), BF16),
        ((width // 2, block), BF16),
        ((width, part), BF16),
        ((width, part), BF16),
        ((total, block), BF16),
    ]
    scratch = [
        pltpu.VMEM((total, width), BF16),
        pltpu.VMEM((total, width), BF16),
        pltpu.VMEM((width, total), BF16),
        pltpu.VMEM((width, total), BF16),
    ]
    if last:
        in_specs += [whole((total, block)), up_block(False)]
        args += [*before, w_up]
        out_shape += [((half, width), F32), ((half, width), BF16)]
        scratch.append(pltpu.VMEM((total, block), BF16))
    else:
        out_shape.append(((total, block), BF16))
    return call(
        functools.partial(feed_kernel, tile=block, last=last),
        (1,), in_specs, [whole(shape) for shape, _ in out_shape], out_shape, scratch, SMALL, mib=20,
    )(where, *args)


def feed_out_kernel(where_ref, first_ref, last_ref, down0_ref, down1_ref, mine_ref, other_ref):
    out = dot(first_ref[...], down0_ref[...]) + dot(last_ref[...], down1_ref[...])

    @pl.when(pl.program_id(0) == 0)
    def _():
        other_ref[...] = out.astype(BF16)

    @pl.when(pl.program_id(0) == 1)
    def _():
        mine_ref[...] = out


def feed_out_call(where, first, last, w_down):
    total, block = first.shape
    width = w_down.shape[1]
    half = total // 2
    row = pl.BlockSpec((half, block), lambda i, w: (1 - i, 0))
    down = [
        pl.BlockSpec((block, width), lambda i, w, last=last: (2 * feed_high(last, w) + w[CORE], 0))
        for last in (False, True)
    ]
    return call(
        feed_out_kernel,
        (2,),
        [row, row, *down],
        [whole((half, width))] * 2,
        [((half, width), F32), ((half, width), BF16)],
        [], SMALL, mib=12,
    )(where, first, last, w_down, w_down)


def output_kernel(where_ref, res_ref, out_ref, got_ref, send_ref, keep_ref):
    step = pl.program_id(0)
    output = res_ref[...] + out_ref[...] + got_ref[...].astype(F32)
    kept = kept_rows(where_ref, 1 - step, *output.shape)
    output = jnp.where(kept, output, jnp.zeros_like(output)).astype(BF16)

    @pl.when(step == 0)
    def _():
        send_ref[...] = output

    @pl.when(step == 1)
    def _():
        keep_ref[0] = output


def output_call(where, residual, out, got):
    half, width = residual.shape
    rows = half // 2
    row = pl.BlockSpec((rows, width), lambda i, w: (1 - i, 0))
    return call(
        output_kernel,
        (2,),
        [row] * 3,
        [whole((rows, width)), pl.BlockSpec((1, rows, width), lambda i, w: (w[ROW], 0, 0))],
        [((rows, width), BF16), ((2, rows, width), BF16)],
        [], SMALL, mib=8,
    )(where, residual, out, got)


def add_sums(sums_ref, step, row, gains, shifts):
    @pl.when(step == 0)
    def _():
        sums_ref[...] = jnp.zeros_like(sums_ref)

    sums_ref[row : row + 1, :] += gains
    sums_ref[row + 1 : row + 2, :] += shifts


def middle_kernel(
    where_ref,
    res_ref, back_ref, back_got_ref, cot0_ref, cot1_ref, gain_ref, grad_low_ref, sums_ref,
):
    step = pl.program_id(0)
    residual = res_ref[...]
    kept = kept_rows(where_ref, step, *residual.shape)
    normal, inverse = normalize(residual)
    back = back_ref[...] + back_got_ref[...].astype(F32)
    gains = jnp.sum(back * normal, axis=0, keepdims=True)
    shifts = jnp.sum(back, axis=0, keepdims=True)

    add_sums(sums_ref, step, 2, gains, shifts)
    cotangent = jnp.where(step == 0, cot0_ref[...], cot1_ref[...]).astype(F32)
    cotangent = jnp.where(kept, cotangent, jnp.zeros_like(cotangent))
    grad = cotangent + norm_back(back, row_vector(gain_ref), normal, inverse)
    grad_low_ref[...] = grad.astype(BF16)


def middle_call(where, residual, back_m, back_got, cot_keep, cot_recv, gain):
    half, width = residual.shape
    rows = half // 2
    row = pl.BlockSpec((rows, width), lambda i, w: (i, 0))
    return call(
        middle_kernel,
        (2,),
        [row] * 3 + [whole((rows, width))] * 2 + [whole((width,))],
        [row, whole((8, width))],
        [((half, width), BF16), ((8, width), F32)],
        [], SMALL, mib=8,
    )(where, residual, back_m, back_got, cot_keep, cot_recv, gain)


def piece_order(where_ref):
    side, row = where_ref[SIDE], where_ref[ROW]
    order = []
    for kept in (0, 1):
        mine = side if kept else 1 - side
        order += [8 * high + 2 * mine + half for high in (0, 1) for half in (0, 1)]
    for kept in (0, 1):
        mine = row if kept else 1 - row
        order += [8 * high + 4 + 2 * one + mine for high in (0, 1) for one in (0, 1)]
    return order


def attend_back_kernel(
    where_ref,
    query_ref, key_ref, value_ref, ctx_ref, grad_m_ref, grad_o_ref, w0_ref, w1_ref, lse_ref,
    ctx_mine_hbm, ctx_got_hbm, cos_hbm, sin_hbm, normed_t_hbm, *rest,
    score_scale, first, last,
):
    if last:
        early_ref, weight_ref, *rest = rest
        out_refs, (back_m_ref, back_o_ref) = rest[:4], rest[4:6]
        *rest, grads_ref = rest[6:]
    else:
        out_refs, grads_ref = rest[:4], rest[4]
        rest = rest[5:]
    bias_ref, grad_ref, columns_ref, dqt_ref, dk_acc, dv_acc, qkv_ref, own_ref = rest[:8]
    ctx_mine_ref, ctx_got_ref, cos_ref, sin_ref, normed_t_ref, semaphores = rest[8:]
    step = pl.program_id(0)
    total = query_ref.shape[0]
    half = total // 2
    model = grad_m_ref.shape[1]
    lane = lax.broadcasted_iota(jnp.int32, (1, LANES), 1)
    unit = model // 16
    group = model // 4
    rows = total // 4
    late = [(ctx_mine_hbm, ctx_mine_ref), (ctx_got_hbm, ctx_got_ref), (normed_t_hbm, normed_t_ref)]
    for source, target in ((cos_hbm, cos_ref), (sin_hbm, sin_ref)):
        for block in range(4):
            begin = pl.multiple_of(where_ref[SPOT + block] * rows, rows)
            late.append((source.at[pl.ds(begin, rows)], target.at[pl.ds(block * rows, rows)]))

    def copies():
        return [
            pltpu.make_async_copy(source, target, semaphores.at[k])
            for k, (source, target) in enumerate(late)
        ]

    @pl.when(step == 0)
    def _():
        for copy in copies():
            copy.start()
        fill_bias(where_ref, bias_ref)
        grad_ref[:half, :] = grad_m_ref[...]
        grad_ref[half:, :] = grad_o_ref[...]

    for place, pair in enumerate(first):
        for core in range(2):

            @pl.when((step == place) & (where_ref[CORE] == core))
            def _():
                columns_ref[...] = pair_columns(grad_ref, core, pair)

    wout = jnp.concatenate([w0_ref[...], w1_ref[...]], axis=0)
    gctx = dot_back(grad_ref[...], wout).astype(BF16)
    products = gctx.astype(F32).T * ctx_ref[...].astype(F32)
    keys = key_ref[...]
    keys_t = keys.T
    values = value_ref[...]
    queries = query_ref[...]
    for head in range(2):
        key_aug = mask_lane(lane, head, keys, bias_ref[...])
        delta = jnp.sum(products[head * HD : (head + 1) * HD, :], axis=0, keepdims=True)
        scores = dot_back(key_aug, with_one(lane, head, queries))
        weights = jnp.exp(scores - lse_ref[0, head : head + 1, :])
        grads = only_head(lane, head, gctx)
        grad_weights = dot_back(values, grads)
        grad_scores = (weights * (grad_weights - delta)).astype(BF16)
        dv = dot(weights.astype(BF16), grads)
        dk = dot(grad_scores, only_head(lane, head, queries))
        dqt_ref[head * HD : (head + 1) * HD, :] = dot(
            keys_t[head * HD : (head + 1) * HD, :], grad_scores
        )
        if head == 0:
            dv_acc[...] = dv
            dk_acc[...] = dk
        else:
            dv_acc[...] += dv
            dk_acc[...] += dk

    @pl.when(step == 0)
    def _():
        for copy in copies():
            copy.wait()

    cosine, sine = cos_ref[...], sin_ref[...]
    dq = dqt_ref[...].T * score_scale
    dk = dk_acc[...]
    dq = (dq * cosine - swap_halves(dq) * sine).astype(BF16)
    dk = (dk * cosine - swap_halves(dk) * sine).astype(BF16)
    grads = jnp.concatenate([dq, dk, dv_acc[...].astype(BF16)], axis=1)
    qkv_ref[...] = dot(normed_t_ref[...], grads).astype(BF16)
    columns = columns_ref[...]
    turned = jnp.concatenate([columns[half:], columns[:half]], axis=0)
    own_ref[0] = dot(ctx_mine_ref[...], columns).astype(BF16)
    own_ref[1] = dot(ctx_got_ref[...], turned).astype(BF16)
    for place, source in enumerate(piece_order(where_ref)):
        ref = out_refs[place // 4]
        span = slice(place % 4 * unit, (place % 4 + 1) * unit)
        ref[span, : 3 * LANES] = qkv_ref[pl.ds(pl.multiple_of(source * unit, unit), unit), :]
        block = source // 4
        other = jnp.where(block % 2 == where_ref[CORE], 0, 1)
        inside = pl.multiple_of((block // 2) * group + (source % 4) * unit, unit)
        ref[span, 3 * LANES :] = own_ref[other, pl.ds(inside, unit), :]
    if not last:
        grads_ref[...] = grads
        return
    width = 3 * LANES
    for place in range(len(first) - 1):

        @pl.when(step == place)
        def _():
            grads_ref[:, place * width : (place + 1) * width] = grads

    @pl.when(step == len(first) - 1)
    def _():
        split = early_ref.shape[1]
        back = dot_back(early_ref[...], weight_ref[:, :split])
        if len(first) > 1:
            back += dot_back(grads_ref[...], weight_ref[:, split:-width])
        back += dot_back(grads, weight_ref[:, -width:])
        back_m_ref[...] = back[:half]
        back_o_ref[...] = back[half:].astype(BF16)


def attend_back_call(
    pairs, where, qkv, ctx_t, ctx_got_t, grad_m, grad_o, w_out, lse, tables, normed_t, weight, early=None
):
    total, width = qkv.shape
    width //= 3
    half, model = grad_m.shape
    quarter = model // 4
    last = early is not None
    begin = pairs[0]
    column = lambda part: pl.BlockSpec((total, LANES), lambda i, w: (0, 3 * (begin + i) + part))

    def head_rows(which):
        per = width // HD // 2

        def at(i, w):
            head = 2 * (begin + i) + which
            return (head // per * 2 * per + w[CORE] * per + head % per, 0)

        return pl.BlockSpec((HD, model), at)

    in_specs = [
        column(0), column(1), column(2),
        pl.BlockSpec((LANES, total), lambda i, w: (begin + i, 0)),
        whole((half, model)), whole((half, model)),
        head_rows(0), head_rows(1),
        pl.BlockSpec((1, 8, total), lambda i, w: (begin + i, 0, 0)),
    ]
    in_specs += [pl.BlockSpec(memory_space=pl.ANY)] * 5
    args = [
        qkv, qkv, qkv, ctx_t, grad_m, grad_o, w_out, w_out, lse, ctx_t, ctx_got_t, *tables, normed_t,
    ]
    out_specs = [pl.BlockSpec((quarter, 4 * LANES), lambda i, w: (0, i))] * 4
    out_shape = [((quarter, 4 * LANES * len(pairs)), BF16)] * 4
    if last:
        in_specs += [whole(early.shape), whole(weight.shape)]
        args += [early, weight]
        out_specs += [whole((half, model))] * 2
        out_shape += [((half, model), F32), ((half, model), BF16)]
    else:
        out_specs.append(pl.BlockSpec((total, 3 * LANES), lambda i, w: (0, i)))
        out_shape.append(((total, 3 * LANES * len(pairs)), BF16))
    return call(
        functools.partial(attend_back_kernel, score_scale=HD ** (-0.5), first=pairs, last=last),
        (len(pairs),), in_specs, out_specs, out_shape,
        [
            pltpu.VMEM((total, LANES), BF16),
            pltpu.VMEM((total, model), BF16),
            pltpu.VMEM((total, LANES), BF16),
            pltpu.VMEM((LANES, total), F32),
            pltpu.VMEM((total, LANES), F32),
            pltpu.VMEM((total, LANES), F32),
            pltpu.VMEM((model, 3 * LANES), BF16),
            pltpu.VMEM((2, width, LANES), BF16),
            pltpu.VMEM((width, total), BF16),
            pltpu.VMEM((width, total), BF16),
            pltpu.VMEM((total, LANES), F32),
            pltpu.VMEM((total, LANES), F32),
            pltpu.VMEM((model, total), BF16),
            pltpu.SemaphoreType.DMA((11,)),
        ]
        + ([pltpu.VMEM((total, max(len(pairs) - 1, 1) * 3 * LANES), BF16)] if last else []),
        SMALL, mib=26,
    )(where, *args)


def stage_one_kernel(
    where_ref,
    up_keep0, up_keep1, up_got0, up_got1, down_keep0, down_keep1, down_got0, down_got1,
    up_sent, up_kept, down_sent, down_kept,
):
    side, row = where_ref[SIDE], where_ref[ROW]
    unit = up_keep0.shape[0] // 4
    for half, (keep, got) in enumerate(((up_keep0, up_got0), (up_keep1, up_got1))):
        for one in range(2):
            to = slice((2 * half + one) * unit, (2 * half + one + 1) * unit)
            for out, mine in ((up_sent, 1 - side), (up_kept, side)):
                span = pl.ds(pl.multiple_of((2 * one + mine) * unit, unit), unit)
                out[to, :] = (keep[span, :].astype(F32) + got[span, :].astype(F32)).astype(BF16)
    size = down_keep0.shape[0] // 2
    for block, keep, got in ((1 - row, down_keep0, down_got0), (row, down_keep1, down_got1)):
        for out, mine in ((down_sent, 1 - row), (down_kept, row)):
            span = pl.ds(pl.multiple_of(mine * size, size), size)
            out[block] = (keep[span, :].astype(F32) + got[span, :].astype(F32)).astype(BF16)


def stage_one_call(where, *parts):
    rows, width = parts[0].shape
    size, lanes = parts[4].shape[0] // 2, parts[4].shape[1]
    out_shape = [((rows, width), BF16)] * 2 + [((2, size, lanes), BF16)] * 2
    return call(
        stage_one_kernel,
        (1,),
        [whole(part.shape) for part in parts],
        [whole(shape) for shape, _ in out_shape],
        out_shape, [], SMALL, mib=8,
    )(where, *parts)


def added(one, two, span):
    return one[span, :].astype(F32) + two[span, :].astype(F32)


def stage_two_kernel(where_ref, up_kept, up_got, down_kept, down_got, sent, kept):
    unit = kept.shape[1] // 2
    size, lanes = down_kept.shape[1] // 2, down_kept.shape[2]
    low = where_ref[HIGH] % 2
    for high in range(2):
        for out, which in ((sent, 1 - low), (kept, low)):
            span = pl.ds(pl.multiple_of((2 * high + which) * unit, unit), unit)
            out[high, :unit, :] = added(up_kept, up_got, span).astype(BF16)
            for fold in range(size // unit):
                span = pl.ds(pl.multiple_of(which * size + fold * unit, unit), unit)
                values = added(down_kept.at[high], down_got.at[high], span)
                out[high, unit:, fold * lanes : (fold + 1) * lanes] = values.astype(BF16)


def halve_kernel(where_ref, before, got, sent, kept):
    high = where_ref[HIGH] // 2
    for out, which in ((sent, 1 - high), (kept, high)):
        out[...] = (before[which].astype(F32) + got[which].astype(F32)).astype(out.dtype)


def halve_call(where, before, got):
    shape = before.shape[1:]
    return stage_call(halve_kernel, where, (before, got), [(shape, BF16), (shape, F32)])


def stage_call(kernel, where, inputs, out_shape, mib=8):
    return call(
        kernel, (1,), [whole(one.shape) for one in inputs], [whole(shape) for shape, _ in out_shape],
        out_shape, [], SMALL, mib=mib,
    )(where, *inputs)


def stage_two_call(where, up_kept, up_got, down_kept, down_got):
    rows, width = up_kept.shape
    part = (2, rows // 2, width)
    return stage_call(
        stage_two_kernel, where, (up_kept, up_got, down_kept, down_got), [(part, BF16)] * 2
    )


def feed_sum_kernel(where_ref, own, got, up, down):
    unit, lanes = up.shape[0], down.shape[1]
    summed = own[...] + got[...].astype(F32)
    up[...] = summed[:unit]
    for fold in range(up.shape[1] // lanes):
        values = summed[unit:, fold * lanes : (fold + 1) * lanes]
        down[fold * unit : (fold + 1) * unit, :] = values.astype(BF16)


def feed_sum_call(where, own, got, lanes):
    rows, width = own.shape
    unit = rows // 2
    return stage_call(
        feed_sum_kernel, where, (own, got), [((unit, width), F32), ((unit * width // lanes, lanes), BF16)]
    )


def stage_three_kernel(where_ref, *refs):
    firsts, seconds, (sums, sums_got) = refs[:4], refs[4:8], refs[8:10]
    first_sent, first_kept, second_sent, second_kept = refs[10:]
    side, row = where_ref[SIDE], where_ref[ROW]
    unit = first_sent.shape[0] // 2
    split = firsts[0].shape[1]
    for parts, mine, sent, kept in (
        (firsts, row, first_sent, first_kept),
        (seconds, side, second_sent, second_kept),
    ):
        for high in range(2):
            to = slice(high * unit, (high + 1) * unit)
            for out, which in ((sent, 1 - mine), (kept, mine)):
                span = pl.ds(pl.multiple_of((2 * high + which) * unit, unit), unit)
                out[to, :split] = added(parts[0], parts[1], span).astype(out.dtype)
                out[to, split:] = added(parts[2], parts[3], span).astype(out.dtype)
    summed = sums[...] + sums_got[...]
    width = summed.shape[1]
    for out in (second_sent, second_kept):
        out[2 * unit :, :] = jnp.zeros_like(out[2 * unit :, :])
        out[2 * unit :, :width] = summed.astype(out.dtype)


def stage_three_call(where, firsts, seconds, sums, sums_got):
    rows = firsts[0].shape[0] // 2
    lanes = firsts[0].shape[1] + firsts[2].shape[1]
    more = sums.shape[0]
    return stage_call(
        stage_three_kernel, where, (*firsts, *seconds, sums, sums_got),
        [
            ((rows, lanes), BF16), ((rows, lanes), F32),
            ((rows + more, lanes), BF16), ((rows + more, lanes), F32),
        ],
    )


def stage_four_kernel(where_ref, first_kept, first_got, second_kept, second_got, sent, kept):
    rows = first_kept.shape[0]
    low = where_ref[HIGH] % 2
    sums = added(second_kept, second_got, slice(rows, None))
    everything = slice(0, rows)
    for which, (before, got) in enumerate(((first_kept, first_got), (second_kept, second_got))):

        @pl.when(low == which)
        def _():
            kept[:rows, :] = added(before, got, everything)

        @pl.when(low != which)
        def _():
            sent[:rows, :] = added(before, got, everything).astype(BF16)

    kept[rows:, :] = sums
    sent[rows:, :] = sums.astype(BF16)


def stage_four_call(where, first_kept, first_got, second_kept, second_got):
    shape = second_kept.shape
    return stage_call(
        stage_four_kernel, where, (first_kept, first_got, second_kept, second_got),
        [(shape, BF16), (shape, F32)],
    )


def halve_rows_kernel(where_ref, before, got, sent, kept):
    unit = (before.shape[0] - 8) // 2
    high = where_ref[HIGH] // 2
    sums = added(before, got, slice(2 * unit, None))
    for out, which in ((sent, 1 - high), (kept, high)):
        span = pl.ds(pl.multiple_of(which * unit, unit), unit)
        out[:unit, :] = added(before, got, span).astype(out.dtype)
        out[unit:, :] = sums.astype(out.dtype)


def halve_rows_call(where, before, got):
    rows, lanes = before.shape
    shape = ((rows - 8) // 2 + 8, lanes)
    return stage_call(halve_rows_kernel, where, (before, got), [(shape, BF16), (shape, F32)])


def stage_five_kernel(where_ref, own, got, sent, mine, *, pairs):
    summed = own[...] + got[...].astype(F32)
    width = mine.shape[1]
    unit = own.shape[0] - 8
    group = width // 4
    blocks = ([], [])
    for part in range(4):
        starts = [(4 * pair + part) * LANES for pair in range(pairs)]
        columns = jnp.concatenate([summed[:unit, at : at + LANES] for at in starts], axis=1)
        blocks[0].append(columns[:, :group])
        blocks[1].append(columns[:, group:])
    for row in range(2):

        @pl.when(where_ref[ROW] == row)
        def _():
            mine[:unit, :] = jnp.concatenate(blocks[row], axis=1)
            sent[:unit, :] = jnp.concatenate(blocks[1 - row], axis=1).astype(BF16)

    mine[unit:, :] = summed[unit:, :width]
    sent[unit:, :] = summed[unit:, :width].astype(BF16)


def stage_five_call(where, own, got, pairs):
    rows, lanes = own.shape
    shape = (rows, lanes // pairs // LANES * HD * pairs)
    return stage_call(
        functools.partial(stage_five_kernel, pairs=pairs), where, (own, got), [(shape, BF16), (shape, F32)]
    )


def stage_six_kernel(where_ref, mine, other, down_got, *outs):
    *weights, sums, down = outs
    unit = mine.shape[0] - sums.shape[0]
    group = weights[0].shape[1]
    row = where_ref[ROW]
    for ref, place in ((mine, row), (other, 1 - row)):
        span = pl.ds(pl.multiple_of(place * unit, unit), unit)
        for part, out in enumerate(weights):
            out[span, :] = ref[:unit, part * group : (part + 1) * group].astype(F32)
    sums[...] = added(mine, other, slice(unit, None))
    down[...] = down_got[...].astype(F32).T


def stage_six_call(where, mine, other, down_got):
    rows, width = mine.shape
    unit, group = rows - 8, width // 4
    rows, lanes = down_got.shape
    return stage_call(
        stage_six_kernel, where, (mine, other, down_got),
        [((2 * unit, group), F32)] * 4 + [((8, width), F32), ((lanes, rows), F32)],
    )


def tokens_grad_kernel(
    where_ref,
    keep_ref, recv_ref, back_ref, got_ref, grad_res_ref, gain_ref, keep_out_ref, send_out_ref, sums_ref,
):
    step = pl.program_id(0)
    values = jnp.where(step == 0, recv_ref[...], keep_ref[...]).astype(F32)
    normal, inverse = normalize(values)
    back = back_ref[...] + got_ref[...].astype(F32)
    gains = jnp.sum(back * normal, axis=0, keepdims=True)
    shifts = jnp.sum(back, axis=0, keepdims=True)
    grad = (grad_res_ref[...].astype(F32) + norm_back(back, row_vector(gain_ref), normal, inverse)).astype(BF16)

    add_sums(sums_ref, step, 0, gains, shifts)

    @pl.when(step == 0)
    def _():
        send_out_ref[...] = grad

    @pl.when(step == 1)
    def _():
        keep_out_ref[0] = grad


def tokens_grad_call(where, keep, recv, back, got, grad_res, gain):
    rows, width = keep.shape
    row = pl.BlockSpec((rows, width), lambda i, w: (1 - i, 0))
    return call(
        tokens_grad_kernel,
        (2,),
        [whole((rows, width))] * 2 + [row] * 3 + [whole((width,))],
        [
            pl.BlockSpec((1, rows, width), lambda i, w: (w[ROW], 0, 0)),
            whole((rows, width)),
            whole((8, width)),
        ],
        [((2, rows, width), BF16), ((rows, width), BF16), ((8, width), F32)],
        [],
        SMALL, mib=8,
    )(where, keep, recv, back, got, grad_res, gain)


def local(
    tokens, gain_one, shift_one, w_query, w_key, w_value, w_out, gain_two, shift_two, w_up, w_down,
    cotangent, lengths,
):
    row_count, piece, width = tokens.shape
    n_dp = lax.axis_size("dp")
    n_seq = lax.axis_size("seq")
    count = n_dp // 4
    place = lax.axis_index("seq")
    core, row = place % 2, place // 2
    data = lax.axis_index("dp")
    high = data // count
    side = (data // (count // 2)) % 2
    total = n_seq * piece
    group = width // n_seq

    tok_recv = swap(pick(tokens, 1 - row), "seq", 2)
    tok_keep = pick(tokens, row)
    tok_keep_o = swap(tok_keep, "seq", 1)
    cot_keep = pick(cotangent, row)
    cot_recv = swap(pick(cotangent, 1 - row), "seq", 2)

    where = jnp.stack(
        [
            core, row, side, pick(lengths, row),
            2 * row + core, 2 * (1 - row) + core, 2 * row + 1 - core, 2 * (1 - row) + 1 - core,
            high,
        ]
    ).astype(jnp.int32)
    tables = tuple(jnp.asarray(table) for table in rotary_tables(total))
    out_blocks = w_out.reshape(n_seq, group, width)

    qkv, normed_t, w_qkv = project_call(
        0, where, tok_keep, tok_keep_o, gain_one, shift_one, (w_query, w_key, w_value), tables, ()
    )
    tok_recv, qkv, normed_t = together(tok_recv, qkv, normed_t)
    tok_recv_o = swap(tok_recv, "seq", 1)
    qkv, normed_t = project_call(
        1, where, tok_recv, tok_recv_o, gain_one, shift_one, (w_qkv,), tables, (qkv, normed_t)
    )
    ctx_m, ctx_o, ctx_t, lse = attend_call(where, qkv)
    cot_keep_o = swap(cot_keep, "seq", 1)
    ctx_m, ctx_o, ctx_t, cot_recv, cot_keep_o = together(ctx_m, ctx_o, ctx_t, cot_recv, cot_keep_o)
    cotangents = (cot_keep, cot_recv, cot_keep_o, swap(cot_recv, "seq", 1))
    ctx_got = swap(ctx_o, "seq", 1)
    residual, normed_two = residual_call(
        where, tok_keep, tok_recv, ctx_m, ctx_got, out_blocks, gain_two, shift_two
    )
    normed_two_o = swap(normed_two, "seq", 1)
    ctx_got_t = swap(ctx_t, "seq", 1)
    up_send0, up_send1, down_send0, down_keep0, active0, hidden0 = feed_call(
        False, where, normed_two, normed_two_o, cotangents, w_up, w_down
    )
    up_got0, up_got1 = swap(up_send0, "seq", 2), swap(up_send1, "seq", 2)
    down_got0 = swap(down_send0, "dp", count // 2)
    up_keep0, up_keep1, down_send1, down_keep1, active1, back_m, back_o = feed_call(
        True, where, normed_two, normed_two_o, cotangents, w_up, w_down, (hidden0,)
    )
    back_o, up_got0, down_got0 = together(back_o, up_got0, down_got0)
    back_got = swap(back_o, "seq", 1)
    down_got1 = swap(down_send1, "dp", count // 2)
    grad_low, sums_two = middle_call(where, residual, back_m, back_got, cot_keep, cot_recv, gain_two)
    grad_low_o = swap(grad_low, "seq", 1)

    block_rows = width // n_dp

    pairs = qkv.shape[1] // (3 * LANES)

    def upper(up, down):
        bit = count // 4
        up = up.reshape(4, count // 2, block_rows, width).astype(F32)
        down = down.reshape(4, group, -1).astype(F32)
        while bit > 0:
            mine = (data // bit) % 2
            size, lanes = up.shape[1] // 2, down.shape[2] // 2
            sent = lax.dynamic_slice_in_dim(up, (1 - mine) * size, size, 1).astype(BF16)
            up = lax.dynamic_slice_in_dim(up, mine * size, size, 1) + swap(sent, "dp", bit)
            sent = lax.dynamic_slice_in_dim(down, (1 - mine) * lanes, lanes, 2).astype(BF16)
            down = lax.dynamic_slice_in_dim(down, mine * lanes, lanes, 2) + swap(sent, "dp", bit)
            bit //= 2
        up = up.reshape(4, block_rows, width)
        folds = width // down.shape[2]
        size = group // folds
        down = jnp.concatenate([down[:, k * size : (k + 1) * size] for k in range(folds)], axis=2)
        both = jnp.concatenate([up, down], axis=1).astype(BF16)
        both = both.reshape((2, 2) + both.shape[1:])
        return pick(both, 1 - high % 2, 1), pick(both, high % 2, 1)

    def halved(before, got):
        if count == 2:
            return halve_call(where, before, got)
        both = before.astype(F32) + got.astype(F32)
        return pick(both, 1 - high // 2).astype(BF16), pick(both, high // 2)

    def feed_sums(own, got):
        lanes = w_down.shape[0] // n_dp
        if count == 2:
            return feed_sum_call(where, own, got, lanes)
        own = own + got.astype(F32)
        up, down = own[:block_rows], own[block_rows:].astype(BF16)
        down = jnp.concatenate([down[:, k * lanes : (k + 1) * lanes] for k in range(width // lanes)])
        return up, down

    def exchanged(values):
        perm = []
        for d in range(n_dp):
            for s in range(n_seq):
                second_bit = (d // count) % 2
                to_d = d + (s % 2 - second_bit) * count
                to_s = s - s % 2 + second_bit
                perm.append((d * n_seq + s, to_d * n_seq + to_s))
        return lax.ppermute(values, ("dp", "seq"), perm)

    inner = count // 2
    attention = (where, qkv, ctx_t, ctx_got_t, grad_low, grad_low_o, w_out, lse, tables, normed_t, w_qkv)
    *first_pieces, early = attend_back_call((0,), *attention)
    up_got1, down_got1, early = together(up_got1, down_got1, early)
    up_sent, up_kept, down_sent, down_kept = stage_one_call(
        where, up_keep0, up_keep1, up_got0, up_got1, down_keep0, down_keep1, down_got0, down_got1
    )
    up_sent, down_sent, early, first_pieces = together(up_sent, down_sent, early, first_pieces)
    up_got2 = swap(up_sent, "dp", inner)
    down_got2 = swap(down_sent, "seq", 2)
    first_got = (swap(first_pieces[0], "dp", inner), swap(first_pieces[2], "seq", 2))
    *pieces, normed_m, normed_o = attend_back_call(tuple(range(1, pairs)), *attention, early)
    pieces, normed_o, up_got2, down_got2, first_got = together(
        pieces, normed_o, up_got2, down_got2, first_got
    )
    last_got = (swap(pieces[0], "dp", inner), swap(pieces[2], "seq", 2))
    normed_got = swap(normed_o, "seq", 1)
    if count == 2:
        feed_sent, feed_kept = stage_two_call(where, up_kept, up_got2, down_kept, down_got2)
    else:
        feed_sent, feed_kept = upper(
            up_kept.astype(F32) + up_got2.astype(F32), down_kept.astype(F32) + down_got2.astype(F32)
        )
    feed_sent, normed_m = together(feed_sent, normed_m)
    feed_got = swap(feed_sent, "dp", count)
    out_m, out_o = feed_out_call(where, active0, active1, w_down)
    tok_buf, tok_send, sums_one = tokens_grad_call(
        where, tok_keep, tok_recv, normed_m, normed_got, grad_low, gain_one
    )

    sums = sums_one + sums_two
    sums_got = swap(sums, "seq", 1)
    if count == 2:
        last_got, tok_send, sums_got, feed_got, out_o = together(last_got, tok_send, sums_got, feed_got, out_o)
        sent_first, kept_first, sent_second, kept_second = stage_three_call(
            where,
            (first_pieces[1], first_got[0], pieces[1], last_got[0]),
            (first_pieces[3], first_got[1], pieces[3], last_got[1]),
            sums, sums_got,
        )
        sent_first, sent_second, tok_send, out_o, feed_got = together(
            sent_first, sent_second, tok_send, out_o, feed_got
        )
        got_first = swap(sent_first, "seq", 2)
        got_second = swap(sent_second, "dp", inner)
        feed_sent, feed_own = halved(feed_kept, feed_got)
        feed_got = swap(feed_sent, "dp", 2 * count)
        tok_back = swap(tok_send, "seq", 2)
        out_got = swap(out_o, "seq", 1)
        got_first, got_second, out_got, feed_sent = together(got_first, got_second, out_got, feed_sent)
        sent, kept = stage_four_call(where, kept_first, got_first, kept_second, got_second)
        sent, out_got = together(sent, out_got)
        got = swap(sent, "dp", count)
        out_send, out_buf = output_call(where, residual, out_m, out_got)
        got, out_send, feed_got = together(got, out_send, feed_got)
        sent, kept = halve_rows_call(where, kept, got)
        sent, out_send, feed_got = together(sent, out_send, feed_got)
        got = swap(sent, "dp", 2 * count)
        out_back = swap(out_send, "seq", 2)
        grad_up, grad_down = feed_sums(feed_own, feed_got)
        grad_down = exchanged(grad_down)
        got, tok_back, out_back = together(got, tok_back, out_back)
        sent, mine = stage_five_call(where, kept, got, pairs)
        other = swap(sent, "seq", 2)
        *ordered, sums, grad_down = stage_six_call(where, mine, other, grad_down)
    else:
        piece0, piece1, piece2, piece3 = (
            jnp.concatenate(two, axis=1) for two in zip(first_pieces, pieces)
        )
        shape = (2, 2, width // 16, -1)
        sides = jnp.stack([piece0, piece1]).reshape((2,) + shape)
        sides = jnp.stack([pick(sides, jnp.where(side == k, 1, 0)) for k in (0, 1)], 1)
        halves = jnp.stack([piece2, piece3]).reshape((2,) + shape)
        halves = jnp.stack([pick(halves, jnp.where(row == k, 1, 0)) for k in (0, 1)], 2)
        summed = jnp.stack([sides, halves], 1).reshape(width, pairs, 4, LANES).transpose(0, 2, 1, 3)
        summed = summed.reshape(width, 4, 2, group)
        other = swap(pick(summed, 1 - row, 2), "seq", 2).astype(F32)
        summed = (pick(summed, row, 2).astype(F32) + other).astype(BF16).reshape(width, -1)
        ordered = lax.psum_scatter(summed, "dp", scatter_dimension=0, tiled=True).astype(F32)
        tok_back = swap(tok_send, "seq", 2)
        out_send, out_buf = output_call(where, residual, out_m, swap(out_o, "seq", 1))
        out_back = swap(out_send, "seq", 2)
        feed_sent, feed_own = halved(feed_kept, feed_got)
        grad_up, grad_down = feed_sums(feed_own, swap(feed_sent, "dp", 2 * count))
        grad_down = exchanged(grad_down).astype(F32).T
        sums = sums + sums_got
        sums = sums + swap(sums, "seq", 2)
        bit = 1
        while bit < n_dp:
            sums = sums + swap(sums, "dp", bit)
            bit *= 2
        ordered = [ordered[:, k * group : (k + 1) * group] for k in range(4)]

    output = lax.dynamic_update_slice(out_buf, out_back[None], (1 - row, 0, 0))
    grad_tokens = lax.dynamic_update_slice(tok_buf, tok_back[None], (1 - row, 0, 0))
    return (
        output,
        grad_tokens,
        sums[0],
        sums[1],
        ordered[0],
        ordered[1],
        ordered[2],
        ordered[3],
        sums[2],
        sums[3],
        grad_up,
        grad_down,
    )


def solution(mesh):
    tokens = P("dp", "seq", None)
    weights = P("dp", "seq")
    return jax.shard_map(
        local,
        mesh=mesh,
        in_specs=(tokens,) + (P(),) * 10 + (tokens, P("dp")),
        out_specs=(tokens, tokens, P(), P(), weights, weights, weights, weights, P(), P(), weights, weights),
        check_vma=False,
    )
```

```python
import functools

import jax
import jax.numpy as jnp
import numpy as np
from jax import lax
from jax.experimental import pallas as pl
from jax.experimental.pallas import tpu as pltpu
from jax.sharding import PartitionSpec as P

HD = 64
EPSILON = 1e-05
MASKED = -1000000000.0
LANES = 128
BF16 = jnp.bfloat16
F32 = jnp.float32
CORE, ROW, SIDE, LENGTH, SPOT, HIGH = 0, 1, 2, 3, 4, 8


def swap(values, axis, bit):
    count = lax.axis_size(axis)
    return lax.ppermute(values, axis, [(i, i ^ bit) for i in range(count)])


def together(*values):
    return lax.optimization_barrier(values)


def pick(values, index, axis=0):
    return lax.dynamic_index_in_dim(values, index, axis, keepdims=False)


def dot(left, right):
    return jnp.dot(left, right, preferred_element_type=F32)


def dot_back(left, right):
    return lax.dot_general(left, right, (((1,), (1,)), ((), ())), preferred_element_type=F32)


def normalize(values):
    average = jnp.mean(values, axis=-1, keepdims=True)
    centred = values - average
    variance = jnp.mean(centred * centred, axis=-1, keepdims=True)
    inverse = lax.rsqrt(variance + EPSILON)
    return centred * inverse, inverse


def norm_back(grad, gain, normal, inverse):
    scaled = grad * gain
    first = jnp.mean(scaled, axis=-1, keepdims=True)
    second = jnp.mean(scaled * normal, axis=-1, keepdims=True)
    return (scaled - first - normal * second) * inverse


def row_vector(ref):
    return ref[...].reshape(1, ref.shape[0])


def swap_halves(values):
    lane = lax.broadcasted_iota(jnp.int32, values.shape, 1)
    up = pltpu.roll(values, LANES - HD // 2, 1)
    down = pltpu.roll(values, HD // 2, 1)
    return jnp.where(lane % HD < HD // 2, up, down)


def rotary_tables(length):
    lane = np.arange(LANES)
    frequency = 10000.0 ** (-2.0 * (lane % (HD // 2)) / HD)
    angles = np.arange(length)[:, None] * frequency[None, :]
    sign = np.where(lane % HD < HD // 2, -1.0, 1.0)
    return np.cos(angles).astype(np.float32), (sign * np.sin(angles)).astype(np.float32)


def kept_rows(where_ref, block, rows, lanes):
    spot = lax.broadcasted_iota(jnp.int32, (rows, lanes), 0) + where_ref[SPOT + block] * rows
    return spot < where_ref[LENGTH]


SMALL = pl.CostEstimate(flops=1, bytes_accessed=1, transcendentals=0)


def whole(shape):
    return pl.BlockSpec(shape, lambda *_: (0,) * len(shape))


def call(kernel, grid, in_specs, out_specs, out_shape, scratch, estimate, aliases=None, mib=16):
    return pl.pallas_call(
        kernel,
        grid_spec=pltpu.PrefetchScalarGridSpec(
            num_scalar_prefetch=1,
            grid=grid,
            in_specs=in_specs,
            out_specs=out_specs,
            scratch_shapes=scratch,
        ),
        out_shape=[jax.ShapeDtypeStruct(shape, kind) for shape, kind in out_shape],
        input_output_aliases=aliases or {},
        compiler_params=pltpu.CompilerParams(vmem_limit_bytes=mib * 1024 * 1024),
        cost_estimate=estimate,
    )


def pair_columns(ref, core, pair):
    group = ref.shape[1] // 4
    pieces = []
    start, end = pair * LANES, (pair + 1) * LANES
    if start < group:
        pieces.append(ref[:, core * group + start : core * group + min(end, group)])
    if end > group:
        begin = max(start, group)
        pieces.append(ref[:, (1 + core) * group + begin : (1 + core) * group + end])
    return pieces[0] if len(pieces) == 1 else jnp.concatenate(pieces, axis=1)


def project_kernel(where_ref, mine_ref, other_ref, gain_ref, shift_ref, *rest, first, pairs):
    step = pl.program_id(0)
    if first:
        wq_ref, wk_ref, wv_ref, cos_ref, sin_ref, qkv_ref, normed_t_ref, weight_ref = rest

        @pl.when(step == 0)
        def _():
            for core in range(2):

                @pl.when(where_ref[CORE] == core)
                def _():
                    for part, ref in enumerate((wq_ref, wk_ref, wv_ref)):
                        for pair in range(pairs):
                            start = (3 * pair + part) * LANES
                            weight_ref[:, start : start + LANES] = pair_columns(ref, core, pair)
    else:
        weight_ref, cos_ref, sin_ref, _, _, qkv_ref, normed_t_ref = rest
    values = jnp.where(step == 0, mine_ref[...], other_ref[...]).astype(F32)
    normal, _ = normalize(values)
    normed = (normal * row_vector(gain_ref) + row_vector(shift_ref)).astype(BF16)
    normed_t_ref[...] = normed.T
    cosine, sine = cos_ref[...], sin_ref[...]
    width = 3 * LANES
    for pair in range(pairs):
        out = dot(normed, weight_ref[:, pair * width : (pair + 1) * width])
        for part in range(3):
            piece = out[:, part * LANES : (part + 1) * LANES]
            if part < 2:
                piece = piece * cosine + swap_halves(piece) * sine
                if part == 0:
                    piece = piece * (HD ** (-0.5))
            start = pair * width + part * LANES
            qkv_ref[:, start : start + LANES] = piece.astype(BF16)


def project_call(turn, where, mine, other, gain, shift, weights, tables, previous):
    rows, width = mine.shape
    out_width = 3 * width // 2
    total = 4 * rows
    block = lambda i, w: (2 * i + turn, 0)
    table = pl.BlockSpec((rows, LANES), lambda i, w: (w[SPOT + 2 * i + turn], 0))
    in_specs = [whole((rows, width))] * 2 + [whole((width,))] * 2
    in_specs += [whole(weight.shape) for weight in weights] + [table, table]
    out_specs = [
        pl.BlockSpec((rows, out_width), block),
        pl.BlockSpec((width, rows), lambda i, w: (0, 2 * i + turn)),
    ]
    out_shape = [((total, out_width), BF16), ((width, total), BF16)]
    aliases = {}
    if previous:
        aliases = {1 + len(in_specs): 0, 2 + len(in_specs): 1}
        in_specs += [pl.BlockSpec(memory_space=pl.ANY)] * 2
    else:
        out_specs.append(whole((width, out_width)))
        out_shape.append(((width, out_width), BF16))
    return call(
        functools.partial(project_kernel, first=not previous, pairs=out_width // (3 * LANES)),
        (2,), in_specs, out_specs, out_shape, [],
        SMALL, aliases, 12,
    )(where, mine, other, gain, shift, *weights, *tables, *previous)


def mask_lane(lane, head, keys, bias):
    return jnp.where(lane == (HD if head == 0 else 0), bias, keys)


def only_head(lane, head, values):
    return jnp.where(lane // HD == head, values, jnp.zeros_like(values))


def with_one(lane, head, values):
    one = lane == (HD if head == 0 else 0)
    return jnp.where(one, jnp.ones_like(values), only_head(lane, head, values))


def fill_bias(where_ref, bias_ref):
    rows = bias_ref.shape[0] // 4
    for block in range(4):
        kept = kept_rows(where_ref, block, rows, LANES)
        bias_ref[block * rows : (block + 1) * rows, :] = jnp.where(kept, 0.0, MASKED).astype(BF16)


def attend_kernel(
    where_ref, query_ref, key_ref, value_ref, mine_ref, other_ref, ctx_t_ref, lse_ref, bias_ref, ctx_ref,
    *, tile,
):
    total = query_ref.shape[0]
    lane = lax.broadcasted_iota(jnp.int32, (1, LANES), 1)

    @pl.when(pl.program_id(0) == 0)
    def _():
        fill_bias(where_ref, bias_ref)

    keys = key_ref[...]
    values_t = value_ref[...].T
    for head in range(2):
        key_aug = mask_lane(lane, head, keys, bias_ref[...])
        for start in range(0, total, tile):
            queries = with_one(lane, head, query_ref[start : start + tile, :])
            scores = dot_back(key_aug, queries)
            highest = jnp.max(scores, axis=0, keepdims=True)
            weights = jnp.exp(scores - highest)
            sums = jnp.sum(weights, axis=0, keepdims=True)
            context = dot(values_t[head * HD : (head + 1) * HD, :], weights.astype(BF16))
            ctx_ref[head * HD : (head + 1) * HD, start : start + tile] = context / sums
            lse_ref[0, head : head + 1, start : start + tile] = highest + jnp.log(sums)
    ctx_t_ref[...] = ctx_ref[...].astype(BF16)
    contexts = ctx_ref[...].T.astype(BF16)
    mine_ref[...] = contexts[: total // 2]
    other_ref[...] = contexts[total // 2 :]


def attend_call(where, qkv):
    total, width = qkv.shape
    pairs = width // (3 * LANES)
    width //= 3
    half = total // 2
    column = lambda part: pl.BlockSpec((total, LANES), lambda p, w: (0, 3 * p + part))
    out_column = pl.BlockSpec((half, LANES), lambda p, w: (0, p))
    return call(
        functools.partial(attend_kernel, tile=total),
        (pairs,),
        [column(0), column(1), column(2)],
        [
            out_column, out_column,
            pl.BlockSpec((LANES, total), lambda p, w: (p, 0)),
            pl.BlockSpec((1, 8, total), lambda p, w: (p, 0, 0)),
        ],
        [((half, width), BF16), ((half, width), BF16), ((width, total), BF16), ((pairs, 8, total), F32)],
        [pltpu.VMEM((total, LANES), BF16), pltpu.VMEM((LANES, total), F32)],
        SMALL, mib=16,
    )(where, qkv, qkv, qkv)


def stack_rows(refs):
    return jnp.concatenate([ref[0] for ref in refs], axis=0)


def residual_kernel(
    where_ref, keep_ref, recv_ref, mine_ref, got_ref, w0_ref, w1_ref, w2_ref, w3_ref,
    gain_ref, shift_ref, res_ref, normed_ref,
):
    step = pl.program_id(0)
    values = jnp.where(step == 0, keep_ref[...], recv_ref[...]).astype(F32)
    attended = dot(mine_ref[...], stack_rows((w0_ref, w1_ref)))
    attended += dot(got_ref[...], stack_rows((w2_ref, w3_ref)))
    residual = values + attended
    res_ref[...] = residual
    normal, _ = normalize(residual)
    normed_ref[...] = (normal * row_vector(gain_ref) + row_vector(shift_ref)).astype(BF16)


def out_weight_specs(group, width):
    places = (
        lambda w: w[CORE],
        lambda w: 2 + w[CORE],
        lambda w: 1 - w[CORE],
        lambda w: 3 - w[CORE],
    )
    return [pl.BlockSpec((1, group, width), lambda i, w, at=at: (at(w), 0, 0)) for at in places]


def residual_call(where, keep, recv, ctx_mine, ctx_got, w_out, gain, shift):
    rows, width = keep.shape
    heads = ctx_mine.shape[1]
    row = lambda lanes: pl.BlockSpec((rows, lanes), lambda i, w: (i, 0))
    return call(
        residual_kernel,
        (2,),
        [whole((rows, width))] * 2 + [row(heads)] * 2
        + out_weight_specs(heads // 2, width) + [whole((width,))] * 2,
        [row(width)] * 2,
        [((2 * rows, width), F32), ((2 * rows, width), BF16)],
        [],
        SMALL, mib=10,
    )(where, keep, recv, ctx_mine, ctx_got, w_out, w_out, w_out, w_out, gain, shift)


def gelu_both(values):
    root = 0.7978845608028654
    bend = (root * 0.044715) * (values * values)
    half = 0.5 * jnp.tanh(values * (root + bend)) + 0.5
    steep = values * (2.0 * root + 6.0 * bend)
    return values * half, half * ((1.0 - half) * steep + 1.0)


def fill_cotangent(where_ref, refs, grad_ref):
    rows, width = refs[0].shape
    for place, ref in enumerate(refs):
        kept = kept_rows(where_ref, place, rows, width)
        grad_ref[place * rows : (place + 1) * rows, :] = jnp.where(kept, ref[...], jnp.zeros_like(ref))


def feed_kernel(
    where_ref,
    normed_m_ref, normed_o_ref, cot0_ref, cot1_ref, cot2_ref, cot3_ref, up_ref, down_ref,
    *rest, tile, last,
):
    if last:
        before_ref, up_before_ref, later_ref, *rest = rest
        up0_ref, up1_ref, send_ref, keep_ref, active_ref, back_m_ref, back_o_ref = rest[:7]
        normed_ref, grad_ref, normed_t_ref, grad_t_ref, hidden_ref = rest[7:]
    else:
        up0_ref, up1_ref, send_ref, later_ref, keep_ref, active_ref, hidden_ref = rest[:7]
        normed_ref, grad_ref, normed_t_ref, grad_t_ref = rest[7:]
    half, width = normed_m_ref.shape
    block = up_ref.shape[1]
    normed_ref[:half, :] = normed_m_ref[...]
    normed_ref[half:, :] = normed_o_ref[...]
    fill_cotangent(where_ref, (cot0_ref, cot1_ref, cot2_ref, cot3_ref), grad_ref)
    normed_t_ref[...] = normed_ref[...].T
    grad_t_ref[...] = grad_ref[...].T
    for start in range(0, block, tile):
        span = slice(start, start + tile)
        hidden = dot(normed_ref[...], up_ref[:, span])
        active, slope = gelu_both(hidden)
        active_ref[:, span] = active.astype(BF16)
        grad_active = dot_back(grad_ref[...], down_ref[span, :])
        hidden_ref[:, span] = (grad_active * slope).astype(BF16)
    up_grad = dot(normed_t_ref[...], hidden_ref[...]).astype(BF16)
    up0_ref[...] = up_grad[: width // 4]
    up1_ref[...] = up_grad[width // 4 :]
    down_grad = dot(grad_t_ref[...], active_ref[...]).astype(BF16)
    part = block // 2
    for side in range(2):
        piece = down_grad[:, side * part : (side + 1) * part]

        @pl.when(where_ref[SIDE] == side)
        def _():
            keep_ref[...] = piece

        @pl.when(where_ref[SIDE] != side)
        def _():
            if last:
                send_ref[later_ref.shape[0] :, :] = piece
            else:
                send_ref[...] = piece[: send_ref.shape[0]]
                later_ref[...] = piece[send_ref.shape[0] :]

    if last:
        send_ref[: later_ref.shape[0], :] = later_ref[...]
        back = dot_back(before_ref[...], up_before_ref[...]) + dot_back(hidden_ref[...], up_ref[...])
        back_m_ref[...] = back[:half]
        back_o_ref[...] = back[half:].astype(BF16)


def feed_high(last, w):
    return w[ROW] if last else 1 - w[ROW]


def feed_call(last, where, normed_m, normed_o, cotangents, w_up, w_down, before=()):
    half, width = normed_m.shape
    total = 2 * half
    block = w_up.shape[1] // 4
    part = block // 2
    token = whole((half, width))
    up_block = lambda last: pl.BlockSpec(
        (width, block), lambda i, w: (0, 2 * feed_high(last, w) + w[CORE])
    )
    down_block = pl.BlockSpec((block, width), lambda i, w: (2 * feed_high(last, w) + w[CORE], 0))
    in_specs = [token, token] + [whole((half // 2, width))] * 4 + [up_block(last), down_block]
    args = [normed_m, normed_o, *cotangents, w_up, w_down]
    out_shape = [
        ((width // 4, block), BF16),
        ((width - width // 4, block), BF16),
        ((width, part), BF16),
        ((total, block), BF16),
    ]
    later = width // 3
    scratch = [
        pltpu.VMEM((total, width), BF16),
        pltpu.VMEM((total, width), BF16),
        pltpu.VMEM((width, total), BF16),
        pltpu.VMEM((width, total), BF16),
    ]
    if last:
        in_specs += [whole((total, block)), up_block(False), whole((later, part))]
        args += [before[0], w_up, before[1]]
        out_shape.insert(2, ((later + width, part), BF16))
        out_shape += [((half, width), F32), ((half, width), BF16)]
        scratch.append(pltpu.VMEM((total, block), BF16))
    else:
        out_shape[2:2] = [((width - later, part), BF16), ((later, part), BF16)]
        out_shape.append(((total, block), BF16))
    return call(
        functools.partial(feed_kernel, tile=block, last=last),
        (1,), in_specs, [whole(shape) for shape, _ in out_shape], out_shape, scratch, SMALL, mib=20,
    )(where, *args)


def feed_out_kernel(where_ref, first_ref, last_ref, down0_ref, down1_ref, mine_ref, *other_refs):
    out = dot(first_ref[...], down0_ref[...]) + dot(last_ref[...], down1_ref[...])
    size = other_refs[0].shape[0]

    @pl.when(pl.program_id(0) == 0)
    def _():
        for part, ref in enumerate(other_refs):
            ref[...] = out[part * size : (part + 1) * size].astype(BF16)

    @pl.when(pl.program_id(0) == 1)
    def _():
        mine_ref[...] = out


def feed_out_call(where, first, last, w_down):
    total, block = first.shape
    width = w_down.shape[1]
    half = total // 2
    row = pl.BlockSpec((half, block), lambda i, w: (1 - i, 0))
    down = [
        pl.BlockSpec((block, width), lambda i, w, last=last: (2 * feed_high(last, w) + w[CORE], 0))
        for last in (False, True)
    ]
    return call(
        feed_out_kernel,
        (2,),
        [row, row, *down],
        [whole((half, width))] + [whole((half // 4, width))] * 4,
        [((half, width), F32)] + [((half // 4, width), BF16)] * 4,
        [], SMALL, mib=12,
    )(where, first, last, w_down, w_down)


def by_step(refs, step):
    low = jnp.concatenate([refs[0][...], refs[1][...]], axis=0)
    high = jnp.concatenate([refs[2][...], refs[3][...]], axis=0)
    return jnp.where(step == 0, high, low).astype(F32)


def output_kernel(where_ref, res_ref, out_ref, got0_ref, got1_ref, got2_ref, got3_ref, send_ref, keep_ref):
    step = pl.program_id(0)
    output = res_ref[...] + out_ref[...] + by_step((got0_ref, got1_ref, got2_ref, got3_ref), step)
    kept = kept_rows(where_ref, 1 - step, *output.shape)
    output = jnp.where(kept, output, jnp.zeros_like(output)).astype(BF16)

    @pl.when(step == 0)
    def _():
        send_ref[...] = output

    @pl.when(step == 1)
    def _():
        keep_ref[0] = output


def output_call(where, residual, out, got):
    half, width = residual.shape
    rows = half // 2
    row = pl.BlockSpec((rows, width), lambda i, w: (1 - i, 0))
    return call(
        output_kernel,
        (2,),
        [row] * 2 + [whole((rows // 2, width))] * 4,
        [whole((rows, width)), pl.BlockSpec((1, rows, width), lambda i, w: (w[ROW], 0, 0))],
        [((rows, width), BF16), ((2, rows, width), BF16)],
        [], SMALL, mib=8,
    )(where, residual, out, *got)


def add_sums(sums_ref, step, row, gains, shifts):
    @pl.when(step == 0)
    def _():
        sums_ref[...] = jnp.zeros_like(sums_ref)

    sums_ref[row : row + 1, :] += gains
    sums_ref[row + 1 : row + 2, :] += shifts


def middle_kernel(
    where_ref,
    res_ref, back_ref, back_got_ref, cot0_ref, cot1_ref, gain_ref, grad_low_ref, sums_ref,
):
    step = pl.program_id(0)
    residual = res_ref[...]
    kept = kept_rows(where_ref, step, *residual.shape)
    normal, inverse = normalize(residual)
    back = back_ref[...] + back_got_ref[...].astype(F32)
    gains = jnp.sum(back * normal, axis=0, keepdims=True)
    shifts = jnp.sum(back, axis=0, keepdims=True)

    add_sums(sums_ref, step, 2, gains, shifts)
    cotangent = jnp.where(step == 0, cot0_ref[...], cot1_ref[...]).astype(F32)
    cotangent = jnp.where(kept, cotangent, jnp.zeros_like(cotangent))
    grad = cotangent + norm_back(back, row_vector(gain_ref), normal, inverse)
    grad_low_ref[...] = grad.astype(BF16)


def middle_call(where, residual, back_m, back_got, cot_keep, cot_recv, gain):
    half, width = residual.shape
    rows = half // 2
    row = pl.BlockSpec((rows, width), lambda i, w: (i, 0))
    return call(
        middle_kernel,
        (2,),
        [row] * 3 + [whole((rows, width))] * 2 + [whole((width,))],
        [row, whole((8, width))],
        [((half, width), BF16), ((8, width), F32)],
        [], SMALL, mib=8,
    )(where, residual, back_m, back_got, cot_keep, cot_recv, gain)


def piece_order(where_ref):
    side, row = where_ref[SIDE], where_ref[ROW]
    order = []
    for kept in (0, 1):
        mine = side if kept else 1 - side
        order += [8 * high + 2 * mine + half for high in (0, 1) for half in (0, 1)]
    for kept in (0, 1):
        mine = row if kept else 1 - row
        order += [8 * high + 4 + 2 * one + mine for high in (0, 1) for one in (0, 1)]
    return order


def attend_back_kernel(
    where_ref,
    query_ref, key_ref, value_ref, ctx_ref, grad_m_ref, grad_o_ref, w0_ref, w1_ref, lse_ref,
    ctx_mine_hbm, ctx_got_hbm, cos_hbm, sin_hbm, normed_t_hbm, *rest,
    score_scale, first, last,
):
    if last:
        early_ref, weight_ref, *rest = rest
        out_refs, back_m_ref, back_o_refs = rest[:4], rest[4], rest[5:9]
        *rest, grads_ref = rest[9:]
    else:
        out_refs, grads_ref = rest[:4], rest[4]
        rest = rest[5:]
    bias_ref, grad_ref, columns_ref, dqt_ref, dk_acc, dv_acc, qkv_ref, own_ref = rest[:8]
    ctx_mine_ref, ctx_got_ref, cos_ref, sin_ref, normed_t_ref, semaphores = rest[8:]
    step = pl.program_id(0)
    total = query_ref.shape[0]
    half = total // 2
    model = grad_m_ref.shape[1]
    lane = lax.broadcasted_iota(jnp.int32, (1, LANES), 1)
    unit = model // 16
    group = model // 4
    rows = total // 4
    late = [(ctx_mine_hbm, ctx_mine_ref), (ctx_got_hbm, ctx_got_ref), (normed_t_hbm, normed_t_ref)]
    for source, target in ((cos_hbm, cos_ref), (sin_hbm, sin_ref)):
        for block in range(4):
            begin = pl.multiple_of(where_ref[SPOT + block] * rows, rows)
            late.append((source.at[pl.ds(begin, rows)], target.at[pl.ds(block * rows, rows)]))

    def copies():
        return [
            pltpu.make_async_copy(source, target, semaphores.at[k])
            for k, (source, target) in enumerate(late)
        ]

    @pl.when(step == 0)
    def _():
        for copy in copies():
            copy.start()
        fill_bias(where_ref, bias_ref)
        grad_ref[:half, :] = grad_m_ref[...]
        grad_ref[half:, :] = grad_o_ref[...]

    for place, pair in enumerate(first):
        for core in range(2):

            @pl.when((step == place) & (where_ref[CORE] == core))
            def _():
                columns_ref[...] = pair_columns(grad_ref, core, pair)

    wout = jnp.concatenate([w0_ref[...], w1_ref[...]], axis=0)
    gctx = dot_back(grad_ref[...], wout).astype(BF16)
    products = gctx.astype(F32).T * ctx_ref[...].astype(F32)
    keys = key_ref[...]
    keys_t = keys.T
    values = value_ref[...]
    queries = query_ref[...]
    for head in range(2):
        key_aug = mask_lane(lane, head, keys, bias_ref[...])
        delta = jnp.sum(products[head * HD : (head + 1) * HD, :], axis=0, keepdims=True)
        scores = dot_back(key_aug, with_one(lane, head, queries))
        weights = jnp.exp(scores - lse_ref[0, head : head + 1, :])
        grads = only_head(lane, head, gctx)
        grad_weights = dot_back(values, grads)
        grad_scores = (weights * (grad_weights - delta)).astype(BF16)
        dv = dot(weights.astype(BF16), grads)
        dk = dot(grad_scores, only_head(lane, head, queries))
        dqt_ref[head * HD : (head + 1) * HD, :] = dot(
            keys_t[head * HD : (head + 1) * HD, :], grad_scores
        )
        if head == 0:
            dv_acc[...] = dv
            dk_acc[...] = dk
        else:
            dv_acc[...] += dv
            dk_acc[...] += dk

    @pl.when(step == 0)
    def _():
        for copy in copies():
            copy.wait()

    cosine, sine = cos_ref[...], sin_ref[...]
    dq = dqt_ref[...].T * score_scale
    dk = dk_acc[...]
    dq = (dq * cosine - swap_halves(dq) * sine).astype(BF16)
    dk = (dk * cosine - swap_halves(dk) * sine).astype(BF16)
    grads = jnp.concatenate([dq, dk, dv_acc[...].astype(BF16)], axis=1)
    qkv_ref[...] = dot(normed_t_ref[...], grads).astype(BF16)
    columns = columns_ref[...]
    turned = jnp.concatenate([columns[half:], columns[:half]], axis=0)
    own_ref[0] = dot(ctx_mine_ref[...], columns).astype(BF16)
    own_ref[1] = dot(ctx_got_ref[...], turned).astype(BF16)
    for place, source in enumerate(piece_order(where_ref)):
        ref = out_refs[place // 4]
        span = slice(place % 4 * unit, (place % 4 + 1) * unit)
        ref[span, : 3 * LANES] = qkv_ref[pl.ds(pl.multiple_of(source * unit, unit), unit), :]
        block = source // 4
        other = jnp.where(block % 2 == where_ref[CORE], 0, 1)
        inside = pl.multiple_of((block // 2) * group + (source % 4) * unit, unit)
        ref[span, 3 * LANES :] = own_ref[other, pl.ds(inside, unit), :]
    if not last:
        grads_ref[...] = grads
        return
    width = 3 * LANES
    for place in range(len(first) - 1):

        @pl.when(step == place)
        def _():
            grads_ref[:, place * width : (place + 1) * width] = grads

    @pl.when(step == len(first) - 1)
    def _():
        split = early_ref.shape[1]
        back = dot_back(early_ref[...], weight_ref[:, :split])
        if len(first) > 1:
            back += dot_back(grads_ref[...], weight_ref[:, split:-width])
        back += dot_back(grads, weight_ref[:, -width:])
        back_m_ref[...] = back[:half]
        size = half // 4
        for part, ref in enumerate(back_o_refs):
            ref[...] = back[half + part * size : half + (part + 1) * size].astype(BF16)


def attend_back_call(
    pairs, where, qkv, ctx_t, ctx_got_t, grad_m, grad_o, w_out, lse, tables, normed_t, weight, early=None
):
    total, width = qkv.shape
    width //= 3
    half, model = grad_m.shape
    quarter = model // 4
    last = early is not None
    begin = pairs[0]
    column = lambda part: pl.BlockSpec((total, LANES), lambda i, w: (0, 3 * (begin + i) + part))

    def head_rows(which):
        per = width // HD // 2

        def at(i, w):
            head = 2 * (begin + i) + which
            return (head // per * 2 * per + w[CORE] * per + head % per, 0)

        return pl.BlockSpec((HD, model), at)

    in_specs = [
        column(0), column(1), column(2),
        pl.BlockSpec((LANES, total), lambda i, w: (begin + i, 0)),
        whole((half, model)), whole((half, model)),
        head_rows(0), head_rows(1),
        pl.BlockSpec((1, 8, total), lambda i, w: (begin + i, 0, 0)),
    ]
    in_specs += [pl.BlockSpec(memory_space=pl.ANY)] * 5
    args = [
        qkv, qkv, qkv, ctx_t, grad_m, grad_o, w_out, w_out, lse, ctx_t, ctx_got_t, *tables, normed_t,
    ]
    out_specs = [pl.BlockSpec((quarter, 4 * LANES), lambda i, w: (0, i))] * 4
    out_shape = [((quarter, 4 * LANES * len(pairs)), BF16)] * 4
    if last:
        in_specs += [whole(early.shape), whole(weight.shape)]
        args += [early, weight]
        out_specs += [whole((half, model))] + [whole((half // 4, model))] * 4
        out_shape += [((half, model), F32)] + [((half // 4, model), BF16)] * 4
    else:
        out_specs.append(pl.BlockSpec((total, 3 * LANES), lambda i, w: (0, i)))
        out_shape.append(((total, 3 * LANES * len(pairs)), BF16))
    return call(
        functools.partial(attend_back_kernel, score_scale=HD ** (-0.5), first=pairs, last=last),
        (len(pairs),), in_specs, out_specs, out_shape,
        [
            pltpu.VMEM((total, LANES), BF16),
            pltpu.VMEM((total, model), BF16),
            pltpu.VMEM((total, LANES), BF16),
            pltpu.VMEM((LANES, total), F32),
            pltpu.VMEM((total, LANES), F32),
            pltpu.VMEM((total, LANES), F32),
            pltpu.VMEM((model, 3 * LANES), BF16),
            pltpu.VMEM((2, width, LANES), BF16),
            pltpu.VMEM((width, total), BF16),
            pltpu.VMEM((width, total), BF16),
            pltpu.VMEM((total, LANES), F32),
            pltpu.VMEM((total, LANES), F32),
            pltpu.VMEM((model, total), BF16),
            pltpu.SemaphoreType.DMA((11,)),
        ]
        + ([pltpu.VMEM((total, max(len(pairs) - 1, 1) * 3 * LANES), BF16)] if last else []),
        SMALL, mib=26,
    )(where, *args)


def stage_one_kernel(
    where_ref,
    up_keep0, up_keep1, up_got0, up_got1, down_keep0, down_keep1, down_got0, down_got1,
    up_sent, up_kept, down_sent, down_kept,
):
    side, row = where_ref[SIDE], where_ref[ROW]
    unit = up_keep0.shape[0] // 2
    for one in range(4):
        keep, got, before = (up_keep1, up_got1, 1) if one else (up_keep0, up_got0, 0)
        to = slice(one * unit, (one + 1) * unit)
        for out, mine in ((up_sent, 1 - side), (up_kept, side)):
            span = pl.ds(pl.multiple_of((2 * (one - before) + mine) * unit, unit), unit)
            out[to, :] = (keep[span, :].astype(F32) + got[span, :].astype(F32)).astype(BF16)
    size = down_keep0.shape[0] // 2
    soon = down_got0.shape[0]
    later = down_keep0.shape[0] - soon
    for half in range(2):
        span = slice(half * size, (half + 1) * size)
        got0 = down_got0[half * size : min((half + 1) * size, soon), :]
        if (half + 1) * size > soon:
            got0 = jnp.concatenate([got0, down_got1[: (half + 1) * size - soon, :]], axis=0)
        got1 = down_got1[later + half * size : later + (half + 1) * size, :]
        for block, keep, got in ((1 - row, down_keep0, got0), (row, down_keep1, got1)):
            values = (keep[span, :].astype(F32) + got.astype(F32)).astype(BF16)

            @pl.when(row == half)
            def _():
                down_kept[block] = values

            @pl.when(row != half)
            def _():
                down_sent[block] = values


def stage_one_call(where, *parts):
    rows, width = 2 * parts[0].shape[0], parts[0].shape[1]
    size, lanes = parts[4].shape[0] // 2, parts[4].shape[1]
    out_shape = [((rows, width), BF16)] * 2 + [((2, size, lanes), BF16)] * 2
    return call(
        stage_one_kernel,
        (1,),
        [whole(part.shape) for part in parts],
        [whole(shape) for shape, _ in out_shape],
        out_shape, [], SMALL, mib=8,
    )(where, *parts)


def added(one, two, span):
    return one[span, :].astype(F32) + two[span, :].astype(F32)


def stage_two_kernel(where_ref, up_kept, up_got, down_kept, down_got, sent, kept):
    unit = kept.shape[1] // 2
    size, lanes = down_kept.shape[1] // 2, down_kept.shape[2]
    low = where_ref[HIGH] % 2
    for high in range(2):
        for out, which in ((sent, 1 - low), (kept, low)):
            span = pl.ds(pl.multiple_of((2 * high + which) * unit, unit), unit)
            out[high, :unit, :] = added(up_kept, up_got, span).astype(BF16)
            for fold in range(size // unit):
                span = pl.ds(pl.multiple_of(which * size + fold * unit, unit), unit)
                values = added(down_kept.at[high], down_got.at[high], span)
                out[high, unit:, fold * lanes : (fold + 1) * lanes] = values.astype(BF16)


def halve_kernel(where_ref, before, got, sent, kept):
    high = where_ref[HIGH] // 2
    for out, which in ((sent, 1 - high), (kept, high)):
        out[...] = (before[which].astype(F32) + got[which].astype(F32)).astype(out.dtype)


def halve_call(where, before, got):
    shape = before.shape[1:]
    return stage_call(halve_kernel, where, (before, got), [(shape, BF16), (shape, F32)])


def stage_call(kernel, where, inputs, out_shape, mib=8):
    return call(
        kernel, (1,), [whole(one.shape) for one in inputs], [whole(shape) for shape, _ in out_shape],
        out_shape, [], SMALL, mib=mib,
    )(where, *inputs)


def stage_two_call(where, up_kept, up_got, down_kept, down_got):
    rows, width = up_kept.shape
    part = (2, rows // 2, width)
    return stage_call(
        stage_two_kernel, where, (up_kept, up_got, down_kept, down_got), [(part, BF16)] * 2
    )


def feed_sum_kernel(where_ref, own, got, up, down):
    unit, lanes = up.shape[0], down.shape[1]
    summed = own[...] + got[...].astype(F32)
    up[...] = summed[:unit]
    for fold in range(up.shape[1] // lanes):
        values = summed[unit:, fold * lanes : (fold + 1) * lanes]
        down[fold * unit : (fold + 1) * unit, :] = values.astype(BF16)


def feed_sum_call(where, own, got, lanes):
    rows, width = own.shape
    unit = rows // 2
    return stage_call(
        feed_sum_kernel, where, (own, got), [((unit, width), F32), ((unit * width // lanes, lanes), BF16)]
    )


def stage_three_kernel(where_ref, *refs):
    firsts, seconds, (sums, sums_got) = refs[:4], refs[4:8], refs[8:10]
    first_sent, first_kept, second_sent, second_kept = refs[10:]
    side, row = where_ref[SIDE], where_ref[ROW]
    unit = first_sent.shape[0] // 2
    split = firsts[0].shape[1]
    for parts, mine, sent, kept in (
        (firsts, row, first_sent, first_kept),
        (seconds, side, second_sent, second_kept),
    ):
        for high in range(2):
            to = slice(high * unit, (high + 1) * unit)
            for out, which in ((sent, 1 - mine), (kept, mine)):
                span = pl.ds(pl.multiple_of((2 * high + which) * unit, unit), unit)
                out[to, :split] = added(parts[0], parts[1], span).astype(out.dtype)
                out[to, split:] = added(parts[2], parts[3], span).astype(out.dtype)
    summed = sums[...] + sums_got[...]
    width = summed.shape[1]
    for out in (second_sent, second_kept):
        out[2 * unit :, :] = jnp.zeros_like(out[2 * unit :, :])
        out[2 * unit :, :width] = summed.astype(out.dtype)


def stage_three_call(where, firsts, seconds, sums, sums_got):
    rows = firsts[0].shape[0] // 2
    lanes = firsts[0].shape[1] + firsts[2].shape[1]
    more = sums.shape[0]
    return stage_call(
        stage_three_kernel, where, (*firsts, *seconds, sums, sums_got),
        [
            ((rows, lanes), BF16), ((rows, lanes), F32),
            ((rows + more, lanes), BF16), ((rows + more, lanes), F32),
        ],
    )


def stage_four_kernel(where_ref, first_kept, first_got, second_kept, second_got, sent0, sent1, kept):
    rows = first_kept.shape[0]
    unit = rows // 2
    low = where_ref[HIGH] % 2
    sums = added(second_kept, second_got, slice(rows, None))
    for which, (before, got) in enumerate(((first_kept, first_got), (second_kept, second_got))):

        @pl.when(low == which)
        def _():
            kept[:rows, :] = added(before, got, slice(0, rows))

        @pl.when(low != which)
        def _():
            sent0[...] = added(before, got, slice(0, unit)).astype(BF16)
            sent1[:unit, :] = added(before, got, slice(unit, rows)).astype(BF16)

    kept[rows:, :] = sums
    sent1[unit:, :] = sums.astype(BF16)


def stage_four_call(where, first_kept, first_got, second_kept, second_got):
    rows, lanes = first_kept.shape
    more = second_kept.shape[0] - rows
    return stage_call(
        stage_four_kernel, where, (first_kept, first_got, second_kept, second_got),
        [((rows // 2, lanes), BF16), ((rows // 2 + more, lanes), BF16), ((rows + more, lanes), F32)],
    )


def halve_rows_kernel(where_ref, before, got0, got1, sent, kept):
    unit = got0.shape[0]
    high = where_ref[HIGH] // 2
    for which, got in enumerate((got0, got1)):
        values = before[which * unit : (which + 1) * unit, :] + got[:unit, :].astype(F32)

        @pl.when(high == which)
        def _():
            kept[:unit, :] = values

        @pl.when(high != which)
        def _():
            sent[:unit, :] = values.astype(BF16)

    sums = before[2 * unit :, :] + got1[unit:, :].astype(F32)
    kept[unit:, :] = sums
    sent[unit:, :] = sums.astype(BF16)


def halve_rows_call(where, before, got0, got1):
    shape = got1.shape
    return stage_call(halve_rows_kernel, where, (before, got0, got1), [(shape, BF16), (shape, F32)])


def stage_five_kernel(where_ref, own, got, sent, mine, *, pairs):
    summed = own[...] + got[...].astype(F32)
    width = mine.shape[1]
    unit = own.shape[0] - 8
    group = width // 4
    blocks = ([], [])
    for part in range(4):
        starts = [(4 * pair + part) * LANES for pair in range(pairs)]
        columns = jnp.concatenate([summed[:unit, at : at + LANES] for at in starts], axis=1)
        blocks[0].append(columns[:, :group])
        blocks[1].append(columns[:, group:])
    for row in range(2):

        @pl.when(where_ref[ROW] == row)
        def _():
            mine[:unit, :] = jnp.concatenate(blocks[row], axis=1)
            sent[:unit, :] = jnp.concatenate(blocks[1 - row], axis=1).astype(BF16)

    mine[unit:, :] = summed[unit:, :width]
    sent[unit:, :] = summed[unit:, :width].astype(BF16)


def stage_five_call(where, own, got, pairs):
    rows, lanes = own.shape
    shape = (rows, lanes // pairs // LANES * HD * pairs)
    return stage_call(
        functools.partial(stage_five_kernel, pairs=pairs), where, (own, got), [(shape, BF16), (shape, F32)]
    )


def stage_six_kernel(where_ref, mine, other, down_got, *outs):
    weights, sums, down = outs[:4], outs[4:8], outs[8]
    unit = mine.shape[0] - 8
    group = weights[0].shape[1]
    row = where_ref[ROW]
    for ref, place in ((mine, row), (other, 1 - row)):
        span = pl.ds(pl.multiple_of(place * unit, unit), unit)
        for part, out in enumerate(weights):
            out[span, :] = ref[:unit, part * group : (part + 1) * group].astype(F32)
    summed = added(mine, other, slice(unit, None))
    for which, out in enumerate(sums):
        out[...] = summed[which : which + 1, :].reshape(out.shape)
    down[...] = down_got[...].astype(F32)


def stage_six_call(where, mine, other, down_got):
    rows, width = mine.shape
    unit, group = rows - 8, width // 4
    rows, lanes = down_got.shape
    return stage_call(
        stage_six_kernel, where, (mine, other, down_got),
        [((2 * unit, group), F32)] * 4 + [((width,), F32)] * 4 + [((rows, lanes), F32)],
    )


def tokens_grad_kernel(
    where_ref,
    keep_ref, recv_ref, back_ref, got0_ref, got1_ref, got2_ref, got3_ref, grad_res_ref, gain_ref,
    keep_out_ref, send_out_ref, sums_ref,
):
    step = pl.program_id(0)
    values = jnp.where(step == 0, recv_ref[...], keep_ref[...]).astype(F32)
    normal, inverse = normalize(values)
    back = back_ref[...] + by_step((got0_ref, got1_ref, got2_ref, got3_ref), step)
    gains = jnp.sum(back * normal, axis=0, keepdims=True)
    shifts = jnp.sum(back, axis=0, keepdims=True)
    grad = (grad_res_ref[...].astype(F32) + norm_back(back, row_vector(gain_ref), normal, inverse)).astype(BF16)

    add_sums(sums_ref, step, 0, gains, shifts)

    @pl.when(step == 0)
    def _():
        send_out_ref[...] = grad

    @pl.when(step == 1)
    def _():
        keep_out_ref[0] = grad


def tokens_grad_call(where, keep, recv, back, got, grad_res, gain):
    rows, width = keep.shape
    row = pl.BlockSpec((rows, width), lambda i, w: (1 - i, 0))
    return call(
        tokens_grad_kernel,
        (2,),
        [whole((rows, width))] * 2 + [row] + [whole((rows // 2, width))] * 4 + [row, whole((width,))],
        [
            pl.BlockSpec((1, rows, width), lambda i, w: (w[ROW], 0, 0)),
            whole((rows, width)),
            whole((8, width)),
        ],
        [((2, rows, width), BF16), ((rows, width), BF16), ((8, width), F32)],
        [],
        SMALL, mib=8,
    )(where, keep, recv, back, *got, grad_res, gain)


def local(
    tokens, gain_one, shift_one, w_query, w_key, w_value, w_out, gain_two, shift_two, w_up, w_down,
    cotangent, lengths,
):
    row_count, piece, width = tokens.shape
    n_dp = lax.axis_size("dp")
    n_seq = lax.axis_size("seq")
    count = n_dp // 4
    place = lax.axis_index("seq")
    core, row = place % 2, place // 2
    data = lax.axis_index("dp")
    high = data // count
    side = (data // (count // 2)) % 2
    total = n_seq * piece
    group = width // n_seq

    tok_recv = swap(pick(tokens, 1 - row), "seq", 2)
    tok_keep = pick(tokens, row)
    tok_keep_o = swap(tok_keep, "seq", 1)
    cot_keep = pick(cotangent, row)
    cot_recv = swap(pick(cotangent, 1 - row), "seq", 2)

    where = jnp.stack(
        [
            core, row, side, pick(lengths, row),
            2 * row + core, 2 * (1 - row) + core, 2 * row + 1 - core, 2 * (1 - row) + 1 - core,
            high,
        ]
    ).astype(jnp.int32)
    tables = tuple(jnp.asarray(table) for table in rotary_tables(total))
    out_blocks = w_out.reshape(n_seq, group, width)

    qkv, normed_t, w_qkv = project_call(
        0, where, tok_keep, tok_keep_o, gain_one, shift_one, (w_query, w_key, w_value), tables, ()
    )
    tok_recv, qkv, normed_t = together(tok_recv, qkv, normed_t)
    tok_recv_o = swap(tok_recv, "seq", 1)
    qkv, normed_t = project_call(
        1, where, tok_recv, tok_recv_o, gain_one, shift_one, (w_qkv,), tables, (qkv, normed_t)
    )
    ctx_m, ctx_o, ctx_t, lse = attend_call(where, qkv)
    cot_keep_o = swap(cot_keep, "seq", 1)
    ctx_m, ctx_o, ctx_t, cot_recv, cot_keep_o = together(ctx_m, ctx_o, ctx_t, cot_recv, cot_keep_o)
    cotangents = (cot_keep, cot_recv, cot_keep_o, swap(cot_recv, "seq", 1))
    ctx_got = swap(ctx_o, "seq", 1)
    residual, normed_two = residual_call(
        where, tok_keep, tok_recv, ctx_m, ctx_got, out_blocks, gain_two, shift_two
    )
    normed_two_o = swap(normed_two, "seq", 1)
    ctx_got_t = swap(ctx_t, "seq", 1)
    up_send0, up_send1, down_send0, down_later, down_keep0, active0, hidden0 = feed_call(
        False, where, normed_two, normed_two_o, cotangents, w_up, w_down
    )
    up_got0, up_got1 = swap(up_send0, "seq", 2), swap(up_send1, "seq", 2)
    down_got0 = swap(down_send0, "dp", count // 2)
    up_keep0, up_keep1, down_send1, down_keep1, active1, back_m, back_o = feed_call(
        True, where, normed_two, normed_two_o, cotangents, w_up, w_down, (hidden0, down_later)
    )
    back_o, up_got0, down_got0 = together(back_o, up_got0, down_got0)
    back_got = swap(back_o, "seq", 1)
    down_got1 = swap(down_send1, "dp", count // 2)
    grad_low, sums_two = middle_call(where, residual, back_m, back_got, cot_keep, cot_recv, gain_two)
    grad_low_o = swap(grad_low, "seq", 1)

    block_rows = width // n_dp

    pairs = qkv.shape[1] // (3 * LANES)

    def upper(up, down):
        bit = count // 4
        up = up.reshape(4, count // 2, block_rows, width).astype(F32)
        down = down.reshape(4, group, -1).astype(F32)
        while bit > 0:
            mine = (data // bit) % 2
            size, lanes = up.shape[1] // 2, down.shape[2] // 2
            sent = lax.dynamic_slice_in_dim(up, (1 - mine) * size, size, 1).astype(BF16)
            up = lax.dynamic_slice_in_dim(up, mine * size, size, 1) + swap(sent, "dp", bit)
            sent = lax.dynamic_slice_in_dim(down, (1 - mine) * lanes, lanes, 2).astype(BF16)
            down = lax.dynamic_slice_in_dim(down, mine * lanes, lanes, 2) + swap(sent, "dp", bit)
            bit //= 2
        up = up.reshape(4, block_rows, width)
        folds = width // down.shape[2]
        size = group // folds
        down = jnp.concatenate([down[:, k * size : (k + 1) * size] for k in range(folds)], axis=2)
        both = jnp.concatenate([up, down], axis=1).astype(BF16)
        both = both.reshape((2, 2) + both.shape[1:])
        return pick(both, 1 - high % 2, 1), pick(both, high % 2, 1)

    def halved(before, got):
        if count == 2:
            return halve_call(where, before, got)
        both = before.astype(F32) + got.astype(F32)
        return pick(both, 1 - high // 2).astype(BF16), pick(both, high // 2)

    def feed_sums(own, got):
        lanes = w_down.shape[0] // n_dp
        if count == 2:
            return feed_sum_call(where, own, got, lanes)
        own = own + got.astype(F32)
        up, down = own[:block_rows], own[block_rows:].astype(BF16)
        down = jnp.concatenate([down[:, k * lanes : (k + 1) * lanes] for k in range(width // lanes)])
        return up, down

    def exchanged(values):
        perm = []
        for d in range(n_dp):
            for s in range(n_seq):
                second_bit = (d // count) % 2
                to_d = d + (s % 2 - second_bit) * count
                to_s = s - s % 2 + second_bit
                perm.append((d * n_seq + s, to_d * n_seq + to_s))
        return lax.ppermute(values, ("dp", "seq"), perm)

    inner = count // 2
    attention = (where, qkv, ctx_t, ctx_got_t, grad_low, grad_low_o, w_out, lse, tables, normed_t, w_qkv)
    *first_pieces, early = attend_back_call(tuple(range(pairs - 1)), *attention)
    up_got1, down_got1, early = together(up_got1, down_got1, early)
    up_sent, up_kept, down_sent, down_kept = stage_one_call(
        where, up_keep0, up_keep1, up_got0, up_got1, down_keep0, down_keep1, down_got0, down_got1
    )
    up_sent, down_sent, early, first_pieces = together(up_sent, down_sent, early, first_pieces)
    up_got2 = swap(up_sent, "dp", inner)
    down_got2 = swap(down_sent, "seq", 2)
    first_got = (swap(first_pieces[0], "dp", inner), swap(first_pieces[2], "seq", 2))
    *pieces, normed_m, normed_o0, normed_o1, normed_o2, normed_o3 = attend_back_call(
        (pairs - 1,), *attention, early
    )
    normed_o = (normed_o0, normed_o1, normed_o2, normed_o3)
    pieces, normed_o, up_got2, down_got2 = together(pieces, normed_o, up_got2, down_got2)
    last_got = (swap(pieces[0], "dp", inner), swap(pieces[2], "seq", 2))
    normed_got = [swap(one, "seq", 1) for one in normed_o]
    if count == 2:
        feed_sent, feed_kept = stage_two_call(where, up_kept, up_got2, down_kept, down_got2)
    else:
        feed_sent, feed_kept = upper(
            up_kept.astype(F32) + up_got2.astype(F32), down_kept.astype(F32) + down_got2.astype(F32)
        )
    feed_sent, normed_m = together(feed_sent, normed_m)
    feed_got = swap(feed_sent, "dp", count)
    normed_m, first_got = together(normed_m, first_got)
    tok_buf, tok_send, sums_one = tokens_grad_call(
        where, tok_keep, tok_recv, normed_m, normed_got, grad_low, gain_one
    )

    sums = sums_one + sums_two
    sums_got = swap(sums, "seq", 1)
    if count == 2:
        last_got, tok_send, sums_got = together(last_got, tok_send, sums_got)
        sent_first, kept_first, sent_second, kept_second = stage_three_call(
            where,
            (first_pieces[1], first_got[0], pieces[1], last_got[0]),
            (first_pieces[3], first_got[1], pieces[3], last_got[1]),
            sums, sums_got,
        )
        sent_first, sent_second, tok_send, active1 = together(sent_first, sent_second, tok_send, active1)
        feed_got, active1 = together(feed_got, active1)
        got_first = swap(sent_first, "seq", 2)
        got_second = swap(sent_second, "dp", inner)
        feed_sent, feed_own = halved(feed_kept, feed_got)
        feed_got = swap(feed_sent, "dp", 2 * count)
        out_m, *out_o = feed_out_call(where, active0, active1, w_down)
        tok_back = swap(tok_send, "seq", 2)
        out_got = [swap(one, "seq", 1) for one in out_o]
        got_first, got_second, out_o, feed_sent = together(got_first, got_second, out_o, feed_sent)
        *sent, kept = stage_four_call(where, kept_first, got_first, kept_second, got_second)
        got = [swap(one, "dp", count) for one in sent]
        out_got, feed_got = together(out_got, feed_got)
        out_send, out_buf = output_call(where, residual, out_m, out_got)
        got, out_send = together(got, out_send)
        sent, kept = halve_rows_call(where, kept, *got)
        sent, out_send = together(sent, out_send)
        got = swap(sent, "dp", 2 * count)
        out_back = swap(out_send, "seq", 2)
        grad_up, grad_down = feed_sums(feed_own, feed_got)
        grad_down = exchanged(grad_down)
        got, tok_back, out_back = together(got, tok_back, out_back)
        sent, mine = stage_five_call(where, kept, got, pairs)
        other = swap(sent, "seq", 2)
        *ordered, sums0, sums1, sums2, sums3, grad_down = stage_six_call(where, mine, other, grad_down)
        sums, grad_down = (sums0, sums1, sums2, sums3), grad_down.T
    else:
        piece0, piece1, piece2, piece3 = (
            jnp.concatenate(two, axis=1) for two in zip(first_pieces, pieces)
        )
        shape = (2, 2, width // 16, -1)
        sides = jnp.stack([piece0, piece1]).reshape((2,) + shape)
        sides = jnp.stack([pick(sides, jnp.where(side == k, 1, 0)) for k in (0, 1)], 1)
        halves = jnp.stack([piece2, piece3]).reshape((2,) + shape)
        halves = jnp.stack([pick(halves, jnp.where(row == k, 1, 0)) for k in (0, 1)], 2)
        summed = jnp.stack([sides, halves], 1).reshape(width, pairs, 4, LANES).transpose(0, 2, 1, 3)
        summed = summed.reshape(width, 4, 2, group)
        other = swap(pick(summed, 1 - row, 2), "seq", 2).astype(F32)
        summed = (pick(summed, row, 2).astype(F32) + other).astype(BF16).reshape(width, -1)
        ordered = lax.psum_scatter(summed, "dp", scatter_dimension=0, tiled=True).astype(F32)
        tok_back = swap(tok_send, "seq", 2)
        out_m, *out_o = feed_out_call(where, active0, active1, w_down)
        out_got = [swap(one, "seq", 1) for one in out_o]
        out_send, out_buf = output_call(where, residual, out_m, out_got)
        out_back = swap(out_send, "seq", 2)
        feed_sent, feed_own = halved(feed_kept, feed_got)
        grad_up, grad_down = feed_sums(feed_own, swap(feed_sent, "dp", 2 * count))
        grad_down = exchanged(grad_down).astype(F32).T
        sums = sums + sums_got
        sums = sums + swap(sums, "seq", 2)
        bit = 1
        while bit < n_dp:
            sums = sums + swap(sums, "dp", bit)
            bit *= 2
        ordered = [ordered[:, k * group : (k + 1) * group] for k in range(4)]

    output = lax.dynamic_update_slice(out_buf, out_back[None], (1 - row, 0, 0))
    grad_tokens = lax.dynamic_update_slice(tok_buf, tok_back[None], (1 - row, 0, 0))
    return (
        output,
        grad_tokens,
        sums[0],
        sums[1],
        ordered[0],
        ordered[1],
        ordered[2],
        ordered[3],
        sums[2],
        sums[3],
        grad_up,
        grad_down,
    )


def solution(mesh):
    tokens = P("dp", "seq", None)
    weights = P("dp", "seq")
    return jax.shard_map(
        local,
        mesh=mesh,
        in_specs=(tokens,) + (P(),) * 10 + (tokens, P("dp")),
        out_specs=(tokens, tokens, P(), P(), weights, weights, weights, weights, P(), P(), weights, weights),
        check_vma=False,
    )
```

```python
import functools

import jax
import jax.numpy as jnp
import numpy as np
from jax import lax
from jax.experimental import pallas as pl
from jax.experimental.pallas import tpu as pltpu
from jax.sharding import PartitionSpec as P

HD = 64
EPSILON = 1e-05
MASKED = -1000000000.0
LANES = 128
BF16 = jnp.bfloat16
F32 = jnp.float32
CORE, ROW, SIDE, LENGTH, SPOT, HIGH = 0, 1, 2, 3, 4, 8


def swap(values, axis, bit):
    count = lax.axis_size(axis)
    return lax.ppermute(values, axis, [(i, i ^ bit) for i in range(count)])


def together(*values):
    return lax.optimization_barrier(values)


def pick(values, index, axis=0):
    return lax.dynamic_index_in_dim(values, index, axis, keepdims=False)


def dot(left, right):
    return jnp.dot(left, right, preferred_element_type=F32)


def dot_back(left, right):
    return lax.dot_general(left, right, (((1,), (1,)), ((), ())), preferred_element_type=F32)


def normalize(values):
    average = jnp.mean(values, axis=-1, keepdims=True)
    centred = values - average
    variance = jnp.mean(centred * centred, axis=-1, keepdims=True)
    inverse = lax.rsqrt(variance + EPSILON)
    return centred * inverse, inverse


def norm_back(grad, gain, normal, inverse):
    scaled = grad * gain
    first = jnp.mean(scaled, axis=-1, keepdims=True)
    second = jnp.mean(scaled * normal, axis=-1, keepdims=True)
    return (scaled - first - normal * second) * inverse


def row_vector(ref):
    return ref[...].reshape(1, ref.shape[0])


def swap_halves(values):
    lane = lax.broadcasted_iota(jnp.int32, values.shape, 1)
    up = pltpu.roll(values, LANES - HD // 2, 1)
    down = pltpu.roll(values, HD // 2, 1)
    return jnp.where(lane % HD < HD // 2, up, down)


def rotary_tables(length):
    lane = np.arange(LANES)
    frequency = 10000.0 ** (-2.0 * (lane % (HD // 2)) / HD)
    angles = np.arange(length)[:, None] * frequency[None, :]
    sign = np.where(lane % HD < HD // 2, -1.0, 1.0)
    return np.cos(angles).astype(np.float32), (sign * np.sin(angles)).astype(np.float32)


def kept_rows(where_ref, block, rows, lanes):
    spot = lax.broadcasted_iota(jnp.int32, (rows, lanes), 0) + where_ref[SPOT + block] * rows
    return spot < where_ref[LENGTH]


SMALL = pl.CostEstimate(flops=1, bytes_accessed=1, transcendentals=0)


def whole(shape):
    return pl.BlockSpec(shape, lambda *_: (0,) * len(shape))


def call(kernel, grid, in_specs, out_specs, out_shape, scratch, estimate, aliases=None, mib=16):
    return pl.pallas_call(
        kernel,
        grid_spec=pltpu.PrefetchScalarGridSpec(
            num_scalar_prefetch=1,
            grid=grid,
            in_specs=in_specs,
            out_specs=out_specs,
            scratch_shapes=scratch,
        ),
        out_shape=[jax.ShapeDtypeStruct(shape, kind) for shape, kind in out_shape],
        input_output_aliases=aliases or {},
        compiler_params=pltpu.CompilerParams(vmem_limit_bytes=mib * 1024 * 1024),
        cost_estimate=estimate,
    )


def pair_columns(ref, core, pair):
    group = ref.shape[1] // 4
    pieces = []
    start, end = pair * LANES, (pair + 1) * LANES
    if start < group:
        pieces.append(ref[:, core * group + start : core * group + min(end, group)])
    if end > group:
        begin = max(start, group)
        pieces.append(ref[:, (1 + core) * group + begin : (1 + core) * group + end])
    return pieces[0] if len(pieces) == 1 else jnp.concatenate(pieces, axis=1)


def project_kernel(where_ref, mine_ref, other_ref, gain_ref, shift_ref, *rest, first, pairs):
    step = pl.program_id(0)
    if first:
        wq_ref, wk_ref, wv_ref, cos_ref, sin_ref, qkv_ref, normed_t_ref, weight_ref = rest

        @pl.when(step == 0)
        def _():
            for core in range(2):

                @pl.when(where_ref[CORE] == core)
                def _():
                    for part, ref in enumerate((wq_ref, wk_ref, wv_ref)):
                        for pair in range(pairs):
                            start = (3 * pair + part) * LANES
                            weight_ref[:, start : start + LANES] = pair_columns(ref, core, pair)
    else:
        weight_ref, cos_ref, sin_ref, _, _, qkv_ref, normed_t_ref = rest
    values = jnp.where(step == 0, mine_ref[...], other_ref[...]).astype(F32)
    normal, _ = normalize(values)
    normed = (normal * row_vector(gain_ref) + row_vector(shift_ref)).astype(BF16)
    normed_t_ref[...] = normed.T
    cosine, sine = cos_ref[...], sin_ref[...]
    width = 3 * LANES
    for pair in range(pairs):
        out = dot(normed, weight_ref[:, pair * width : (pair + 1) * width])
        for part in range(3):
            piece = out[:, part * LANES : (part + 1) * LANES]
            if part < 2:
                piece = piece * cosine + swap_halves(piece) * sine
                if part == 0:
                    piece = piece * (HD ** (-0.5))
            start = pair * width + part * LANES
            qkv_ref[:, start : start + LANES] = piece.astype(BF16)


def project_call(turn, where, mine, other, gain, shift, weights, tables, previous):
    rows, width = mine.shape
    out_width = 3 * width // 2
    total = 4 * rows
    block = lambda i, w: (2 * i + turn, 0)
    table = pl.BlockSpec((rows, LANES), lambda i, w: (w[SPOT + 2 * i + turn], 0))
    in_specs = [whole((rows, width))] * 2 + [whole((width,))] * 2
    in_specs += [whole(weight.shape) for weight in weights] + [table, table]
    out_specs = [
        pl.BlockSpec((rows, out_width), block),
        pl.BlockSpec((width, rows), lambda i, w: (0, 2 * i + turn)),
    ]
    out_shape = [((total, out_width), BF16), ((width, total), BF16)]
    aliases = {}
    if previous:
        aliases = {1 + len(in_specs): 0, 2 + len(in_specs): 1}
        in_specs += [pl.BlockSpec(memory_space=pl.ANY)] * 2
    else:
        out_specs.append(whole((width, out_width)))
        out_shape.append(((width, out_width), BF16))
    return call(
        functools.partial(project_kernel, first=not previous, pairs=out_width // (3 * LANES)),
        (2,), in_specs, out_specs, out_shape, [],
        SMALL, aliases, 12,
    )(where, mine, other, gain, shift, *weights, *tables, *previous)


def mask_lane(lane, head, keys, bias):
    return jnp.where(lane == (HD if head == 0 else 0), bias, keys)


def only_head(lane, head, values):
    return jnp.where(lane // HD == head, values, jnp.zeros_like(values))


def with_one(lane, head, values):
    one = lane == (HD if head == 0 else 0)
    return jnp.where(one, jnp.ones_like(values), only_head(lane, head, values))


def fill_bias(where_ref, bias_ref):
    rows = bias_ref.shape[0] // 4
    for block in range(4):
        kept = kept_rows(where_ref, block, rows, LANES)
        bias_ref[block * rows : (block + 1) * rows, :] = jnp.where(kept, 0.0, MASKED).astype(BF16)


def attend_kernel(
    where_ref, query_ref, key_ref, value_ref, mine_ref, other_ref, ctx_t_ref, lse_ref, bias_ref, ctx_ref,
    *, tile,
):
    total = query_ref.shape[0]
    lane = lax.broadcasted_iota(jnp.int32, (1, LANES), 1)

    @pl.when(pl.program_id(0) == 0)
    def _():
        fill_bias(where_ref, bias_ref)

    keys = key_ref[...]
    values_t = value_ref[...].T
    for head in range(2):
        key_aug = mask_lane(lane, head, keys, bias_ref[...])
        for start in range(0, total, tile):
            queries = with_one(lane, head, query_ref[start : start + tile, :])
            scores = dot_back(key_aug, queries)
            highest = jnp.max(scores, axis=0, keepdims=True)
            weights = jnp.exp(scores - highest)
            sums = jnp.sum(weights, axis=0, keepdims=True)
            context = dot(values_t[head * HD : (head + 1) * HD, :], weights.astype(BF16))
            ctx_ref[head * HD : (head + 1) * HD, start : start + tile] = context / sums
            lse_ref[0, head : head + 1, start : start + tile] = highest + jnp.log(sums)
    ctx_t_ref[...] = ctx_ref[...].astype(BF16)
    contexts = ctx_ref[...].T.astype(BF16)
    mine_ref[...] = contexts[: total // 2]
    other_ref[...] = contexts[total // 2 :]


def attend_call(where, qkv):
    total, width = qkv.shape
    pairs = width // (3 * LANES)
    width //= 3
    half = total // 2
    column = lambda part: pl.BlockSpec((total, LANES), lambda p, w: (0, 3 * p + part))
    out_column = pl.BlockSpec((half, LANES), lambda p, w: (0, p))
    return call(
        functools.partial(attend_kernel, tile=total),
        (pairs,),
        [column(0), column(1), column(2)],
        [
            out_column, out_column,
            pl.BlockSpec((LANES, total), lambda p, w: (p, 0)),
            pl.BlockSpec((1, 8, total), lambda p, w: (p, 0, 0)),
        ],
        [((half, width), BF16), ((half, width), BF16), ((width, total), BF16), ((pairs, 8, total), F32)],
        [pltpu.VMEM((total, LANES), BF16), pltpu.VMEM((LANES, total), F32)],
        SMALL, mib=16,
    )(where, qkv, qkv, qkv)


def stack_rows(refs):
    return jnp.concatenate([ref[0] for ref in refs], axis=0)


def residual_kernel(
    where_ref, keep_ref, recv_ref, mine_ref, got_ref, w0_ref, w1_ref, w2_ref, w3_ref,
    gain_ref, shift_ref, res_ref, normed_ref,
):
    step = pl.program_id(0)
    values = jnp.where(step == 0, keep_ref[...], recv_ref[...]).astype(F32)
    attended = dot(mine_ref[...], stack_rows((w0_ref, w1_ref)))
    attended += dot(got_ref[...], stack_rows((w2_ref, w3_ref)))
    residual = values + attended
    res_ref[...] = residual
    normal, _ = normalize(residual)
    normed_ref[...] = (normal * row_vector(gain_ref) + row_vector(shift_ref)).astype(BF16)


def out_weight_specs(group, width):
    places = (
        lambda w: w[CORE],
        lambda w: 2 + w[CORE],
        lambda w: 1 - w[CORE],
        lambda w: 3 - w[CORE],
    )
    return [pl.BlockSpec((1, group, width), lambda i, w, at=at: (at(w), 0, 0)) for at in places]


def residual_call(where, keep, recv, ctx_mine, ctx_got, w_out, gain, shift):
    rows, width = keep.shape
    heads = ctx_mine.shape[1]
    row = lambda lanes: pl.BlockSpec((rows, lanes), lambda i, w: (i, 0))
    return call(
        residual_kernel,
        (2,),
        [whole((rows, width))] * 2 + [row(heads)] * 2
        + out_weight_specs(heads // 2, width) + [whole((width,))] * 2,
        [row(width)] * 2,
        [((2 * rows, width), F32), ((2 * rows, width), BF16)],
        [],
        SMALL, mib=10,
    )(where, keep, recv, ctx_mine, ctx_got, w_out, w_out, w_out, w_out, gain, shift)


def gelu_both(values):
    root = 0.7978845608028654
    bend = (root * 0.044715) * (values * values)
    half = 0.5 * jnp.tanh(values * (root + bend)) + 0.5
    steep = values * (2.0 * root + 6.0 * bend)
    return values * half, half * ((1.0 - half) * steep + 1.0)


def fill_cotangent(where_ref, refs, grad_ref):
    rows, width = refs[0].shape
    for place, ref in enumerate(refs):
        kept = kept_rows(where_ref, place, rows, width)
        grad_ref[place * rows : (place + 1) * rows, :] = jnp.where(kept, ref[...], jnp.zeros_like(ref))


def feed_kernel(
    where_ref,
    normed_m_ref, normed_o_ref, cot0_ref, cot1_ref, cot2_ref, cot3_ref, up_ref, down_ref,
    up_send_ref, up_keep_ref, send_ref, keep_ref, active_ref, back_m_ref, back_o_ref,
    normed_ref, grad_ref, normed_t_ref, grad_t_ref, hidden_ref, before_ref, up_before_ref,
):
    step = pl.program_id(0)
    half, width = normed_m_ref.shape
    block = up_ref.shape[1]

    @pl.when(step == 0)
    def _():
        normed_ref[:half, :] = normed_m_ref[...]
        normed_ref[half:, :] = normed_o_ref[...]
        fill_cotangent(where_ref, (cot0_ref, cot1_ref, cot2_ref, cot3_ref), grad_ref)
        normed_t_ref[...] = normed_ref[...].T
        grad_t_ref[...] = grad_ref[...].T

    hidden = dot(normed_ref[...], up_ref[...])
    active, slope = gelu_both(hidden)
    active_ref[...] = active.astype(BF16)
    grad_active = dot_back(grad_ref[...], down_ref[...])
    hidden_ref[...] = (grad_active * slope).astype(BF16)
    up_grad = dot(normed_t_ref[...], hidden_ref[...]).astype(BF16)
    down_grad = dot(grad_t_ref[...], active_ref[...]).astype(BF16)
    part = block // 2
    for side in range(2):
        piece = down_grad[:, side * part : (side + 1) * part]

        @pl.when(where_ref[SIDE] == side)
        def _():
            keep_ref[0] = piece

        @pl.when(where_ref[SIDE] != side)
        def _():
            send_ref[0] = piece

    @pl.when(step == 0)
    def _():
        up_send_ref[...] = up_grad
        before_ref[...] = hidden_ref[...]
        up_before_ref[...] = up_ref[...]

    @pl.when(step == 1)
    def _():
        up_keep_ref[...] = up_grad
        back = dot_back(before_ref[...], up_before_ref[...]) + dot_back(hidden_ref[...], up_ref[...])
        back_m_ref[...] = back[:half]
        back_o_ref[...] = back[half:].astype(BF16)


def feed_high(last, w):
    return jnp.where(last, w[ROW], 1 - w[ROW])


def feed_call(where, normed_m, normed_o, cotangents, w_up, w_down):
    half, width = normed_m.shape
    total = 2 * half
    block = w_up.shape[1] // 4
    part = block // 2
    token = whole((half, width))
    piece = pl.BlockSpec((1, width, part), lambda j, w: (j, 0, 0))
    return call(
        feed_kernel,
        (2,),
        [token, token]
        + [whole((half // 2, width))] * 4
        + [
            pl.BlockSpec((width, block), lambda j, w: (0, 2 * feed_high(j == 1, w) + w[CORE])),
            pl.BlockSpec((block, width), lambda j, w: (2 * feed_high(j == 1, w) + w[CORE], 0)),
        ],
        [
            whole((width, block)), whole((width, block)), piece, piece,
            pl.BlockSpec((total, block), lambda j, w: (0, j)),
            token, token,
        ],
        [
            ((width, block), BF16),
            ((width, block), BF16),
            ((2, width, part), BF16),
            ((2, width, part), BF16),
            ((total, 2 * block), BF16),
            ((half, width), F32),
            ((half, width), BF16),
        ],
        [
            pltpu.VMEM((total, width), BF16),
            pltpu.VMEM((total, width), BF16),
            pltpu.VMEM((width, total), BF16),
            pltpu.VMEM((width, total), BF16),
            pltpu.VMEM((total, block), BF16),
            pltpu.VMEM((total, block), BF16),
            pltpu.VMEM((width, block), BF16),
        ],
        SMALL, mib=28,
    )(where, normed_m, normed_o, *cotangents, w_up, w_down)


def feed_out_kernel(where_ref, active_ref, down0_ref, down1_ref, mine_ref, *other_refs):
    block = down0_ref.shape[0]
    out = dot(active_ref[:, :block], down0_ref[...]) + dot(active_ref[:, block:], down1_ref[...])
    size = other_refs[0].shape[0]

    @pl.when(pl.program_id(0) == 0)
    def _():
        for part, ref in enumerate(other_refs):
            ref[...] = out[part * size : (part + 1) * size].astype(BF16)

    @pl.when(pl.program_id(0) == 1)
    def _():
        mine_ref[...] = out


def feed_out_call(where, active, w_down):
    total, block = active.shape
    block //= 2
    width = w_down.shape[1]
    half = total // 2
    row = pl.BlockSpec((half, 2 * block), lambda i, w: (1 - i, 0))
    down = [
        pl.BlockSpec((block, width), lambda i, w, last=last: (2 * feed_high(last, w) + w[CORE], 0))
        for last in (False, True)
    ]
    return call(
        feed_out_kernel,
        (2,),
        [row, *down],
        [whole((half, width))] + [whole((half // 4, width))] * 4,
        [((half, width), F32)] + [((half // 4, width), BF16)] * 4,
        [], SMALL, mib=12,
    )(where, active, w_down, w_down)


def by_step(refs, step):
    low = jnp.concatenate([refs[0][...], refs[1][...]], axis=0)
    high = jnp.concatenate([refs[2][...], refs[3][...]], axis=0)
    return jnp.where(step == 0, high, low).astype(F32)


def output_kernel(where_ref, res_ref, out_ref, got0_ref, got1_ref, got2_ref, got3_ref, send_ref, keep_ref):
    step = pl.program_id(0)
    output = res_ref[...] + out_ref[...] + by_step((got0_ref, got1_ref, got2_ref, got3_ref), step)
    kept = kept_rows(where_ref, 1 - step, *output.shape)
    output = jnp.where(kept, output, jnp.zeros_like(output)).astype(BF16)

    @pl.when(step == 0)
    def _():
        send_ref[...] = output

    @pl.when(step == 1)
    def _():
        keep_ref[0] = output


def output_call(where, residual, out, got):
    half, width = residual.shape
    rows = half // 2
    row = pl.BlockSpec((rows, width), lambda i, w: (1 - i, 0))
    return call(
        output_kernel,
        (2,),
        [row] * 2 + [whole((rows // 2, width))] * 4,
        [whole((rows, width)), pl.BlockSpec((1, rows, width), lambda i, w: (w[ROW], 0, 0))],
        [((rows, width), BF16), ((2, rows, width), BF16)],
        [], SMALL, mib=8,
    )(where, residual, out, *got)


def add_sums(sums_ref, step, row, gains, shifts):
    @pl.when(step == 0)
    def _():
        sums_ref[...] = jnp.zeros_like(sums_ref)

    sums_ref[row : row + 1, :] += gains
    sums_ref[row + 1 : row + 2, :] += shifts


def middle_kernel(
    where_ref,
    res_ref, back_ref, back_got_ref, cot0_ref, cot1_ref, gain_ref, grad_low_ref, sums_ref,
):
    step = pl.program_id(0)
    residual = res_ref[...]
    kept = kept_rows(where_ref, step, *residual.shape)
    normal, inverse = normalize(residual)
    back = back_ref[...] + back_got_ref[...].astype(F32)
    gains = jnp.sum(back * normal, axis=0, keepdims=True)
    shifts = jnp.sum(back, axis=0, keepdims=True)

    add_sums(sums_ref, step, 2, gains, shifts)
    cotangent = jnp.where(step == 0, cot0_ref[...], cot1_ref[...]).astype(F32)
    cotangent = jnp.where(kept, cotangent, jnp.zeros_like(cotangent))
    grad = cotangent + norm_back(back, row_vector(gain_ref), normal, inverse)
    grad_low_ref[...] = grad.astype(BF16)


def middle_call(where, residual, back_m, back_got, cot_keep, cot_recv, gain):
    half, width = residual.shape
    rows = half // 2
    row = pl.BlockSpec((rows, width), lambda i, w: (i, 0))
    return call(
        middle_kernel,
        (2,),
        [row] * 3 + [whole((rows, width))] * 2 + [whole((width,))],
        [row, whole((8, width))],
        [((half, width), BF16), ((8, width), F32)],
        [], SMALL, mib=8,
    )(where, residual, back_m, back_got, cot_keep, cot_recv, gain)


def piece_order(where_ref):
    side, row = where_ref[SIDE], where_ref[ROW]
    order = []
    for kept in (0, 1):
        mine = side if kept else 1 - side
        order += [8 * high + 2 * mine + half for high in (0, 1) for half in (0, 1)]
    for kept in (0, 1):
        mine = row if kept else 1 - row
        order += [8 * high + 4 + 2 * one + mine for high in (0, 1) for one in (0, 1)]
    return order


def attend_back_kernel(
    where_ref,
    query_ref, key_ref, value_ref, ctx_ref, grad_m_ref, grad_o_ref, w0_ref, w1_ref, lse_ref,
    ctx_mine_hbm, ctx_got_hbm, cos_hbm, sin_hbm, normed_t_hbm, *rest,
    score_scale, first, last,
):
    if last:
        rest = rest[4:]
    out_refs, grads_ref = rest[:4], rest[4]
    rest = rest[5:]
    bias_ref, grad_ref, columns_ref, dqt_ref, dk_acc, dv_acc, qkv_ref, own_ref = rest[:8]
    ctx_mine_ref, ctx_got_ref, cos_ref, sin_ref, normed_t_ref, semaphores = rest[8:]
    step = pl.program_id(0)
    total = query_ref.shape[0]
    half = total // 2
    model = grad_m_ref.shape[1]
    lane = lax.broadcasted_iota(jnp.int32, (1, LANES), 1)
    unit = model // 16
    group = model // 4
    rows = total // 4
    late = [(ctx_mine_hbm, ctx_mine_ref), (ctx_got_hbm, ctx_got_ref), (normed_t_hbm, normed_t_ref)]
    for source, target in ((cos_hbm, cos_ref), (sin_hbm, sin_ref)):
        for block in range(4):
            begin = pl.multiple_of(where_ref[SPOT + block] * rows, rows)
            late.append((source.at[pl.ds(begin, rows)], target.at[pl.ds(block * rows, rows)]))

    def copies():
        return [
            pltpu.make_async_copy(source, target, semaphores.at[k])
            for k, (source, target) in enumerate(late)
        ]

    @pl.when(step == 0)
    def _():
        for copy in copies():
            copy.start()
        fill_bias(where_ref, bias_ref)
        grad_ref[:half, :] = grad_m_ref[...]
        grad_ref[half:, :] = grad_o_ref[...]

    for place, pair in enumerate(first):
        for core in range(2):

            @pl.when((step == place) & (where_ref[CORE] == core))
            def _():
                columns_ref[...] = pair_columns(grad_ref, core, pair)

    wout = jnp.concatenate([w0_ref[...], w1_ref[...]], axis=0)
    gctx = dot_back(grad_ref[...], wout).astype(BF16)
    products = gctx.astype(F32).T * ctx_ref[...].astype(F32)
    keys = key_ref[...]
    keys_t = keys.T
    values = value_ref[...]
    queries = query_ref[...]
    for head in range(2):
        key_aug = mask_lane(lane, head, keys, bias_ref[...])
        delta = jnp.sum(products[head * HD : (head + 1) * HD, :], axis=0, keepdims=True)
        scores = dot_back(key_aug, with_one(lane, head, queries))
        weights = jnp.exp(scores - lse_ref[0, head : head + 1, :])
        grads = only_head(lane, head, gctx)
        grad_weights = dot_back(values, grads)
        grad_scores = (weights * (grad_weights - delta)).astype(BF16)
        dv = dot(weights.astype(BF16), grads)
        dk = dot(grad_scores, only_head(lane, head, queries))
        dqt_ref[head * HD : (head + 1) * HD, :] = dot(
            keys_t[head * HD : (head + 1) * HD, :], grad_scores
        )
        if head == 0:
            dv_acc[...] = dv
            dk_acc[...] = dk
        else:
            dv_acc[...] += dv
            dk_acc[...] += dk

    @pl.when(step == 0)
    def _():
        for copy in copies():
            copy.wait()

    cosine, sine = cos_ref[...], sin_ref[...]
    dq = dqt_ref[...].T * score_scale
    dk = dk_acc[...]
    dq = (dq * cosine - swap_halves(dq) * sine).astype(BF16)
    dk = (dk * cosine - swap_halves(dk) * sine).astype(BF16)
    grads = jnp.concatenate([dq, dk, dv_acc[...].astype(BF16)], axis=1)
    qkv_ref[...] = dot(normed_t_ref[...], grads).astype(BF16)
    columns = columns_ref[...]
    turned = jnp.concatenate([columns[half:], columns[:half]], axis=0)
    own_ref[0] = dot(ctx_mine_ref[...], columns).astype(BF16)
    own_ref[1] = dot(ctx_got_ref[...], turned).astype(BF16)
    for place, source in enumerate(piece_order(where_ref)):
        ref = out_refs[place // 4]
        span = slice(place % 4 * unit, (place % 4 + 1) * unit)
        ref[span, : 3 * LANES] = qkv_ref[pl.ds(pl.multiple_of(source * unit, unit), unit), :]
        block = source // 4
        other = jnp.where(block % 2 == where_ref[CORE], 0, 1)
        inside = pl.multiple_of((block // 2) * group + (source % 4) * unit, unit)
        ref[span, 3 * LANES :] = own_ref[other, pl.ds(inside, unit), :]
    grads_ref[...] = grads


def normed_grad_kernel(where_ref, early_ref, late_ref, weight_ref, mine_ref, *other_refs):
    split = early_ref.shape[1]
    back = dot_back(early_ref[...], weight_ref[:, :split])
    back += dot_back(late_ref[...], weight_ref[:, split:])
    half = mine_ref.shape[0]
    size = half // len(other_refs)
    mine_ref[...] = back[:half]
    for part, ref in enumerate(other_refs):
        ref[...] = back[half + part * size : half + (part + 1) * size].astype(BF16)


def normed_grad_call(where, early, late, weight):
    half, width = early.shape[0] // 2, weight.shape[0]
    return stage_call(
        normed_grad_kernel, where, (early, late, weight),
        [((half, width), F32)] + [((half // 4, width), BF16)] * 4,
    )


def attend_back_call(
    pairs, where, qkv, ctx_t, ctx_got_t, grad_m, grad_o, w_out, lse, tables, normed_t,
    pieces=(),
):
    total, width = qkv.shape
    width //= 3
    half, model = grad_m.shape
    quarter = model // 4
    last = bool(pieces)
    begin = pairs[0]
    column = lambda part: pl.BlockSpec((total, LANES), lambda i, w: (0, 3 * (begin + i) + part))

    def head_rows(which):
        per = width // HD // 2

        def at(i, w):
            head = 2 * (begin + i) + which
            return (head // per * 2 * per + w[CORE] * per + head % per, 0)

        return pl.BlockSpec((HD, model), at)

    in_specs = [
        column(0), column(1), column(2),
        pl.BlockSpec((LANES, total), lambda i, w: (begin + i, 0)),
        whole((half, model)), whole((half, model)),
        head_rows(0), head_rows(1),
        pl.BlockSpec((1, 8, total), lambda i, w: (begin + i, 0, 0)),
    ]
    in_specs += [pl.BlockSpec(memory_space=pl.ANY)] * 5
    args = [
        qkv, qkv, qkv, ctx_t, grad_m, grad_o, w_out, w_out, lse, ctx_t, ctx_got_t, *tables, normed_t,
    ]
    out_specs = [pl.BlockSpec((quarter, 4 * LANES), lambda i, w: (0, begin + i))] * 4
    out_shape = [((quarter, 4 * width), BF16)] * 4
    aliases = {}
    if last:
        aliases = {1 + len(args) + k: k for k in range(4)}
        in_specs += [pl.BlockSpec(memory_space=pl.ANY)] * 4
        args += list(pieces)
    out_specs.append(pl.BlockSpec((total, 3 * LANES), lambda i, w: (0, i)))
    out_shape.append(((total, 3 * LANES * len(pairs)), BF16))
    return call(
        functools.partial(attend_back_kernel, score_scale=HD ** (-0.5), first=pairs, last=last),
        (len(pairs),), in_specs, out_specs, out_shape,
        [
            pltpu.VMEM((total, LANES), BF16),
            pltpu.VMEM((total, model), BF16),
            pltpu.VMEM((total, LANES), BF16),
            pltpu.VMEM((LANES, total), F32),
            pltpu.VMEM((total, LANES), F32),
            pltpu.VMEM((total, LANES), F32),
            pltpu.VMEM((model, 3 * LANES), BF16),
            pltpu.VMEM((2, width, LANES), BF16),
            pltpu.VMEM((width, total), BF16),
            pltpu.VMEM((width, total), BF16),
            pltpu.VMEM((total, LANES), F32),
            pltpu.VMEM((total, LANES), F32),
            pltpu.VMEM((model, total), BF16),
            pltpu.SemaphoreType.DMA((11,)),
        ],
        SMALL, aliases, mib=26,
    )(where, *args)


def stage_one_kernel(
    where_ref, up_keep, up_got, down_keep, down_got, up_sent, up_kept, down_sent, down_kept
):
    side, row = where_ref[SIDE], where_ref[ROW]
    unit = up_keep.shape[0] // 8
    for one in range(4):
        to = slice(one * unit, (one + 1) * unit)
        for out, mine in ((up_sent, 1 - side), (up_kept, side)):
            span = pl.ds(pl.multiple_of((2 * one + mine) * unit, unit), unit)
            out[to, :] = added(up_keep, up_got, span).astype(BF16)
    size = down_keep.shape[1] // 2
    for place, block in enumerate((1 - row, row)):
        for out, mine in ((down_sent, 1 - row), (down_kept, row)):
            span = pl.ds(pl.multiple_of(mine * size, size), size)
            out[block] = added(down_keep.at[place], down_got.at[place], span).astype(BF16)


def stage_one_call(where, up_keep, up_got, down_keep, down_got):
    rows, width = up_keep.shape
    _, size, lanes = down_keep.shape
    return stage_call(
        stage_one_kernel, where, (up_keep, up_got, down_keep, down_got),
        [((rows // 2, width), BF16)] * 2 + [((2, size // 2, lanes), BF16)] * 2,
    )


def added(one, two, span):
    return one[span, :].astype(F32) + two[span, :].astype(F32)


def stage_two_kernel(where_ref, up_kept, up_got, down_kept, down_got, sent, kept):
    unit = kept.shape[1] // 2
    size, lanes = down_kept.shape[1] // 2, down_kept.shape[2]
    low = where_ref[HIGH] % 2
    for high in range(2):
        for out, which in ((sent, 1 - low), (kept, low)):
            span = pl.ds(pl.multiple_of((2 * high + which) * unit, unit), unit)
            out[high, :unit, :] = added(up_kept, up_got, span).astype(BF16)
            for fold in range(size // unit):
                span = pl.ds(pl.multiple_of(which * size + fold * unit, unit), unit)
                values = added(down_kept.at[high], down_got.at[high], span)
                out[high, unit:, fold * lanes : (fold + 1) * lanes] = values.astype(BF16)


def halve_kernel(where_ref, before, got, sent, kept):
    high = where_ref[HIGH] // 2
    for out, which in ((sent, 1 - high), (kept, high)):
        out[...] = (before[which].astype(F32) + got[which].astype(F32)).astype(out.dtype)


def halve_call(where, before, got):
    shape = before.shape[1:]
    return stage_call(halve_kernel, where, (before, got), [(shape, BF16), (shape, F32)])


def stage_call(kernel, where, inputs, out_shape, mib=8):
    return call(
        kernel, (1,), [whole(one.shape) for one in inputs], [whole(shape) for shape, _ in out_shape],
        out_shape, [], SMALL, mib=mib,
    )(where, *inputs)


def stage_two_call(where, up_kept, up_got, down_kept, down_got):
    rows, width = up_kept.shape
    part = (2, rows // 2, width)
    return stage_call(
        stage_two_kernel, where, (up_kept, up_got, down_kept, down_got), [(part, BF16)] * 2
    )


def feed_sum_kernel(where_ref, own, got, up, down):
    unit, lanes = up.shape[0], down.shape[1]
    summed = own[...] + got[...].astype(F32)
    up[...] = summed[:unit]
    for fold in range(up.shape[1] // lanes):
        values = summed[unit:, fold * lanes : (fold + 1) * lanes]
        down[fold * unit : (fold + 1) * unit, :] = values.astype(BF16)


def feed_sum_call(where, own, got, lanes):
    rows, width = own.shape
    unit = rows // 2
    return stage_call(
        feed_sum_kernel, where, (own, got), [((unit, width), F32), ((unit * width // lanes, lanes), BF16)]
    )


def stage_three_kernel(where_ref, *refs):
    first_keep, first_got, second_keep, second_got, sums, sums_got = refs[:6]
    first_sent, first_kept, second_sent, second_kept = refs[6:]
    side, row = where_ref[SIDE], where_ref[ROW]
    unit = first_sent.shape[0] // 2
    for keep, got, mine, sent, kept in (
        (first_keep, first_got, row, first_sent, first_kept),
        (second_keep, second_got, side, second_sent, second_kept),
    ):
        for high in range(2):
            to = slice(high * unit, (high + 1) * unit)
            for out, which in ((sent, 1 - mine), (kept, mine)):
                span = pl.ds(pl.multiple_of((2 * high + which) * unit, unit), unit)
                out[to, :] = added(keep, got, span).astype(out.dtype)
    summed = sums[...] + sums_got[...]
    width = summed.shape[1]
    for out in (second_sent, second_kept):
        out[2 * unit :, :] = jnp.zeros_like(out[2 * unit :, :])
        out[2 * unit :, :width] = summed.astype(out.dtype)


def stage_three_call(where, first_keep, first_got, second_keep, second_got, sums, sums_got):
    rows, lanes = first_keep.shape[0] // 2, first_keep.shape[1]
    more = sums.shape[0]
    return stage_call(
        stage_three_kernel, where, (first_keep, first_got, second_keep, second_got, sums, sums_got),
        [
            ((rows, lanes), BF16), ((rows, lanes), F32),
            ((rows + more, lanes), BF16), ((rows + more, lanes), F32),
        ],
    )


def stage_four_kernel(where_ref, first_kept, first_got, second_kept, second_got, sent0, sent1, kept):
    rows = first_kept.shape[0]
    unit = rows // 2
    low = where_ref[HIGH] % 2
    sums = added(second_kept, second_got, slice(rows, None))
    for which, (before, got) in enumerate(((first_kept, first_got), (second_kept, second_got))):

        @pl.when(low == which)
        def _():
            kept[:rows, :] = added(before, got, slice(0, rows))

        @pl.when(low != which)
        def _():
            sent0[...] = added(before, got, slice(0, unit)).astype(BF16)
            sent1[:unit, :] = added(before, got, slice(unit, rows)).astype(BF16)

    kept[rows:, :] = sums
    sent1[unit:, :] = sums.astype(BF16)


def stage_four_call(where, first_kept, first_got, second_kept, second_got):
    rows, lanes = first_kept.shape
    more = second_kept.shape[0] - rows
    return stage_call(
        stage_four_kernel, where, (first_kept, first_got, second_kept, second_got),
        [((rows // 2, lanes), BF16), ((rows // 2 + more, lanes), BF16), ((rows + more, lanes), F32)],
    )


def halve_rows_kernel(where_ref, before, got0, got1, sent, kept):
    unit = got0.shape[0]
    high = where_ref[HIGH] // 2
    for which, got in enumerate((got0, got1)):
        values = before[which * unit : (which + 1) * unit, :] + got[:unit, :].astype(F32)

        @pl.when(high == which)
        def _():
            kept[:unit, :] = values

        @pl.when(high != which)
        def _():
            sent[:unit, :] = values.astype(BF16)

    sums = before[2 * unit :, :] + got1[unit:, :].astype(F32)
    kept[unit:, :] = sums
    sent[unit:, :] = sums.astype(BF16)


def halve_rows_call(where, before, got0, got1):
    shape = got1.shape
    return stage_call(halve_rows_kernel, where, (before, got0, got1), [(shape, BF16), (shape, F32)])


def stage_five_kernel(where_ref, own, got, sent, mine, *, pairs):
    summed = own[...] + got[...].astype(F32)
    width = mine.shape[1]
    unit = own.shape[0] - 8
    group = width // 4
    blocks = ([], [])
    for part in range(4):
        starts = [(4 * pair + part) * LANES for pair in range(pairs)]
        columns = jnp.concatenate([summed[:unit, at : at + LANES] for at in starts], axis=1)
        blocks[0].append(columns[:, :group])
        blocks[1].append(columns[:, group:])
    for row in range(2):

        @pl.when(where_ref[ROW] == row)
        def _():
            mine[:unit, :] = jnp.concatenate(blocks[row], axis=1)
            sent[:unit, :] = jnp.concatenate(blocks[1 - row], axis=1).astype(BF16)

    mine[unit:, :] = summed[unit:, :width]
    sent[unit:, :] = summed[unit:, :width].astype(BF16)


def stage_five_call(where, own, got, pairs):
    rows, lanes = own.shape
    shape = (rows, lanes // pairs // LANES * HD * pairs)
    return stage_call(
        functools.partial(stage_five_kernel, pairs=pairs), where, (own, got), [(shape, BF16), (shape, F32)]
    )


def stage_six_kernel(where_ref, mine, other, down_got, *outs):
    weights, sums, down = outs[:4], outs[4:8], outs[8]
    unit = mine.shape[0] - 8
    group = weights[0].shape[1]
    row = where_ref[ROW]
    for ref, place in ((mine, row), (other, 1 - row)):
        span = pl.ds(pl.multiple_of(place * unit, unit), unit)
        for part, out in enumerate(weights):
            out[span, :] = ref[:unit, part * group : (part + 1) * group].astype(F32)
    summed = added(mine, other, slice(unit, None))
    for which, out in enumerate(sums):
        out[...] = summed[which : which + 1, :].reshape(out.shape)
    down[...] = down_got[...].astype(F32)


def stage_six_call(where, mine, other, down_got):
    rows, width = mine.shape
    unit, group = rows - 8, width // 4
    rows, lanes = down_got.shape
    return stage_call(
        stage_six_kernel, where, (mine, other, down_got),
        [((2 * unit, group), F32)] * 4 + [((width,), F32)] * 4 + [((rows, lanes), F32)],
    )


def tokens_grad_kernel(
    where_ref,
    keep_ref, recv_ref, back_ref, got0_ref, got1_ref, got2_ref, got3_ref, grad_res_ref, gain_ref,
    keep_out_ref, send_out_ref, sums_ref,
):
    step = pl.program_id(0)
    values = jnp.where(step == 0, recv_ref[...], keep_ref[...]).astype(F32)
    normal, inverse = normalize(values)
    back = back_ref[...] + by_step((got0_ref, got1_ref, got2_ref, got3_ref), step)
    gains = jnp.sum(back * normal, axis=0, keepdims=True)
    shifts = jnp.sum(back, axis=0, keepdims=True)
    grad = (grad_res_ref[...].astype(F32) + norm_back(back, row_vector(gain_ref), normal, inverse)).astype(BF16)

    add_sums(sums_ref, step, 0, gains, shifts)

    @pl.when(step == 0)
    def _():
        send_out_ref[...] = grad

    @pl.when(step == 1)
    def _():
        keep_out_ref[0] = grad


def tokens_grad_call(where, keep, recv, back, got, grad_res, gain):
    rows, width = keep.shape
    row = pl.BlockSpec((rows, width), lambda i, w: (1 - i, 0))
    return call(
        tokens_grad_kernel,
        (2,),
        [whole((rows, width))] * 2 + [row] + [whole((rows // 2, width))] * 4 + [row, whole((width,))],
        [
            pl.BlockSpec((1, rows, width), lambda i, w: (w[ROW], 0, 0)),
            whole((rows, width)),
            whole((8, width)),
        ],
        [((2, rows, width), BF16), ((rows, width), BF16), ((8, width), F32)],
        [],
        SMALL, mib=8,
    )(where, keep, recv, back, *got, grad_res, gain)


def local(
    tokens, gain_one, shift_one, w_query, w_key, w_value, w_out, gain_two, shift_two, w_up, w_down,
    cotangent, lengths,
):
    row_count, piece, width = tokens.shape
    n_dp = lax.axis_size("dp")
    n_seq = lax.axis_size("seq")
    count = n_dp // 4
    place = lax.axis_index("seq")
    core, row = place % 2, place // 2
    data = lax.axis_index("dp")
    high = data // count
    side = (data // (count // 2)) % 2
    total = n_seq * piece
    group = width // n_seq

    tok_send, tokens = together(pick(tokens, 1 - row), tokens)
    tok_recv = swap(tok_send, "seq", 2)
    tok_keep = pick(tokens, row)
    tok_keep_o = swap(tok_keep, "seq", 1)
    cot_keep = pick(cotangent, row)
    cot_recv = swap(pick(cotangent, 1 - row), "seq", 2)

    where = jnp.stack(
        [
            core, row, side, pick(lengths, row),
            2 * row + core, 2 * (1 - row) + core, 2 * row + 1 - core, 2 * (1 - row) + 1 - core,
            high,
        ]
    ).astype(jnp.int32)
    tables = tuple(jnp.asarray(table) for table in rotary_tables(total))
    out_blocks = w_out.reshape(n_seq, group, width)

    qkv, normed_t, w_qkv = project_call(
        0, where, tok_keep, tok_keep_o, gain_one, shift_one, (w_query, w_key, w_value), tables, ()
    )
    tok_recv, qkv, normed_t = together(tok_recv, qkv, normed_t)
    tok_recv_o = swap(tok_recv, "seq", 1)
    qkv, normed_t = project_call(
        1, where, tok_recv, tok_recv_o, gain_one, shift_one, (w_qkv,), tables, (qkv, normed_t)
    )
    ctx_m, ctx_o, ctx_t, lse = attend_call(where, qkv)
    cot_keep_o = swap(cot_keep, "seq", 1)
    ctx_m, ctx_o, ctx_t, cot_recv, cot_keep_o = together(ctx_m, ctx_o, ctx_t, cot_recv, cot_keep_o)
    cotangents = (cot_keep, cot_recv, cot_keep_o, swap(cot_recv, "seq", 1))
    ctx_got = swap(ctx_o, "seq", 1)
    residual, normed_two = residual_call(
        where, tok_keep, tok_recv, ctx_m, ctx_got, out_blocks, gain_two, shift_two
    )
    normed_two_o = swap(normed_two, "seq", 1)
    ctx_got_t = swap(ctx_t, "seq", 1)
    up_send, up_keep, down_send, down_keep, active, back_m, back_o = feed_call(
        where, normed_two, normed_two_o, cotangents, w_up, w_down
    )
    up_got = swap(up_send, "seq", 2)
    down_got = swap(down_send, "dp", count // 2)
    back_got = swap(back_o, "seq", 1)
    grad_low, sums_two = middle_call(where, residual, back_m, back_got, cot_keep, cot_recv, gain_two)
    grad_low_o = swap(grad_low, "seq", 1)

    block_rows = width // n_dp

    pairs = qkv.shape[1] // (3 * LANES)

    def upper(up, down):
        bit = count // 4
        up = up.reshape(4, count // 2, block_rows, width).astype(F32)
        down = down.reshape(4, group, -1).astype(F32)
        while bit > 0:
            mine = (data // bit) % 2
            size, lanes = up.shape[1] // 2, down.shape[2] // 2
            sent = lax.dynamic_slice_in_dim(up, (1 - mine) * size, size, 1).astype(BF16)
            up = lax.dynamic_slice_in_dim(up, mine * size, size, 1) + swap(sent, "dp", bit)
            sent = lax.dynamic_slice_in_dim(down, (1 - mine) * lanes, lanes, 2).astype(BF16)
            down = lax.dynamic_slice_in_dim(down, mine * lanes, lanes, 2) + swap(sent, "dp", bit)
            bit //= 2
        up = up.reshape(4, block_rows, width)
        folds = width // down.shape[2]
        size = group // folds
        down = jnp.concatenate([down[:, k * size : (k + 1) * size] for k in range(folds)], axis=2)
        both = jnp.concatenate([up, down], axis=1).astype(BF16)
        both = both.reshape((2, 2) + both.shape[1:])
        return pick(both, 1 - high % 2, 1), pick(both, high % 2, 1)

    def halved(before, got):
        if count == 2:
            return halve_call(where, before, got)
        both = before.astype(F32) + got.astype(F32)
        return pick(both, 1 - high // 2).astype(BF16), pick(both, high // 2)

    def feed_sums(own, got):
        lanes = w_down.shape[0] // n_dp
        if count == 2:
            return feed_sum_call(where, own, got, lanes)
        own = own + got.astype(F32)
        up, down = own[:block_rows], own[block_rows:].astype(BF16)
        down = jnp.concatenate([down[:, k * lanes : (k + 1) * lanes] for k in range(width // lanes)])
        return up, down

    def exchanged(values):
        perm = []
        for d in range(n_dp):
            for s in range(n_seq):
                second_bit = (d // count) % 2
                to_d = d + (s % 2 - second_bit) * count
                to_s = s - s % 2 + second_bit
                perm.append((d * n_seq + s, to_d * n_seq + to_s))
        return lax.ppermute(values, ("dp", "seq"), perm)

    inner = count // 2
    attention = (where, qkv, ctx_t, ctx_got_t, grad_low, grad_low_o, w_out, lse, tables, normed_t)
    *first_pieces, early = attend_back_call(tuple(range(pairs - 1)), *attention)
    active, early = together(active, early)
    out_m, *out_o = feed_out_call(where, active, w_down)
    up_got, down_got, early, out_o = together(up_got, down_got, early, out_o)
    up_sent, up_kept, down_sent, down_kept = stage_one_call(where, up_keep, up_got, down_keep, down_got)
    up_sent, down_sent, early = together(up_sent, down_sent, early)
    up_got2 = swap(up_sent, "dp", inner)
    down_got2 = swap(down_sent, "seq", 2)
    *pieces, late = attend_back_call((pairs - 1,), *attention, first_pieces)
    pieces, late = together(pieces, late)
    last_got = (swap(pieces[0], "dp", inner), swap(pieces[2], "seq", 2))
    normed_m, *normed_o = normed_grad_call(where, early, late, w_qkv)
    normed_o, up_got2, down_got2 = together(normed_o, up_got2, down_got2)
    normed_got = [swap(one, "seq", 1) for one in normed_o]
    if count == 2:
        feed_sent, feed_kept = stage_two_call(where, up_kept, up_got2, down_kept, down_got2)
    else:
        feed_sent, feed_kept = upper(
            up_kept.astype(F32) + up_got2.astype(F32), down_kept.astype(F32) + down_got2.astype(F32)
        )
    feed_sent, normed_m = together(feed_sent, normed_m)
    feed_got = swap(feed_sent, "dp", count)
    tok_buf, tok_send, sums_one = tokens_grad_call(
        where, tok_keep, tok_recv, normed_m, normed_got, grad_low, gain_one
    )

    sums = sums_one + sums_two
    sums_got = swap(sums, "seq", 1)
    if count == 2:
        last_got, tok_send, sums_got = together(last_got, tok_send, sums_got)
        sent_first, kept_first, sent_second, kept_second = stage_three_call(
            where, pieces[1], last_got[0], pieces[3], last_got[1], sums, sums_got
        )
        sent_first, sent_second, tok_send = together(sent_first, sent_second, tok_send)
        got_first = swap(sent_first, "seq", 2)
        got_second = swap(sent_second, "dp", inner)
        feed_sent, feed_own = halved(feed_kept, feed_got)
        feed_got = swap(feed_sent, "dp", 2 * count)
        tok_back = swap(tok_send, "seq", 2)
        out_got = [swap(one, "seq", 1) for one in out_o]
        got_first, got_second, feed_sent = together(got_first, got_second, feed_sent)
        *sent, kept = stage_four_call(where, kept_first, got_first, kept_second, got_second)
        got = [swap(one, "dp", count) for one in sent]
        out_got, feed_got = together(out_got, feed_got)
        out_send, out_buf = output_call(where, residual, out_m, out_got)
        got, out_send = together(got, out_send)
        sent, kept = halve_rows_call(where, kept, *got)
        sent, out_send = together(sent, out_send)
        got = swap(sent, "dp", 2 * count)
        out_back = swap(out_send, "seq", 2)
        grad_up, grad_down = feed_sums(feed_own, feed_got)
        grad_down = exchanged(grad_down)
        got, tok_back, out_back = together(got, tok_back, out_back)
        sent, mine = stage_five_call(where, kept, got, pairs)
        other = swap(sent, "seq", 2)
        *ordered, sums0, sums1, sums2, sums3, grad_down = stage_six_call(where, mine, other, grad_down)
        sums, grad_down = (sums0, sums1, sums2, sums3), grad_down.T
    else:
        piece0, piece1, piece2, piece3 = pieces
        shape = (2, 2, width // 16, -1)
        sides = jnp.stack([piece0, piece1]).reshape((2,) + shape)
        sides = jnp.stack([pick(sides, jnp.where(side == k, 1, 0)) for k in (0, 1)], 1)
        halves = jnp.stack([piece2, piece3]).reshape((2,) + shape)
        halves = jnp.stack([pick(halves, jnp.where(row == k, 1, 0)) for k in (0, 1)], 2)
        summed = jnp.stack([sides, halves], 1).reshape(width, pairs, 4, LANES).transpose(0, 2, 1, 3)
        summed = summed.reshape(width, 4, 2, group)
        other = swap(pick(summed, 1 - row, 2), "seq", 2).astype(F32)
        summed = (pick(summed, row, 2).astype(F32) + other).astype(BF16).reshape(width, -1)
        ordered = lax.psum_scatter(summed, "dp", scatter_dimension=0, tiled=True).astype(F32)
        tok_back = swap(tok_send, "seq", 2)
        out_got = [swap(one, "seq", 1) for one in out_o]
        out_send, out_buf = output_call(where, residual, out_m, out_got)
        out_back = swap(out_send, "seq", 2)
        feed_sent, feed_own = halved(feed_kept, feed_got)
        grad_up, grad_down = feed_sums(feed_own, swap(feed_sent, "dp", 2 * count))
        grad_down = exchanged(grad_down).astype(F32).T
        sums = sums + sums_got
        sums = sums + swap(sums, "seq", 2)
        bit = 1
        while bit < n_dp:
            sums = sums + swap(sums, "dp", bit)
            bit *= 2
        ordered = [ordered[:, k * group : (k + 1) * group] for k in range(4)]

    output = lax.dynamic_update_slice(out_buf, out_back[None], (1 - row, 0, 0))
    grad_tokens = lax.dynamic_update_slice(tok_buf, tok_back[None], (1 - row, 0, 0))
    return (
        output,
        grad_tokens,
        sums[0],
        sums[1],
        ordered[0],
        ordered[1],
        ordered[2],
        ordered[3],
        sums[2],
        sums[3],
        grad_up,
        grad_down,
    )


def solution(mesh):
    tokens = P("dp", "seq", None)
    weights = P("dp", "seq")
    return jax.shard_map(
        local,
        mesh=mesh,
        in_specs=(tokens,) + (P(),) * 10 + (tokens, P("dp")),
        out_specs=(tokens, tokens, P(), P(), weights, weights, weights, weights, P(), P(), weights, weights),
        check_vma=False,
    )
```

```python
import functools

import jax
import jax.numpy as jnp
import numpy as np
from jax import lax
from jax.experimental import pallas as pl
from jax.experimental.pallas import tpu as pltpu
from jax.sharding import PartitionSpec as P

HD = 64
EPSILON = 1e-05
MASKED = -1000000000.0
LANES = 128
BF16 = jnp.bfloat16
F32 = jnp.float32
CORE, ROW, SIDE, LENGTH, SPOT, HIGH = 0, 1, 2, 3, 4, 8


def swap(values, axis, bit):
    count = lax.axis_size(axis)
    return lax.ppermute(values, axis, [(i, i ^ bit) for i in range(count)])


def together(*values):
    return lax.optimization_barrier(values)


def pick(values, index, axis=0):
    return lax.dynamic_index_in_dim(values, index, axis, keepdims=False)


def dot(left, right):
    return jnp.dot(left, right, preferred_element_type=F32)


def dot_back(left, right):
    return lax.dot_general(left, right, (((1,), (1,)), ((), ())), preferred_element_type=F32)


def normalize(values):
    average = jnp.mean(values, axis=-1, keepdims=True)
    centred = values - average
    variance = jnp.mean(centred * centred, axis=-1, keepdims=True)
    inverse = lax.rsqrt(variance + EPSILON)
    return centred * inverse, inverse


def norm_back(grad, gain, normal, inverse):
    scaled = grad * gain
    first = jnp.mean(scaled, axis=-1, keepdims=True)
    second = jnp.mean(scaled * normal, axis=-1, keepdims=True)
    return (scaled - first - normal * second) * inverse


def row_vector(ref):
    return ref[...].reshape(1, ref.shape[0])


def swap_halves(values):
    lane = lax.broadcasted_iota(jnp.int32, values.shape, 1)
    up = pltpu.roll(values, LANES - HD // 2, 1)
    down = pltpu.roll(values, HD // 2, 1)
    return jnp.where(lane % HD < HD // 2, up, down)


def rotary_tables(length):
    lane = np.arange(LANES)
    frequency = 10000.0 ** (-2.0 * (lane % (HD // 2)) / HD)
    angles = np.arange(length)[:, None] * frequency[None, :]
    sign = np.where(lane % HD < HD // 2, -1.0, 1.0)
    return np.cos(angles).astype(np.float32), (sign * np.sin(angles)).astype(np.float32)


def kept_rows(where_ref, block, rows, lanes):
    spot = lax.broadcasted_iota(jnp.int32, (rows, lanes), 0) + where_ref[SPOT + block] * rows
    return spot < where_ref[LENGTH]


SMALL = pl.CostEstimate(flops=1, bytes_accessed=1, transcendentals=0)


def whole(shape):
    return pl.BlockSpec(shape, lambda *_: (0,) * len(shape))


def call(kernel, grid, in_specs, out_specs, out_shape, scratch, estimate, aliases=None, mib=16):
    return pl.pallas_call(
        kernel,
        grid_spec=pltpu.PrefetchScalarGridSpec(
            num_scalar_prefetch=1,
            grid=grid,
            in_specs=in_specs,
            out_specs=out_specs,
            scratch_shapes=scratch,
        ),
        out_shape=[jax.ShapeDtypeStruct(shape, kind) for shape, kind in out_shape],
        input_output_aliases=aliases or {},
        compiler_params=pltpu.CompilerParams(vmem_limit_bytes=mib * 1024 * 1024),
        cost_estimate=estimate,
    )


def pair_columns(ref, core, pair):
    group = ref.shape[1] // 4
    pieces = []
    start, end = pair * LANES, (pair + 1) * LANES
    if start < group:
        pieces.append(ref[:, core * group + start : core * group + min(end, group)])
    if end > group:
        begin = max(start, group)
        pieces.append(ref[:, (1 + core) * group + begin : (1 + core) * group + end])
    return pieces[0] if len(pieces) == 1 else jnp.concatenate(pieces, axis=1)


def project_kernel(where_ref, mine_ref, other_ref, gain_ref, shift_ref, *rest, first, pairs):
    step = pl.program_id(0)
    if first:
        wq_ref, wk_ref, wv_ref, cos_ref, sin_ref, qkv_ref, normed_t_ref, weight_ref = rest

        @pl.when(step == 0)
        def _():
            for core in range(2):

                @pl.when(where_ref[CORE] == core)
                def _():
                    for part, ref in enumerate((wq_ref, wk_ref, wv_ref)):
                        for pair in range(pairs):
                            start = (3 * pair + part) * LANES
                            weight_ref[:, start : start + LANES] = pair_columns(ref, core, pair)
    else:
        weight_ref, cos_ref, sin_ref, _, _, qkv_ref, normed_t_ref = rest
    values = jnp.where(step == 0, mine_ref[...], other_ref[...]).astype(F32)
    normal, _ = normalize(values)
    normed = (normal * row_vector(gain_ref) + row_vector(shift_ref)).astype(BF16)
    normed_t_ref[...] = normed.T
    cosine, sine = cos_ref[...], sin_ref[...]
    width = 3 * LANES
    for pair in range(pairs):
        out = dot(normed, weight_ref[:, pair * width : (pair + 1) * width])
        for part in range(3):
            piece = out[:, part * LANES : (part + 1) * LANES]
            if part < 2:
                piece = piece * cosine + swap_halves(piece) * sine
                if part == 0:
                    piece = piece * (HD ** (-0.5))
            start = pair * width + part * LANES
            qkv_ref[:, start : start + LANES] = piece.astype(BF16)


def project_call(turn, where, mine, other, gain, shift, weights, tables, previous):
    rows, width = mine.shape
    out_width = 3 * width // 2
    total = 4 * rows
    block = lambda i, w: (2 * i + turn, 0)
    table = pl.BlockSpec((rows, LANES), lambda i, w: (w[SPOT + 2 * i + turn], 0))
    in_specs = [whole((rows, width))] * 2 + [whole((width,))] * 2
    in_specs += [whole(weight.shape) for weight in weights] + [table, table]
    out_specs = [
        pl.BlockSpec((rows, out_width), block),
        pl.BlockSpec((width, rows), lambda i, w: (0, 2 * i + turn)),
    ]
    out_shape = [((total, out_width), BF16), ((width, total), BF16)]
    aliases = {}
    if previous:
        aliases = {1 + len(in_specs): 0, 2 + len(in_specs): 1}
        in_specs += [pl.BlockSpec(memory_space=pl.ANY)] * 2
    else:
        out_specs.append(whole((width, out_width)))
        out_shape.append(((width, out_width), BF16))
    return call(
        functools.partial(project_kernel, first=not previous, pairs=out_width // (3 * LANES)),
        (2,), in_specs, out_specs, out_shape, [],
        SMALL, aliases, 12,
    )(where, mine, other, gain, shift, *weights, *tables, *previous)


def mask_lane(lane, head, keys, bias):
    return jnp.where(lane == (HD if head == 0 else 0), bias, keys)


def only_head(lane, head, values):
    return jnp.where(lane // HD == head, values, jnp.zeros_like(values))


def with_one(lane, head, values):
    one = lane == (HD if head == 0 else 0)
    return jnp.where(one, jnp.ones_like(values), only_head(lane, head, values))


def fill_bias(where_ref, bias_ref):
    rows = bias_ref.shape[0] // 4
    for block in range(4):
        kept = kept_rows(where_ref, block, rows, LANES)
        bias_ref[block * rows : (block + 1) * rows, :] = jnp.where(kept, 0.0, MASKED).astype(BF16)


def attend_kernel(
    where_ref, query_ref, key_ref, value_ref, mine_ref, other_ref, ctx_t_ref, lse_ref,
    bias_ref, ctx_ref, scores_ref, weights_ref, *, tile,
):
    total = query_ref.shape[0]
    lane = lax.broadcasted_iota(jnp.int32, (1, LANES), 1)

    @pl.when(pl.program_id(0) == 0)
    def _():
        fill_bias(where_ref, bias_ref)

    keys = key_ref[...]
    values_t = value_ref[...].T
    keys_aug = [mask_lane(lane, head, keys, bias_ref[...]) for head in range(2)]
    work = [(head, start) for head in range(2) for start in range(0, total, tile)]

    def score(place):
        head, start = work[place]
        queries = with_one(lane, head, query_ref[start : start + tile, :])
        scores_ref[place % 2] = dot_back(keys_aug[head], queries)

    def weigh(place):
        scores = scores_ref[place % 2]
        highest = jnp.max(scores, axis=0, keepdims=True)
        weights = jnp.exp(scores - highest)
        weights_ref[place % 2] = weights.astype(BF16)
        return highest, jnp.sum(weights, axis=0, keepdims=True)

    def attend(place, highest, sums):
        head, start = work[place]
        context = dot(values_t[head * HD : (head + 1) * HD, :], weights_ref[place % 2])
        ctx_ref[head * HD : (head + 1) * HD, start : start + tile] = context / sums
        lse_ref[0, head : head + 1, start : start + tile] = highest + jnp.log(sums)

    score(0)
    before = None
    for place in range(len(work) + 1):
        if place + 1 < len(work):
            score(place + 1)
        if before is not None:
            attend(place - 1, *before)
        if place < len(work):
            before = weigh(place)
    ctx_t_ref[...] = ctx_ref[...].astype(BF16)
    contexts = ctx_ref[...].T.astype(BF16)
    mine_ref[...] = contexts[: total // 2]
    other_ref[...] = contexts[total // 2 :]


def attend_call(where, qkv):
    total, width = qkv.shape
    pairs = width // (3 * LANES)
    width //= 3
    half = total // 2
    tile = half
    column = lambda part: pl.BlockSpec((total, LANES), lambda p, w: (0, 3 * p + part))
    out_column = pl.BlockSpec((half, LANES), lambda p, w: (0, p))
    return call(
        functools.partial(attend_kernel, tile=tile),
        (pairs,),
        [column(0), column(1), column(2)],
        [
            out_column, out_column,
            pl.BlockSpec((LANES, total), lambda p, w: (p, 0)),
            pl.BlockSpec((1, 8, total), lambda p, w: (p, 0, 0)),
        ],
        [((half, width), BF16), ((half, width), BF16), ((width, total), BF16), ((pairs, 8, total), F32)],
        [
            pltpu.VMEM((total, LANES), BF16),
            pltpu.VMEM((LANES, total), F32),
            pltpu.VMEM((2, total, tile), F32),
            pltpu.VMEM((2, total, tile), BF16),
        ],
        SMALL, mib=16,
    )(where, qkv, qkv, qkv)


def stack_rows(refs):
    return jnp.concatenate([ref[0] for ref in refs], axis=0)


def residual_kernel(
    where_ref, keep_ref, recv_ref, mine_ref, got_ref, w0_ref, w1_ref, w2_ref, w3_ref,
    gain_ref, shift_ref, res_ref, normed_ref,
):
    step = pl.program_id(0)
    values = jnp.where(step == 0, keep_ref[...], recv_ref[...]).astype(F32)
    attended = dot(mine_ref[...], stack_rows((w0_ref, w1_ref)))
    attended += dot(got_ref[...], stack_rows((w2_ref, w3_ref)))
    residual = values + attended
    res_ref[...] = residual
    normal, _ = normalize(residual)
    normed_ref[...] = (normal * row_vector(gain_ref) + row_vector(shift_ref)).astype(BF16)


def out_weight_specs(group, width):
    places = (
        lambda w: w[CORE],
        lambda w: 2 + w[CORE],
        lambda w: 1 - w[CORE],
        lambda w: 3 - w[CORE],
    )
    return [pl.BlockSpec((1, group, width), lambda i, w, at=at: (at(w), 0, 0)) for at in places]


def residual_call(where, keep, recv, ctx_mine, ctx_got, w_out, gain, shift):
    rows, width = keep.shape
    heads = ctx_mine.shape[1]
    row = lambda lanes: pl.BlockSpec((rows, lanes), lambda i, w: (i, 0))
    return call(
        residual_kernel,
        (2,),
        [whole((rows, width))] * 2 + [row(heads)] * 2
        + out_weight_specs(heads // 2, width) + [whole((width,))] * 2,
        [row(width)] * 2,
        [((2 * rows, width), F32), ((2 * rows, width), BF16)],
        [],
        SMALL, mib=10,
    )(where, keep, recv, ctx_mine, ctx_got, w_out, w_out, w_out, w_out, gain, shift)


def gelu_both(values):
    root = 0.7978845608028654
    bend = (root * 0.044715) * (values * values)
    half = 0.5 * jnp.tanh(values * (root + bend)) + 0.5
    steep = values * (2.0 * root + 6.0 * bend)
    return values * half, half * ((1.0 - half) * steep + 1.0)


def fill_cotangent(where_ref, refs, grad_ref):
    rows, width = refs[0].shape
    for place, ref in enumerate(refs):
        kept = kept_rows(where_ref, place, rows, width)
        grad_ref[place * rows : (place + 1) * rows, :] = jnp.where(kept, ref[...], jnp.zeros_like(ref))


def feed_kernel(
    where_ref,
    normed_m_ref, normed_o_ref, cot0_ref, cot1_ref, cot2_ref, cot3_ref, up_ref, down_ref,
    up_send_ref, up_keep_ref, send_ref, keep_ref, active_ref, back_m_ref, back_o_ref,
    normed_ref, grad_ref, normed_t_ref, grad_t_ref, hidden_ref, before_ref, up_before_ref,
):
    step = pl.program_id(0)
    half, width = normed_m_ref.shape
    block = up_ref.shape[1]

    @pl.when(step == 0)
    def _():
        normed_ref[:half, :] = normed_m_ref[...]
        normed_ref[half:, :] = normed_o_ref[...]
        fill_cotangent(where_ref, (cot0_ref, cot1_ref, cot2_ref, cot3_ref), grad_ref)
        normed_t_ref[...] = normed_ref[...].T
        grad_t_ref[...] = grad_ref[...].T

    hidden = dot(normed_ref[...], up_ref[...])
    active, slope = gelu_both(hidden)
    active_ref[...] = active.astype(BF16)
    grad_active = dot_back(grad_ref[...], down_ref[...])
    hidden_ref[...] = (grad_active * slope).astype(BF16)
    up_grad = dot(normed_t_ref[...], hidden_ref[...]).astype(BF16)
    down_grad = dot(grad_t_ref[...], active_ref[...]).astype(BF16)
    part = block // 2
    for side in range(2):
        piece = down_grad[:, side * part : (side + 1) * part]

        @pl.when(where_ref[SIDE] == side)
        def _():
            keep_ref[0] = piece

        @pl.when(where_ref[SIDE] != side)
        def _():
            send_ref[0] = piece

    @pl.when(step == 0)
    def _():
        up_send_ref[...] = up_grad
        before_ref[...] = hidden_ref[...]
        up_before_ref[...] = up_ref[...]

    @pl.when(step == 1)
    def _():
        up_keep_ref[...] = up_grad
        back = dot_back(before_ref[...], up_before_ref[...]) + dot_back(hidden_ref[...], up_ref[...])
        back_m_ref[...] = back[:half]
        back_o_ref[...] = back[half:].astype(BF16)


def feed_high(last, w):
    return jnp.where(last, w[ROW], 1 - w[ROW])


def feed_call(where, normed_m, normed_o, cotangents, w_up, w_down):
    half, width = normed_m.shape
    total = 2 * half
    block = w_up.shape[1] // 4
    part = block // 2
    token = whole((half, width))
    piece = pl.BlockSpec((1, width, part), lambda j, w: (j, 0, 0))
    return call(
        feed_kernel,
        (2,),
        [token, token]
        + [whole((half // 2, width))] * 4
        + [
            pl.BlockSpec((width, block), lambda j, w: (0, 2 * feed_high(j == 1, w) + w[CORE])),
            pl.BlockSpec((block, width), lambda j, w: (2 * feed_high(j == 1, w) + w[CORE], 0)),
        ],
        [
            whole((width, block)), whole((width, block)), piece, piece,
            pl.BlockSpec((total, block), lambda j, w: (0, j)),
            token, token,
        ],
        [
            ((width, block), BF16),
            ((width, block), BF16),
            ((2, width, part), BF16),
            ((2, width, part), BF16),
            ((total, 2 * block), BF16),
            ((half, width), F32),
            ((half, width), BF16),
        ],
        [
            pltpu.VMEM((total, width), BF16),
            pltpu.VMEM((total, width), BF16),
            pltpu.VMEM((width, total), BF16),
            pltpu.VMEM((width, total), BF16),
            pltpu.VMEM((total, block), BF16),
            pltpu.VMEM((total, block), BF16),
            pltpu.VMEM((width, block), BF16),
        ],
        SMALL, mib=28,
    )(where, normed_m, normed_o, *cotangents, w_up, w_down)


def feed_out_kernel(where_ref, active_ref, down0_ref, down1_ref, mine_ref, *other_refs):
    block = down0_ref.shape[0]
    out = dot(active_ref[:, :block], down0_ref[...]) + dot(active_ref[:, block:], down1_ref[...])
    size = other_refs[0].shape[0]

    @pl.when(pl.program_id(0) == 0)
    def _():
        for part, ref in enumerate(other_refs):
            ref[...] = out[part * size : (part + 1) * size].astype(BF16)

    @pl.when(pl.program_id(0) == 1)
    def _():
        mine_ref[...] = out


def feed_out_call(where, active, w_down):
    total, block = active.shape
    block //= 2
    width = w_down.shape[1]
    half = total // 2
    row = pl.BlockSpec((half, 2 * block), lambda i, w: (1 - i, 0))
    down = [
        pl.BlockSpec((block, width), lambda i, w, last=last: (2 * feed_high(last, w) + w[CORE], 0))
        for last in (False, True)
    ]
    return call(
        feed_out_kernel,
        (2,),
        [row, *down],
        [whole((half, width))] + [whole((half // 4, width))] * 4,
        [((half, width), F32)] + [((half // 4, width), BF16)] * 4,
        [], SMALL, mib=12,
    )(where, active, w_down, w_down)


def by_step(refs, step):
    low = jnp.concatenate([refs[0][...], refs[1][...]], axis=0)
    high = jnp.concatenate([refs[2][...], refs[3][...]], axis=0)
    return jnp.where(step == 0, high, low).astype(F32)


def output_kernel(where_ref, res_ref, out_ref, got0_ref, got1_ref, got2_ref, got3_ref, send_ref, keep_ref):
    step = pl.program_id(0)
    output = res_ref[...] + out_ref[...] + by_step((got0_ref, got1_ref, got2_ref, got3_ref), step)
    kept = kept_rows(where_ref, 1 - step, *output.shape)
    output = jnp.where(kept, output, jnp.zeros_like(output)).astype(BF16)

    @pl.when(step == 0)
    def _():
        send_ref[...] = output

    @pl.when(step == 1)
    def _():
        keep_ref[0] = output


def output_call(where, residual, out, got):
    half, width = residual.shape
    rows = half // 2
    row = pl.BlockSpec((rows, width), lambda i, w: (1 - i, 0))
    return call(
        output_kernel,
        (2,),
        [row] * 2 + [whole((rows // 2, width))] * 4,
        [whole((rows, width)), pl.BlockSpec((1, rows, width), lambda i, w: (w[ROW], 0, 0))],
        [((rows, width), BF16), ((2, rows, width), BF16)],
        [], SMALL, mib=8,
    )(where, residual, out, *got)


def add_sums(sums_ref, step, row, gains, shifts):
    @pl.when(step == 0)
    def _():
        sums_ref[...] = jnp.zeros_like(sums_ref)

    sums_ref[row : row + 1, :] += gains
    sums_ref[row + 1 : row + 2, :] += shifts


def middle_kernel(
    where_ref,
    res_ref, back_ref, back_got_ref, cot0_ref, cot1_ref, gain_ref, grad_low_ref, sums_ref,
):
    step = pl.program_id(0)
    residual = res_ref[...]
    kept = kept_rows(where_ref, step, *residual.shape)
    normal, inverse = normalize(residual)
    back = back_ref[...] + back_got_ref[...].astype(F32)
    gains = jnp.sum(back * normal, axis=0, keepdims=True)
    shifts = jnp.sum(back, axis=0, keepdims=True)

    add_sums(sums_ref, step, 2, gains, shifts)
    cotangent = jnp.where(step == 0, cot0_ref[...], cot1_ref[...]).astype(F32)
    cotangent = jnp.where(kept, cotangent, jnp.zeros_like(cotangent))
    grad = cotangent + norm_back(back, row_vector(gain_ref), normal, inverse)
    grad_low_ref[...] = grad.astype(BF16)


def middle_call(where, residual, back_m, back_got, cot_keep, cot_recv, gain):
    half, width = residual.shape
    rows = half // 2
    row = pl.BlockSpec((rows, width), lambda i, w: (i, 0))
    return call(
        middle_kernel,
        (2,),
        [row] * 3 + [whole((rows, width))] * 2 + [whole((width,))],
        [row, whole((8, width))],
        [((half, width), BF16), ((8, width), F32)],
        [], SMALL, mib=8,
    )(where, residual, back_m, back_got, cot_keep, cot_recv, gain)


def piece_order(where_ref):
    side, row = where_ref[SIDE], where_ref[ROW]
    order = []
    for kept in (0, 1):
        mine = side if kept else 1 - side
        order += [8 * high + 2 * mine + half for high in (0, 1) for half in (0, 1)]
    for kept in (0, 1):
        mine = row if kept else 1 - row
        order += [8 * high + 4 + 2 * one + mine for high in (0, 1) for one in (0, 1)]
    return order


def attend_back_kernel(
    where_ref,
    query_ref, key_ref, value_ref, ctx_ref, grad_m_ref, grad_o_ref, w0_ref, w1_ref, lse_ref,
    ctx_mine_hbm, ctx_got_hbm, cos_hbm, sin_hbm, normed_t_hbm, *rest,
    score_scale, first, last,
):
    if last:
        rest = rest[4:]
    out_refs, grads_ref = rest[:4], rest[4]
    rest = rest[5:]
    bias_ref, grad_ref, columns_ref, dqt_ref, dk_acc, dv_acc, qkv_ref, own_ref = rest[:8]
    ctx_mine_ref, ctx_got_ref, cos_ref, sin_ref, normed_t_ref, semaphores = rest[8:]
    step = pl.program_id(0)
    total = query_ref.shape[0]
    half = total // 2
    model = grad_m_ref.shape[1]
    lane = lax.broadcasted_iota(jnp.int32, (1, LANES), 1)
    unit = model // 16
    group = model // 4
    rows = total // 4
    late = [(ctx_mine_hbm, ctx_mine_ref), (ctx_got_hbm, ctx_got_ref), (normed_t_hbm, normed_t_ref)]
    for source, target in ((cos_hbm, cos_ref), (sin_hbm, sin_ref)):
        for block in range(4):
            begin = pl.multiple_of(where_ref[SPOT + block] * rows, rows)
            late.append((source.at[pl.ds(begin, rows)], target.at[pl.ds(block * rows, rows)]))

    def copies():
        return [
            pltpu.make_async_copy(source, target, semaphores.at[k])
            for k, (source, target) in enumerate(late)
        ]

    @pl.when(step == 0)
    def _():
        for copy in copies():
            copy.start()
        fill_bias(where_ref, bias_ref)
        grad_ref[:half, :] = grad_m_ref[...]
        grad_ref[half:, :] = grad_o_ref[...]

    for place, pair in enumerate(first):
        for core in range(2):

            @pl.when((step == place) & (where_ref[CORE] == core))
            def _():
                columns_ref[...] = pair_columns(grad_ref, core, pair)

    wout = jnp.concatenate([w0_ref[...], w1_ref[...]], axis=0)
    gctx = dot_back(grad_ref[...], wout).astype(BF16)
    products = gctx.astype(F32).T * ctx_ref[...].astype(F32)
    keys = key_ref[...]
    keys_t = keys.T
    values = value_ref[...]
    queries = query_ref[...]
    for head in range(2):
        key_aug = mask_lane(lane, head, keys, bias_ref[...])
        delta = jnp.sum(products[head * HD : (head + 1) * HD, :], axis=0, keepdims=True)
        scores = dot_back(key_aug, with_one(lane, head, queries))
        weights = jnp.exp(scores - lse_ref[0, head : head + 1, :])
        grads = only_head(lane, head, gctx)
        grad_weights = dot_back(values, grads)
        grad_scores = (weights * (grad_weights - delta)).astype(BF16)
        dv = dot(weights.astype(BF16), grads)
        dk = dot(grad_scores, only_head(lane, head, queries))
        dqt_ref[head * HD : (head + 1) * HD, :] = dot(
            keys_t[head * HD : (head + 1) * HD, :], grad_scores
        )
        if head == 0:
            dv_acc[...] = dv
            dk_acc[...] = dk
        else:
            dv_acc[...] += dv
            dk_acc[...] += dk

    @pl.when(step == 0)
    def _():
        for copy in copies():
            copy.wait()

    cosine, sine = cos_ref[...], sin_ref[...]
    dq = dqt_ref[...].T * score_scale
    dk = dk_acc[...]
    dq = (dq * cosine - swap_halves(dq) * sine).astype(BF16)
    dk = (dk * cosine - swap_halves(dk) * sine).astype(BF16)
    grads = jnp.concatenate([dq, dk, dv_acc[...].astype(BF16)], axis=1)
    qkv_ref[...] = dot(normed_t_ref[...], grads).astype(BF16)
    columns = columns_ref[...]
    turned = jnp.concatenate([columns[half:], columns[:half]], axis=0)
    own_ref[0] = dot(ctx_mine_ref[...], columns).astype(BF16)
    own_ref[1] = dot(ctx_got_ref[...], turned).astype(BF16)
    for place, source in enumerate(piece_order(where_ref)):
        ref = out_refs[place // 4]
        span = slice(place % 4 * unit, (place % 4 + 1) * unit)
        ref[span, : 3 * LANES] = qkv_ref[pl.ds(pl.multiple_of(source * unit, unit), unit), :]
        block = source // 4
        other = jnp.where(block % 2 == where_ref[CORE], 0, 1)
        inside = pl.multiple_of((block // 2) * group + (source % 4) * unit, unit)
        ref[span, 3 * LANES :] = own_ref[other, pl.ds(inside, unit), :]
    grads_ref[...] = grads


def normed_grad_kernel(where_ref, early_ref, late_ref, weight_ref, mine_ref, *other_refs):
    split = early_ref.shape[1]
    back = dot_back(early_ref[...], weight_ref[:, :split])
    back += dot_back(late_ref[...], weight_ref[:, split:])
    half = mine_ref.shape[0]
    size = half // len(other_refs)
    mine_ref[...] = back[:half]
    for part, ref in enumerate(other_refs):
        ref[...] = back[half + part * size : half + (part + 1) * size].astype(BF16)


def normed_grad_call(where, early, late, weight):
    half, width = early.shape[0] // 2, weight.shape[0]
    return stage_call(
        normed_grad_kernel, where, (early, late, weight),
        [((half, width), F32)] + [((half // 4, width), BF16)] * 4,
    )


def attend_back_call(
    pairs, where, qkv, ctx_t, ctx_got_t, grad_m, grad_o, w_out, lse, tables, normed_t,
    pieces=(),
):
    total, width = qkv.shape
    width //= 3
    half, model = grad_m.shape
    quarter = model // 4
    last = bool(pieces)
    begin = pairs[0]
    column = lambda part: pl.BlockSpec((total, LANES), lambda i, w: (0, 3 * (begin + i) + part))

    def head_rows(which):
        per = width // HD // 2

        def at(i, w):
            head = 2 * (begin + i) + which
            return (head // per * 2 * per + w[CORE] * per + head % per, 0)

        return pl.BlockSpec((HD, model), at)

    in_specs = [
        column(0), column(1), column(2),
        pl.BlockSpec((LANES, total), lambda i, w: (begin + i, 0)),
        whole((half, model)), whole((half, model)),
        head_rows(0), head_rows(1),
        pl.BlockSpec((1, 8, total), lambda i, w: (begin + i, 0, 0)),
    ]
    in_specs += [pl.BlockSpec(memory_space=pl.ANY)] * 5
    args = [
        qkv, qkv, qkv, ctx_t, grad_m, grad_o, w_out, w_out, lse, ctx_t, ctx_got_t, *tables, normed_t,
    ]
    out_specs = [pl.BlockSpec((quarter, 4 * LANES), lambda i, w: (0, begin + i))] * 4
    out_shape = [((quarter, 4 * width), BF16)] * 4
    aliases = {}
    if last:
        aliases = {1 + len(args) + k: k for k in range(4)}
        in_specs += [pl.BlockSpec(memory_space=pl.ANY)] * 4
        args += list(pieces)
    out_specs.append(pl.BlockSpec((total, 3 * LANES), lambda i, w: (0, i)))
    out_shape.append(((total, 3 * LANES * len(pairs)), BF16))
    return call(
        functools.partial(attend_back_kernel, score_scale=HD ** (-0.5), first=pairs, last=last),
        (len(pairs),), in_specs, out_specs, out_shape,
        [
            pltpu.VMEM((total, LANES), BF16),
            pltpu.VMEM((total, model), BF16),
            pltpu.VMEM((total, LANES), BF16),
            pltpu.VMEM((LANES, total), F32),
            pltpu.VMEM((total, LANES), F32),
            pltpu.VMEM((total, LANES), F32),
            pltpu.VMEM((model, 3 * LANES), BF16),
            pltpu.VMEM((2, width, LANES), BF16),
            pltpu.VMEM((width, total), BF16),
            pltpu.VMEM((width, total), BF16),
            pltpu.VMEM((total, LANES), F32),
            pltpu.VMEM((total, LANES), F32),
            pltpu.VMEM((model, total), BF16),
            pltpu.SemaphoreType.DMA((11,)),
        ],
        SMALL, aliases, mib=26,
    )(where, *args)


def stage_one_kernel(
    where_ref, up_keep, up_got, down_keep, down_got, up_sent, up_kept, down_sent, down_kept
):
    side, row = where_ref[SIDE], where_ref[ROW]
    unit = up_keep.shape[0] // 8
    for one in range(4):
        to = slice(one * unit, (one + 1) * unit)
        for out, mine in ((up_sent, 1 - side), (up_kept, side)):
            span = pl.ds(pl.multiple_of((2 * one + mine) * unit, unit), unit)
            out[to, :] = added(up_keep, up_got, span).astype(BF16)
    size = down_keep.shape[1] // 2
    for place, block in enumerate((1 - row, row)):
        for out, mine in ((down_sent, 1 - row), (down_kept, row)):
            span = pl.ds(pl.multiple_of(mine * size, size), size)
            out[block] = added(down_keep.at[place], down_got.at[place], span).astype(BF16)


def stage_one_call(where, up_keep, up_got, down_keep, down_got):
    rows, width = up_keep.shape
    _, size, lanes = down_keep.shape
    return stage_call(
        stage_one_kernel, where, (up_keep, up_got, down_keep, down_got),
        [((rows // 2, width), BF16)] * 2 + [((2, size // 2, lanes), BF16)] * 2,
    )


def added(one, two, span):
    return one[span, :].astype(F32) + two[span, :].astype(F32)


def stage_two_kernel(where_ref, up_kept, up_got, down_kept, down_got, sent, kept):
    unit = kept.shape[1] // 2
    size, lanes = down_kept.shape[1] // 2, down_kept.shape[2]
    low = where_ref[HIGH] % 2
    for high in range(2):
        for out, which in ((sent, 1 - low), (kept, low)):
            span = pl.ds(pl.multiple_of((2 * high + which) * unit, unit), unit)
            out[high, :unit, :] = added(up_kept, up_got, span).astype(BF16)
            for fold in range(size // unit):
                span = pl.ds(pl.multiple_of(which * size + fold * unit, unit), unit)
                values = added(down_kept.at[high], down_got.at[high], span)
                out[high, unit:, fold * lanes : (fold + 1) * lanes] = values.astype(BF16)


def halve_kernel(where_ref, before, got, sent, kept):
    high = where_ref[HIGH] // 2
    for out, which in ((sent, 1 - high), (kept, high)):
        out[...] = (before[which].astype(F32) + got[which].astype(F32)).astype(out.dtype)


def halve_call(where, before, got):
    shape = before.shape[1:]
    return stage_call(halve_kernel, where, (before, got), [(shape, BF16), (shape, F32)])


def stage_call(kernel, where, inputs, out_shape, mib=8):
    return call(
        kernel, (1,), [whole(one.shape) for one in inputs], [whole(shape) for shape, _ in out_shape],
        out_shape, [], SMALL, mib=mib,
    )(where, *inputs)


def stage_two_call(where, up_kept, up_got, down_kept, down_got):
    rows, width = up_kept.shape
    part = (2, rows // 2, width)
    return stage_call(
        stage_two_kernel, where, (up_kept, up_got, down_kept, down_got), [(part, BF16)] * 2
    )


def feed_sum_kernel(where_ref, own, got, up, down):
    unit, lanes = up.shape[0], down.shape[1]
    summed = own[...] + got[...].astype(F32)
    up[...] = summed[:unit]
    for fold in range(up.shape[1] // lanes):
        values = summed[unit:, fold * lanes : (fold + 1) * lanes]
        down[fold * unit : (fold + 1) * unit, :] = values.astype(BF16)


def feed_sum_call(where, own, got, lanes):
    rows, width = own.shape
    unit = rows // 2
    return stage_call(
        feed_sum_kernel, where, (own, got), [((unit, width), F32), ((unit * width // lanes, lanes), BF16)]
    )


def stage_three_kernel(where_ref, *refs):
    first_keep, first_got, second_keep, second_got, sums, sums_got = refs[:6]
    first_sent, first_kept, second_sent, second_kept = refs[6:]
    side, row = where_ref[SIDE], where_ref[ROW]
    unit = first_sent.shape[0] // 2
    for keep, got, mine, sent, kept in (
        (first_keep, first_got, row, first_sent, first_kept),
        (second_keep, second_got, side, second_sent, second_kept),
    ):
        for high in range(2):
            to = slice(high * unit, (high + 1) * unit)
            for out, which in ((sent, 1 - mine), (kept, mine)):
                span = pl.ds(pl.multiple_of((2 * high + which) * unit, unit), unit)
                out[to, :] = added(keep, got, span).astype(out.dtype)
    summed = sums[...] + sums_got[...]
    width = summed.shape[1]
    for out in (second_sent, second_kept):
        out[2 * unit :, :] = jnp.zeros_like(out[2 * unit :, :])
        out[2 * unit :, :width] = summed.astype(out.dtype)


def stage_three_call(where, first_keep, first_got, second_keep, second_got, sums, sums_got):
    rows, lanes = first_keep.shape[0] // 2, first_keep.shape[1]
    more = sums.shape[0]
    return stage_call(
        stage_three_kernel, where, (first_keep, first_got, second_keep, second_got, sums, sums_got),
        [
            ((rows, lanes), BF16), ((rows, lanes), F32),
            ((rows + more, lanes), BF16), ((rows + more, lanes), F32),
        ],
    )


def stage_four_kernel(where_ref, first_kept, first_got, second_kept, second_got, sent0, sent1, kept):
    rows = first_kept.shape[0]
    unit = rows // 2
    low = where_ref[HIGH] % 2
    sums = added(second_kept, second_got, slice(rows, None))
    for which, (before, got) in enumerate(((first_kept, first_got), (second_kept, second_got))):

        @pl.when(low == which)
        def _():
            kept[:rows, :] = added(before, got, slice(0, rows))

        @pl.when(low != which)
        def _():
            sent0[...] = added(before, got, slice(0, unit)).astype(BF16)
            sent1[:unit, :] = added(before, got, slice(unit, rows)).astype(BF16)

    kept[rows:, :] = sums
    sent1[unit:, :] = sums.astype(BF16)


def stage_four_call(where, first_kept, first_got, second_kept, second_got):
    rows, lanes = first_kept.shape
    more = second_kept.shape[0] - rows
    return stage_call(
        stage_four_kernel, where, (first_kept, first_got, second_kept, second_got),
        [((rows // 2, lanes), BF16), ((rows // 2 + more, lanes), BF16), ((rows + more, lanes), F32)],
    )


def halve_rows_kernel(where_ref, before, got0, got1, sent, kept):
    unit = got0.shape[0]
    high = where_ref[HIGH] // 2
    for which, got in enumerate((got0, got1)):
        values = before[which * unit : (which + 1) * unit, :] + got[:unit, :].astype(F32)

        @pl.when(high == which)
        def _():
            kept[:unit, :] = values

        @pl.when(high != which)
        def _():
            sent[:unit, :] = values.astype(BF16)

    sums = before[2 * unit :, :] + got1[unit:, :].astype(F32)
    kept[unit:, :] = sums
    sent[unit:, :] = sums.astype(BF16)


def halve_rows_call(where, before, got0, got1):
    shape = got1.shape
    return stage_call(halve_rows_kernel, where, (before, got0, got1), [(shape, BF16), (shape, F32)])


def stage_five_kernel(where_ref, own, got, sent, mine, *, pairs):
    summed = own[...] + got[...].astype(F32)
    width = mine.shape[1]
    unit = own.shape[0] - 8
    group = width // 4
    blocks = ([], [])
    for part in range(4):
        starts = [(4 * pair + part) * LANES for pair in range(pairs)]
        columns = jnp.concatenate([summed[:unit, at : at + LANES] for at in starts], axis=1)
        blocks[0].append(columns[:, :group])
        blocks[1].append(columns[:, group:])
    for row in range(2):

        @pl.when(where_ref[ROW] == row)
        def _():
            mine[:unit, :] = jnp.concatenate(blocks[row], axis=1)
            sent[:unit, :] = jnp.concatenate(blocks[1 - row], axis=1).astype(BF16)

    mine[unit:, :] = summed[unit:, :width]
    sent[unit:, :] = summed[unit:, :width].astype(BF16)


def stage_five_call(where, own, got, pairs):
    rows, lanes = own.shape
    shape = (rows, lanes // pairs // LANES * HD * pairs)
    return stage_call(
        functools.partial(stage_five_kernel, pairs=pairs), where, (own, got), [(shape, BF16), (shape, F32)]
    )


def stage_six_kernel(where_ref, mine, other, down_got, *outs):
    weights, sums, down = outs[:4], outs[4:8], outs[8]
    unit = mine.shape[0] - 8
    group = weights[0].shape[1]
    row = where_ref[ROW]
    for ref, place in ((mine, row), (other, 1 - row)):
        span = pl.ds(pl.multiple_of(place * unit, unit), unit)
        for part, out in enumerate(weights):
            out[span, :] = ref[:unit, part * group : (part + 1) * group].astype(F32)
    summed = added(mine, other, slice(unit, None))
    for which, out in enumerate(sums):
        out[...] = summed[which : which + 1, :].reshape(out.shape)
    down[...] = down_got[...].astype(F32)


def stage_six_call(where, mine, other, down_got):
    rows, width = mine.shape
    unit, group = rows - 8, width // 4
    rows, lanes = down_got.shape
    return stage_call(
        stage_six_kernel, where, (mine, other, down_got),
        [((2 * unit, group), F32)] * 4 + [((width,), F32)] * 4 + [((rows, lanes), F32)],
    )


def tokens_grad_kernel(
    where_ref,
    keep_ref, recv_ref, back_ref, got0_ref, got1_ref, got2_ref, got3_ref, grad_res_ref, gain_ref,
    keep_out_ref, send_out_ref, sums_ref,
):
    step = pl.program_id(0)
    values = jnp.where(step == 0, recv_ref[...], keep_ref[...]).astype(F32)
    normal, inverse = normalize(values)
    back = back_ref[...] + by_step((got0_ref, got1_ref, got2_ref, got3_ref), step)
    gains = jnp.sum(back * normal, axis=0, keepdims=True)
    shifts = jnp.sum(back, axis=0, keepdims=True)
    grad = (grad_res_ref[...].astype(F32) + norm_back(back, row_vector(gain_ref), normal, inverse)).astype(BF16)

    add_sums(sums_ref, step, 0, gains, shifts)

    @pl.when(step == 0)
    def _():
        send_out_ref[...] = grad

    @pl.when(step == 1)
    def _():
        keep_out_ref[0] = grad


def tokens_grad_call(where, keep, recv, back, got, grad_res, gain):
    rows, width = keep.shape
    row = pl.BlockSpec((rows, width), lambda i, w: (1 - i, 0))
    return call(
        tokens_grad_kernel,
        (2,),
        [whole((rows, width))] * 2 + [row] + [whole((rows // 2, width))] * 4 + [row, whole((width,))],
        [
            pl.BlockSpec((1, rows, width), lambda i, w: (w[ROW], 0, 0)),
            whole((rows, width)),
            whole((8, width)),
        ],
        [((2, rows, width), BF16), ((rows, width), BF16), ((8, width), F32)],
        [],
        SMALL, mib=8,
    )(where, keep, recv, back, *got, grad_res, gain)


def local(
    tokens, gain_one, shift_one, w_query, w_key, w_value, w_out, gain_two, shift_two, w_up, w_down,
    cotangent, lengths,
):
    row_count, piece, width = tokens.shape
    n_dp = lax.axis_size("dp")
    n_seq = lax.axis_size("seq")
    count = n_dp // 4
    place = lax.axis_index("seq")
    core, row = place % 2, place // 2
    data = lax.axis_index("dp")
    high = data // count
    side = (data // (count // 2)) % 2
    total = n_seq * piece
    group = width // n_seq

    tok_send, tokens = together(pick(tokens, 1 - row), tokens)
    tok_recv = swap(tok_send, "seq", 2)
    tok_keep = pick(tokens, row)
    tok_keep_o = swap(tok_keep, "seq", 1)
    cot_keep = pick(cotangent, row)
    cot_recv = swap(pick(cotangent, 1 - row), "seq", 2)

    where = jnp.stack(
        [
            core, row, side, pick(lengths, row),
            2 * row + core, 2 * (1 - row) + core, 2 * row + 1 - core, 2 * (1 - row) + 1 - core,
            high,
        ]
    ).astype(jnp.int32)
    tables = tuple(jnp.asarray(table) for table in rotary_tables(total))
    out_blocks = w_out.reshape(n_seq, group, width)

    qkv, normed_t, w_qkv = project_call(
        0, where, tok_keep, tok_keep_o, gain_one, shift_one, (w_query, w_key, w_value), tables, ()
    )
    tok_recv, qkv, normed_t = together(tok_recv, qkv, normed_t)
    tok_recv_o = swap(tok_recv, "seq", 1)
    qkv, normed_t = project_call(
        1, where, tok_recv, tok_recv_o, gain_one, shift_one, (w_qkv,), tables, (qkv, normed_t)
    )
    ctx_m, ctx_o, ctx_t, lse = attend_call(where, qkv)
    cot_keep_o = swap(cot_keep, "seq", 1)
    ctx_m, ctx_o, ctx_t, cot_recv, cot_keep_o = together(ctx_m, ctx_o, ctx_t, cot_recv, cot_keep_o)
    cotangents = (cot_keep, cot_recv, cot_keep_o, swap(cot_recv, "seq", 1))
    ctx_got = swap(ctx_o, "seq", 1)
    residual, normed_two = residual_call(
        where, tok_keep, tok_recv, ctx_m, ctx_got, out_blocks, gain_two, shift_two
    )
    normed_two_o = swap(normed_two, "seq", 1)
    ctx_got_t = swap(ctx_t, "seq", 1)
    up_send, up_keep, down_send, down_keep, active, back_m, back_o = feed_call(
        where, normed_two, normed_two_o, cotangents, w_up, w_down
    )
    up_got = swap(up_send, "seq", 2)
    down_got = swap(down_send, "dp", count // 2)
    back_got = swap(back_o, "seq", 1)
    grad_low, sums_two = middle_call(where, residual, back_m, back_got, cot_keep, cot_recv, gain_two)
    grad_low_o = swap(grad_low, "seq", 1)

    block_rows = width // n_dp

    pairs = qkv.shape[1] // (3 * LANES)

    def upper(up, down):
        bit = count // 4
        up = up.reshape(4, count // 2, block_rows, width).astype(F32)
        down = down.reshape(4, group, -1).astype(F32)
        while bit > 0:
            mine = (data // bit) % 2
            size, lanes = up.shape[1] // 2, down.shape[2] // 2
            sent = lax.dynamic_slice_in_dim(up, (1 - mine) * size, size, 1).astype(BF16)
            up = lax.dynamic_slice_in_dim(up, mine * size, size, 1) + swap(sent, "dp", bit)
            sent = lax.dynamic_slice_in_dim(down, (1 - mine) * lanes, lanes, 2).astype(BF16)
            down = lax.dynamic_slice_in_dim(down, mine * lanes, lanes, 2) + swap(sent, "dp", bit)
            bit //= 2
        up = up.reshape(4, block_rows, width)
        folds = width // down.shape[2]
        size = group // folds
        down = jnp.concatenate([down[:, k * size : (k + 1) * size] for k in range(folds)], axis=2)
        both = jnp.concatenate([up, down], axis=1).astype(BF16)
        both = both.reshape((2, 2) + both.shape[1:])
        return pick(both, 1 - high % 2, 1), pick(both, high % 2, 1)

    def halved(before, got):
        if count == 2:
            return halve_call(where, before, got)
        both = before.astype(F32) + got.astype(F32)
        return pick(both, 1 - high // 2).astype(BF16), pick(both, high // 2)

    def feed_sums(own, got):
        lanes = w_down.shape[0] // n_dp
        if count == 2:
            return feed_sum_call(where, own, got, lanes)
        own = own + got.astype(F32)
        up, down = own[:block_rows], own[block_rows:].astype(BF16)
        down = jnp.concatenate([down[:, k * lanes : (k + 1) * lanes] for k in range(width // lanes)])
        return up, down

    def exchanged(values):
        perm = []
        for d in range(n_dp):
            for s in range(n_seq):
                second_bit = (d // count) % 2
                to_d = d + (s % 2 - second_bit) * count
                to_s = s - s % 2 + second_bit
                perm.append((d * n_seq + s, to_d * n_seq + to_s))
        return lax.ppermute(values, ("dp", "seq"), perm)

    inner = count // 2
    attention = (where, qkv, ctx_t, ctx_got_t, grad_low, grad_low_o, w_out, lse, tables, normed_t)
    *first_pieces, early = attend_back_call(tuple(range(pairs - 1)), *attention)
    active, early = together(active, early)
    out_m, *out_o = feed_out_call(where, active, w_down)
    up_got, down_got, early, out_o = together(up_got, down_got, early, out_o)
    up_sent, up_kept, down_sent, down_kept = stage_one_call(where, up_keep, up_got, down_keep, down_got)
    up_sent, down_sent, early = together(up_sent, down_sent, early)
    up_got2 = swap(up_sent, "dp", inner)
    down_got2 = swap(down_sent, "seq", 2)
    *pieces, late = attend_back_call((pairs - 1,), *attention, first_pieces)
    pieces, late = together(pieces, late)
    last_got = (swap(pieces[0], "dp", inner), swap(pieces[2], "seq", 2))
    normed_m, *normed_o = normed_grad_call(where, early, late, w_qkv)
    normed_o, up_got2, down_got2 = together(normed_o, up_got2, down_got2)
    normed_got = [swap(one, "seq", 1) for one in normed_o]
    if count == 2:
        feed_sent, feed_kept = stage_two_call(where, up_kept, up_got2, down_kept, down_got2)
    else:
        feed_sent, feed_kept = upper(
            up_kept.astype(F32) + up_got2.astype(F32), down_kept.astype(F32) + down_got2.astype(F32)
        )
    feed_sent, normed_m = together(feed_sent, normed_m)
    feed_got = swap(feed_sent, "dp", count)
    tok_buf, tok_send, sums_one = tokens_grad_call(
        where, tok_keep, tok_recv, normed_m, normed_got, grad_low, gain_one
    )

    sums = sums_one + sums_two
    sums_got = swap(sums, "seq", 1)
    if count == 2:
        last_got, tok_send, sums_got = together(last_got, tok_send, sums_got)
        sent_first, kept_first, sent_second, kept_second = stage_three_call(
            where, pieces[1], last_got[0], pieces[3], last_got[1], sums, sums_got
        )
        sent_first, sent_second, tok_send = together(sent_first, sent_second, tok_send)
        got_first = swap(sent_first, "seq", 2)
        got_second = swap(sent_second, "dp", inner)
        feed_sent, feed_own = halved(feed_kept, feed_got)
        feed_got = swap(feed_sent, "dp", 2 * count)
        tok_back = swap(tok_send, "seq", 2)
        out_got = [swap(one, "seq", 1) for one in out_o]
        got_first, got_second, feed_sent = together(got_first, got_second, feed_sent)
        *sent, kept = stage_four_call(where, kept_first, got_first, kept_second, got_second)
        got = [swap(one, "dp", count) for one in sent]
        out_got, feed_got = together(out_got, feed_got)
        out_send, out_buf = output_call(where, residual, out_m, out_got)
        got, out_send = together(got, out_send)
        sent, kept = halve_rows_call(where, kept, *got)
        sent, out_send = together(sent, out_send)
        got = swap(sent, "dp", 2 * count)
        out_back = swap(out_send, "seq", 2)
        grad_up, grad_down = feed_sums(feed_own, feed_got)
        grad_down = exchanged(grad_down)
        got, tok_back, out_back = together(got, tok_back, out_back)
        sent, mine = stage_five_call(where, kept, got, pairs)
        other = swap(sent, "seq", 2)
        *ordered, sums0, sums1, sums2, sums3, grad_down = stage_six_call(where, mine, other, grad_down)
        sums, grad_down = (sums0, sums1, sums2, sums3), grad_down.T
    else:
        piece0, piece1, piece2, piece3 = pieces
        shape = (2, 2, width // 16, -1)
        sides = jnp.stack([piece0, piece1]).reshape((2,) + shape)
        sides = jnp.stack([pick(sides, jnp.where(side == k, 1, 0)) for k in (0, 1)], 1)
        halves = jnp.stack([piece2, piece3]).reshape((2,) + shape)
        halves = jnp.stack([pick(halves, jnp.where(row == k, 1, 0)) for k in (0, 1)], 2)
        summed = jnp.stack([sides, halves], 1).reshape(width, pairs, 4, LANES).transpose(0, 2, 1, 3)
        summed = summed.reshape(width, 4, 2, group)
        other = swap(pick(summed, 1 - row, 2), "seq", 2).astype(F32)
        summed = (pick(summed, row, 2).astype(F32) + other).astype(BF16).reshape(width, -1)
        ordered = lax.psum_scatter(summed, "dp", scatter_dimension=0, tiled=True).astype(F32)
        tok_back = swap(tok_send, "seq", 2)
        out_got = [swap(one, "seq", 1) for one in out_o]
        out_send, out_buf = output_call(where, residual, out_m, out_got)
        out_back = swap(out_send, "seq", 2)
        feed_sent, feed_own = halved(feed_kept, feed_got)
        grad_up, grad_down = feed_sums(feed_own, swap(feed_sent, "dp", 2 * count))
        grad_down = exchanged(grad_down).astype(F32).T
        sums = sums + sums_got
        sums = sums + swap(sums, "seq", 2)
        bit = 1
        while bit < n_dp:
            sums = sums + swap(sums, "dp", bit)
            bit *= 2
        ordered = [ordered[:, k * group : (k + 1) * group] for k in range(4)]

    output = lax.dynamic_update_slice(out_buf, out_back[None], (1 - row, 0, 0))
    grad_tokens = lax.dynamic_update_slice(tok_buf, tok_back[None], (1 - row, 0, 0))
    return (
        output,
        grad_tokens,
        sums[0],
        sums[1],
        ordered[0],
        ordered[1],
        ordered[2],
        ordered[3],
        sums[2],
        sums[3],
        grad_up,
        grad_down,
    )


def solution(mesh):
    tokens = P("dp", "seq", None)
    weights = P("dp", "seq")
    return jax.shard_map(
        local,
        mesh=mesh,
        in_specs=(tokens,) + (P(),) * 10 + (tokens, P("dp")),
        out_specs=(tokens, tokens, P(), P(), weights, weights, weights, weights, P(), P(), weights, weights),
        check_vma=False,
    )
```

```python
import functools

import jax
import jax.numpy as jnp
import numpy as np
from jax import lax
from jax.experimental import pallas as pl
from jax.experimental.pallas import tpu as pltpu
from jax.sharding import PartitionSpec as P

HD = 64
EPSILON = 1e-05
MASKED = -1000000000.0
LANES = 128
BF16 = jnp.bfloat16
F32 = jnp.float32
CORE, ROW, SIDE, LENGTH, SPOT, HIGH = 0, 1, 2, 3, 4, 8


def swap(values, axis, bit):
    count = lax.axis_size(axis)
    return lax.ppermute(values, axis, [(i, i ^ bit) for i in range(count)])


def together(*values):
    return lax.optimization_barrier(values)


def pick(values, index, axis=0):
    return lax.dynamic_index_in_dim(values, index, axis, keepdims=False)


def dot(left, right):
    return jnp.dot(left, right, preferred_element_type=F32)


def dot_back(left, right):
    return lax.dot_general(left, right, (((1,), (1,)), ((), ())), preferred_element_type=F32)


def normalize(values):
    average = jnp.mean(values, axis=-1, keepdims=True)
    centred = values - average
    variance = jnp.mean(centred * centred, axis=-1, keepdims=True)
    inverse = lax.rsqrt(variance + EPSILON)
    return centred * inverse, inverse


def norm_back(grad, gain, normal, inverse):
    scaled = grad * gain
    first = jnp.mean(scaled, axis=-1, keepdims=True)
    second = jnp.mean(scaled * normal, axis=-1, keepdims=True)
    return (scaled - first - normal * second) * inverse


def row_vector(ref):
    return ref[...].reshape(1, ref.shape[0])


def swap_halves(values):
    lane = lax.broadcasted_iota(jnp.int32, values.shape, 1)
    up = pltpu.roll(values, LANES - HD // 2, 1)
    down = pltpu.roll(values, HD // 2, 1)
    return jnp.where(lane % HD < HD // 2, up, down)


def rotary_tables(length):
    lane = np.arange(LANES)
    frequency = 10000.0 ** (-2.0 * (lane % (HD // 2)) / HD)
    angles = np.arange(length)[:, None] * frequency[None, :]
    sign = np.where(lane % HD < HD // 2, -1.0, 1.0)
    return np.cos(angles).astype(np.float32), (sign * np.sin(angles)).astype(np.float32)


def kept_rows(where_ref, block, rows, lanes):
    spot = lax.broadcasted_iota(jnp.int32, (rows, lanes), 0) + where_ref[SPOT + block] * rows
    return spot < where_ref[LENGTH]


SMALL = pl.CostEstimate(flops=1, bytes_accessed=1, transcendentals=0)


def whole(shape):
    return pl.BlockSpec(shape, lambda *_: (0,) * len(shape))


def call(kernel, grid, in_specs, out_specs, out_shape, scratch, estimate, aliases=None, mib=16):
    return pl.pallas_call(
        kernel,
        grid_spec=pltpu.PrefetchScalarGridSpec(
            num_scalar_prefetch=1,
            grid=grid,
            in_specs=in_specs,
            out_specs=out_specs,
            scratch_shapes=scratch,
        ),
        out_shape=[jax.ShapeDtypeStruct(shape, kind) for shape, kind in out_shape],
        input_output_aliases=aliases or {},
        compiler_params=pltpu.CompilerParams(vmem_limit_bytes=mib * 1024 * 1024),
        cost_estimate=estimate,
    )


def pair_columns(ref, core, pair):
    group = ref.shape[1] // 4
    pieces = []
    start, end = pair * LANES, (pair + 1) * LANES
    if start < group:
        pieces.append(ref[:, core * group + start : core * group + min(end, group)])
    if end > group:
        begin = max(start, group)
        pieces.append(ref[:, (1 + core) * group + begin : (1 + core) * group + end])
    return pieces[0] if len(pieces) == 1 else jnp.concatenate(pieces, axis=1)


def project_kernel(where_ref, mine_ref, other_ref, gain_ref, shift_ref, *rest, first, pairs):
    step = pl.program_id(0)
    if first:
        wq_ref, wk_ref, wv_ref, cos_ref, sin_ref, qkv_ref, normed_t_ref, weight_ref = rest

        @pl.when(step == 0)
        def _():
            for core in range(2):

                @pl.when(where_ref[CORE] == core)
                def _():
                    for part, ref in enumerate((wq_ref, wk_ref, wv_ref)):
                        for pair in range(pairs):
                            start = (3 * pair + part) * LANES
                            weight_ref[:, start : start + LANES] = pair_columns(ref, core, pair)
    else:
        weight_ref, cos_ref, sin_ref, _, _, qkv_ref, normed_t_ref = rest
    values = jnp.where(step == 0, mine_ref[...], other_ref[...]).astype(F32)
    normal, _ = normalize(values)
    normed = (normal * row_vector(gain_ref) + row_vector(shift_ref)).astype(BF16)
    normed_t_ref[...] = normed.T
    cosine, sine = cos_ref[...], sin_ref[...]
    width = 3 * LANES
    for pair in range(pairs):
        out = dot(normed, weight_ref[:, pair * width : (pair + 1) * width])
        for part in range(3):
            piece = out[:, part * LANES : (part + 1) * LANES]
            if part < 2:
                piece = piece * cosine + swap_halves(piece) * sine
                if part == 0:
                    piece = piece * (HD ** (-0.5))
            start = pair * width + part * LANES
            qkv_ref[:, start : start + LANES] = piece.astype(BF16)


def project_call(turn, where, mine, other, gain, shift, weights, tables, previous):
    rows, width = mine.shape
    out_width = 3 * width // 2
    total = 4 * rows
    block = lambda i, w: (2 * i + turn, 0)
    table = pl.BlockSpec((rows, LANES), lambda i, w: (w[SPOT + 2 * i + turn], 0))
    in_specs = [whole((rows, width))] * 2 + [whole((width,))] * 2
    in_specs += [whole(weight.shape) for weight in weights] + [table, table]
    out_specs = [
        pl.BlockSpec((rows, out_width), block),
        pl.BlockSpec((width, rows), lambda i, w: (0, 2 * i + turn)),
    ]
    out_shape = [((total, out_width), BF16), ((width, total), BF16)]
    aliases = {}
    if previous:
        aliases = {1 + len(in_specs): 0, 2 + len(in_specs): 1}
        in_specs += [pl.BlockSpec(memory_space=pl.ANY)] * 2
    else:
        out_specs.append(whole((width, out_width)))
        out_shape.append(((width, out_width), BF16))
    return call(
        functools.partial(project_kernel, first=not previous, pairs=out_width // (3 * LANES)),
        (2,), in_specs, out_specs, out_shape, [],
        SMALL, aliases, 12,
    )(where, mine, other, gain, shift, *weights, *tables, *previous)


def mask_lane(lane, head, keys, bias):
    return jnp.where(lane == (HD if head == 0 else 0), bias, keys)


def only_head(lane, head, values):
    return jnp.where(lane // HD == head, values, jnp.zeros_like(values))


def with_one(lane, head, values):
    one = lane == (HD if head == 0 else 0)
    return jnp.where(one, jnp.ones_like(values), only_head(lane, head, values))


def fill_bias(where_ref, bias_ref):
    rows = bias_ref.shape[0] // 4
    for block in range(4):
        kept = kept_rows(where_ref, block, rows, LANES)
        bias_ref[block * rows : (block + 1) * rows, :] = jnp.where(kept, 0.0, MASKED).astype(BF16)


def attend_kernel(
    where_ref, query_ref, key_ref, value_ref, mine_ref, other_ref, ctx_t_ref, lse_ref,
    bias_ref, ctx_ref, scores_ref, weights_ref, *, tile,
):
    total = query_ref.shape[0]
    lane = lax.broadcasted_iota(jnp.int32, (1, LANES), 1)

    @pl.when(pl.program_id(0) == 0)
    def _():
        fill_bias(where_ref, bias_ref)

    keys = key_ref[...]
    values_t = value_ref[...].T
    keys_aug = [mask_lane(lane, head, keys, bias_ref[...]) for head in range(2)]
    work = [(head, start) for head in range(2) for start in range(0, total, tile)]

    def score(place):
        head, start = work[place]
        queries = with_one(lane, head, query_ref[start : start + tile, :])
        scores_ref[place % 2] = dot_back(keys_aug[head], queries)

    def weigh(place):
        scores = scores_ref[place % 2]
        highest = jnp.max(scores, axis=0, keepdims=True)
        weights = jnp.exp(scores - highest)
        weights_ref[place % 2] = weights.astype(BF16)
        return highest, jnp.sum(weights, axis=0, keepdims=True)

    def attend(place, highest, sums):
        head, start = work[place]
        context = dot(values_t[head * HD : (head + 1) * HD, :], weights_ref[place % 2])
        ctx_ref[head * HD : (head + 1) * HD, start : start + tile] = context / sums
        lse_ref[0, head : head + 1, start : start + tile] = highest + jnp.log(sums)

    score(0)
    before = None
    for place in range(len(work) + 1):
        if place + 1 < len(work):
            score(place + 1)
        if before is not None:
            attend(place - 1, *before)
        if place < len(work):
            before = weigh(place)
    ctx_t_ref[...] = ctx_ref[...].astype(BF16)
    contexts = ctx_ref[...].T.astype(BF16)
    mine_ref[...] = contexts[: total // 2]
    other_ref[...] = contexts[total // 2 :]


def attend_call(where, qkv):
    total, width = qkv.shape
    pairs = width // (3 * LANES)
    width //= 3
    half = total // 2
    tile = half
    column = lambda part: pl.BlockSpec((total, LANES), lambda p, w: (0, 3 * p + part))
    out_column = pl.BlockSpec((half, LANES), lambda p, w: (0, p))
    return call(
        functools.partial(attend_kernel, tile=tile),
        (pairs,),
        [column(0), column(1), column(2)],
        [
            out_column, out_column,
            pl.BlockSpec((LANES, total), lambda p, w: (p, 0)),
            pl.BlockSpec((1, 8, total), lambda p, w: (p, 0, 0)),
        ],
        [((half, width), BF16), ((half, width), BF16), ((width, total), BF16), ((pairs, 8, total), F32)],
        [
            pltpu.VMEM((total, LANES), BF16),
            pltpu.VMEM((LANES, total), F32),
            pltpu.VMEM((2, total, tile), F32),
            pltpu.VMEM((2, total, tile), BF16),
        ],
        SMALL, mib=16,
    )(where, qkv, qkv, qkv)


def stack_rows(refs):
    return jnp.concatenate([ref[0] for ref in refs], axis=0)


def residual_kernel(
    where_ref, keep_ref, recv_ref, mine_ref, got_ref, w0_ref, w1_ref, w2_ref, w3_ref,
    gain_ref, shift_ref, res_ref, normed_ref,
):
    step = pl.program_id(0)
    values = jnp.where(step == 0, keep_ref[...], recv_ref[...]).astype(F32)
    attended = dot(mine_ref[...], stack_rows((w0_ref, w1_ref)))
    attended += dot(got_ref[...], stack_rows((w2_ref, w3_ref)))
    residual = values + attended
    res_ref[...] = residual
    normal, _ = normalize(residual)
    normed_ref[...] = (normal * row_vector(gain_ref) + row_vector(shift_ref)).astype(BF16)


def out_weight_specs(group, width):
    places = (
        lambda w: w[CORE],
        lambda w: 2 + w[CORE],
        lambda w: 1 - w[CORE],
        lambda w: 3 - w[CORE],
    )
    return [pl.BlockSpec((1, group, width), lambda i, w, at=at: (at(w), 0, 0)) for at in places]


def residual_call(where, keep, recv, ctx_mine, ctx_got, w_out, gain, shift):
    rows, width = keep.shape
    heads = ctx_mine.shape[1]
    row = lambda lanes: pl.BlockSpec((rows, lanes), lambda i, w: (i, 0))
    return call(
        residual_kernel,
        (2,),
        [whole((rows, width))] * 2 + [row(heads)] * 2
        + out_weight_specs(heads // 2, width) + [whole((width,))] * 2,
        [row(width)] * 2,
        [((2 * rows, width), F32), ((2 * rows, width), BF16)],
        [],
        SMALL, mib=10,
    )(where, keep, recv, ctx_mine, ctx_got, w_out, w_out, w_out, w_out, gain, shift)


def gelu_both(values):
    root = 0.7978845608028654
    bend = (root * 0.044715) * (values * values)
    half = 0.5 * jnp.tanh(values * (root + bend)) + 0.5
    steep = values * (2.0 * root + 6.0 * bend)
    return values * half, half * ((1.0 - half) * steep + 1.0)


def fill_cotangent(where_ref, refs, grad_ref):
    rows, width = refs[0].shape
    for place, ref in enumerate(refs):
        kept = kept_rows(where_ref, place, rows, width)
        grad_ref[place * rows : (place + 1) * rows, :] = jnp.where(kept, ref[...], jnp.zeros_like(ref))


def feed_kernel(
    where_ref,
    normed_m_ref, normed_o_ref, cot0_ref, cot1_ref, cot2_ref, cot3_ref, up_ref, down_ref,
    up_send_ref, up_keep_ref, send_ref, keep_ref, active_ref, back_m_ref, back_o_ref,
    normed_ref, grad_ref, normed_t_ref, grad_t_ref, hidden_ref, before_ref, up_before_ref,
):
    step = pl.program_id(0)
    half, width = normed_m_ref.shape
    block = up_ref.shape[1]

    @pl.when(step == 0)
    def _():
        normed_ref[:half, :] = normed_m_ref[...]
        normed_ref[half:, :] = normed_o_ref[...]
        fill_cotangent(where_ref, (cot0_ref, cot1_ref, cot2_ref, cot3_ref), grad_ref)
        normed_t_ref[...] = normed_ref[...].T
        grad_t_ref[...] = grad_ref[...].T

    hidden = dot(normed_ref[...], up_ref[...])
    active, slope = gelu_both(hidden)
    active_ref[...] = active.astype(BF16)
    grad_active = dot_back(grad_ref[...], down_ref[...])
    hidden_ref[...] = (grad_active * slope).astype(BF16)
    up_grad = dot(normed_t_ref[...], hidden_ref[...]).astype(BF16)
    down_grad = dot(grad_t_ref[...], active_ref[...]).astype(BF16)
    part = block // 2
    for side in range(2):
        piece = down_grad[:, side * part : (side + 1) * part]

        @pl.when(where_ref[SIDE] == side)
        def _():
            keep_ref[0] = piece

        @pl.when(where_ref[SIDE] != side)
        def _():
            send_ref[0] = piece

    @pl.when(step == 0)
    def _():
        up_send_ref[...] = up_grad
        before_ref[...] = hidden_ref[...]
        up_before_ref[...] = up_ref[...]

    @pl.when(step == 1)
    def _():
        up_keep_ref[...] = up_grad
        back = dot_back(before_ref[...], up_before_ref[...]) + dot_back(hidden_ref[...], up_ref[...])
        back_m_ref[...] = back[:half]
        back_o_ref[...] = back[half:].astype(BF16)


def feed_high(last, w):
    return jnp.where(last, w[ROW], 1 - w[ROW])


def feed_call(where, normed_m, normed_o, cotangents, w_up, w_down):
    half, width = normed_m.shape
    total = 2 * half
    block = w_up.shape[1] // 4
    part = block // 2
    token = whole((half, width))
    piece = pl.BlockSpec((1, width, part), lambda j, w: (j, 0, 0))
    return call(
        feed_kernel,
        (2,),
        [token, token]
        + [whole((half // 2, width))] * 4
        + [
            pl.BlockSpec((width, block), lambda j, w: (0, 2 * feed_high(j == 1, w) + w[CORE])),
            pl.BlockSpec((block, width), lambda j, w: (2 * feed_high(j == 1, w) + w[CORE], 0)),
        ],
        [
            whole((width, block)), whole((width, block)), piece, piece,
            pl.BlockSpec((total, block), lambda j, w: (0, j)),
            token, token,
        ],
        [
            ((width, block), BF16),
            ((width, block), BF16),
            ((2, width, part), BF16),
            ((2, width, part), BF16),
            ((total, 2 * block), BF16),
            ((half, width), F32),
            ((half, width), BF16),
        ],
        [
            pltpu.VMEM((total, width), BF16),
            pltpu.VMEM((total, width), BF16),
            pltpu.VMEM((width, total), BF16),
            pltpu.VMEM((width, total), BF16),
            pltpu.VMEM((total, block), BF16),
            pltpu.VMEM((total, block), BF16),
            pltpu.VMEM((width, block), BF16),
        ],
        SMALL, mib=24,
    )(where, normed_m, normed_o, *cotangents, w_up, w_down)


def feed_out_kernel(where_ref, active_ref, down0_ref, down1_ref, mine_ref, *other_refs):
    block = down0_ref.shape[0]
    out = dot(active_ref[:, :block], down0_ref[...]) + dot(active_ref[:, block:], down1_ref[...])
    size = other_refs[0].shape[0]

    @pl.when(pl.program_id(0) == 0)
    def _():
        for part, ref in enumerate(other_refs):
            ref[...] = out[part * size : (part + 1) * size].astype(BF16)

    @pl.when(pl.program_id(0) == 1)
    def _():
        mine_ref[...] = out


def feed_out_call(where, active, w_down):
    total, block = active.shape
    block //= 2
    width = w_down.shape[1]
    half = total // 2
    row = pl.BlockSpec((half, 2 * block), lambda i, w: (1 - i, 0))
    down = [
        pl.BlockSpec((block, width), lambda i, w, last=last: (2 * feed_high(last, w) + w[CORE], 0))
        for last in (False, True)
    ]
    return call(
        feed_out_kernel,
        (2,),
        [row, *down],
        [whole((half, width))] + [whole((half // 4, width))] * 4,
        [((half, width), F32)] + [((half // 4, width), BF16)] * 4,
        [], SMALL, mib=12,
    )(where, active, w_down, w_down)


def by_step(refs, step):
    count = len(refs) // 2
    low = jnp.concatenate([ref[...] for ref in refs[:count]], axis=0)
    high = jnp.concatenate([ref[...] for ref in refs[count:]], axis=0)
    return jnp.where(step == 0, high, low).astype(F32)


def output_kernel(where_ref, res_ref, out_ref, got0_ref, got1_ref, got2_ref, got3_ref, send_ref, keep_ref):
    step = pl.program_id(0)
    output = res_ref[...] + out_ref[...] + by_step((got0_ref, got1_ref, got2_ref, got3_ref), step)
    kept = kept_rows(where_ref, 1 - step, *output.shape)
    output = jnp.where(kept, output, jnp.zeros_like(output)).astype(BF16)

    @pl.when(step == 0)
    def _():
        send_ref[...] = output

    @pl.when(step == 1)
    def _():
        keep_ref[0] = output


def output_call(where, residual, out, got):
    half, width = residual.shape
    rows = half // 2
    row = pl.BlockSpec((rows, width), lambda i, w: (1 - i, 0))
    return call(
        output_kernel,
        (2,),
        [row] * 2 + [whole((rows // 2, width))] * 4,
        [whole((rows, width)), pl.BlockSpec((1, rows, width), lambda i, w: (w[ROW], 0, 0))],
        [((rows, width), BF16), ((2, rows, width), BF16)],
        [], SMALL, mib=8,
    )(where, residual, out, *got)


def add_sums(sums_ref, step, row, gains, shifts):
    @pl.when(step == 0)
    def _():
        sums_ref[...] = jnp.zeros_like(sums_ref)

    sums_ref[row : row + 1, :] += gains
    sums_ref[row + 1 : row + 2, :] += shifts


def middle_kernel(
    where_ref,
    res_ref, back_ref, back_got_ref, cot0_ref, cot1_ref, gain_ref, grad_low_ref, sums_ref,
):
    step = pl.program_id(0)
    residual = res_ref[...]
    kept = kept_rows(where_ref, step, *residual.shape)
    normal, inverse = normalize(residual)
    back = back_ref[...] + back_got_ref[...].astype(F32)
    gains = jnp.sum(back * normal, axis=0, keepdims=True)
    shifts = jnp.sum(back, axis=0, keepdims=True)

    add_sums(sums_ref, step, 2, gains, shifts)
    cotangent = jnp.where(step == 0, cot0_ref[...], cot1_ref[...]).astype(F32)
    cotangent = jnp.where(kept, cotangent, jnp.zeros_like(cotangent))
    grad = cotangent + norm_back(back, row_vector(gain_ref), normal, inverse)
    grad_low_ref[...] = grad.astype(BF16)


def middle_call(where, residual, back_m, back_got, cot_keep, cot_recv, gain):
    half, width = residual.shape
    rows = half // 2
    row = pl.BlockSpec((rows, width), lambda i, w: (i, 0))
    return call(
        middle_kernel,
        (2,),
        [row] * 3 + [whole((rows, width))] * 2 + [whole((width,))],
        [row, whole((8, width))],
        [((half, width), BF16), ((8, width), F32)],
        [], SMALL, mib=8,
    )(where, residual, back_m, back_got, cot_keep, cot_recv, gain)


def piece_order(where_ref):
    side, row = where_ref[SIDE], where_ref[ROW]
    order = []
    for kept in (0, 1):
        mine = side if kept else 1 - side
        order += [8 * high + 2 * mine + half for high in (0, 1) for half in (0, 1)]
    for kept in (0, 1):
        mine = row if kept else 1 - row
        order += [8 * high + 4 + 2 * one + mine for high in (0, 1) for one in (0, 1)]
    return order


def attend_back_kernel(
    where_ref,
    query_ref, key_ref, value_ref, ctx_ref, grad_m_ref, grad_o_ref, w0_ref, w1_ref, lse_ref,
    ctx_mine_hbm, ctx_got_hbm, cos_hbm, sin_hbm, normed_t_hbm, *rest,
    score_scale, first, last,
):
    if last:
        rest = rest[4:]
    out_refs, grads_ref = rest[:4], rest[4]
    rest = rest[5:]
    bias_ref, grad_ref, columns_ref, dqt_ref, dk_acc, dv_acc, qkv_ref, own_ref = rest[:8]
    ctx_mine_ref, ctx_got_ref, cos_ref, sin_ref, normed_t_ref, semaphores = rest[8:]
    step = pl.program_id(0)
    total = query_ref.shape[0]
    half = total // 2
    model = grad_m_ref.shape[1]
    lane = lax.broadcasted_iota(jnp.int32, (1, LANES), 1)
    unit = model // 16
    group = model // 4
    rows = total // 4
    late = [(ctx_mine_hbm, ctx_mine_ref), (ctx_got_hbm, ctx_got_ref), (normed_t_hbm, normed_t_ref)]
    for source, target in ((cos_hbm, cos_ref), (sin_hbm, sin_ref)):
        for block in range(4):
            begin = pl.multiple_of(where_ref[SPOT + block] * rows, rows)
            late.append((source.at[pl.ds(begin, rows)], target.at[pl.ds(block * rows, rows)]))

    def copies():
        return [
            pltpu.make_async_copy(source, target, semaphores.at[k])
            for k, (source, target) in enumerate(late)
        ]

    @pl.when(step == 0)
    def _():
        for copy in copies():
            copy.start()
        fill_bias(where_ref, bias_ref)
        grad_ref[:half, :] = grad_m_ref[...]
        grad_ref[half:, :] = grad_o_ref[...]

    for place, pair in enumerate(first):
        for core in range(2):

            @pl.when((step == place) & (where_ref[CORE] == core))
            def _():
                columns_ref[...] = pair_columns(grad_ref, core, pair)

    wout = jnp.concatenate([w0_ref[...], w1_ref[...]], axis=0)
    gctx = dot_back(grad_ref[...], wout).astype(BF16)
    products = gctx.astype(F32).T * ctx_ref[...].astype(F32)
    keys = key_ref[...]
    keys_t = keys.T
    values = value_ref[...]
    queries = query_ref[...]
    for head in range(2):
        key_aug = mask_lane(lane, head, keys, bias_ref[...])
        delta = jnp.sum(products[head * HD : (head + 1) * HD, :], axis=0, keepdims=True)
        scores = dot_back(key_aug, with_one(lane, head, queries))
        weights = jnp.exp(scores - lse_ref[0, head : head + 1, :])
        grads = only_head(lane, head, gctx)
        grad_weights = dot_back(values, grads)
        grad_scores = (weights * (grad_weights - delta)).astype(BF16)
        dv = dot(weights.astype(BF16), grads)
        dk = dot(grad_scores, only_head(lane, head, queries))
        dqt_ref[head * HD : (head + 1) * HD, :] = dot(
            keys_t[head * HD : (head + 1) * HD, :], grad_scores
        )
        if head == 0:
            dv_acc[...] = dv
            dk_acc[...] = dk
        else:
            dv_acc[...] += dv
            dk_acc[...] += dk

    @pl.when(step == 0)
    def _():
        for copy in copies():
            copy.wait()

    cosine, sine = cos_ref[...], sin_ref[...]
    dq = dqt_ref[...].T * score_scale
    dk = dk_acc[...]
    dq = (dq * cosine - swap_halves(dq) * sine).astype(BF16)
    dk = (dk * cosine - swap_halves(dk) * sine).astype(BF16)
    grads = jnp.concatenate([dq, dk, dv_acc[...].astype(BF16)], axis=1)
    qkv_ref[...] = dot(normed_t_ref[...], grads).astype(BF16)
    columns = columns_ref[...]
    turned = jnp.concatenate([columns[half:], columns[:half]], axis=0)
    own_ref[0] = dot(ctx_mine_ref[...], columns).astype(BF16)
    own_ref[1] = dot(ctx_got_ref[...], turned).astype(BF16)
    for place, source in enumerate(piece_order(where_ref)):
        ref = out_refs[place // 4]
        span = slice(place % 4 * unit, (place % 4 + 1) * unit)
        ref[span, : 3 * LANES] = qkv_ref[pl.ds(pl.multiple_of(source * unit, unit), unit), :]
        block = source // 4
        other = jnp.where(block % 2 == where_ref[CORE], 0, 1)
        inside = pl.multiple_of((block // 2) * group + (source % 4) * unit, unit)
        ref[span, 3 * LANES :] = own_ref[other, pl.ds(inside, unit), :]
    grads_ref[...] = grads


def normed_grad_kernel(where_ref, early_ref, late_ref, weight_ref, mine_ref, *other_refs):
    split = early_ref.shape[1]
    back = dot_back(early_ref[...], weight_ref[:, :split])
    back += dot_back(late_ref[...], weight_ref[:, split:])
    half = mine_ref.shape[0]
    size = half // len(other_refs)
    mine_ref[...] = back[:half]
    for part, ref in enumerate(other_refs):
        ref[...] = back[half + part * size : half + (part + 1) * size].astype(BF16)


def normed_grad_call(where, early, late, weight):
    half, width = early.shape[0] // 2, weight.shape[0]
    return stage_call(
        normed_grad_kernel, where, (early, late, weight),
        [((half, width), F32)] + [((half // 2, width), BF16)] * 2,
    )


def attend_back_call(
    pairs, where, qkv, ctx_t, ctx_got_t, grad_m, grad_o, w_out, lse, tables, normed_t,
    pieces=(),
):
    total, width = qkv.shape
    width //= 3
    half, model = grad_m.shape
    quarter = model // 4
    last = bool(pieces)
    begin = pairs[0]
    column = lambda part: pl.BlockSpec((total, LANES), lambda i, w: (0, 3 * (begin + i) + part))

    def head_rows(which):
        per = width // HD // 2

        def at(i, w):
            head = 2 * (begin + i) + which
            return (head // per * 2 * per + w[CORE] * per + head % per, 0)

        return pl.BlockSpec((HD, model), at)

    in_specs = [
        column(0), column(1), column(2),
        pl.BlockSpec((LANES, total), lambda i, w: (begin + i, 0)),
        whole((half, model)), whole((half, model)),
        head_rows(0), head_rows(1),
        pl.BlockSpec((1, 8, total), lambda i, w: (begin + i, 0, 0)),
    ]
    in_specs += [pl.BlockSpec(memory_space=pl.ANY)] * 5
    args = [
        qkv, qkv, qkv, ctx_t, grad_m, grad_o, w_out, w_out, lse, ctx_t, ctx_got_t, *tables, normed_t,
    ]
    out_specs = [pl.BlockSpec((quarter, 4 * LANES), lambda i, w: (0, begin + i))] * 4
    out_shape = [((quarter, 4 * width), BF16)] * 4
    aliases = {}
    if last:
        aliases = {1 + len(args) + k: k for k in range(4)}
        in_specs += [pl.BlockSpec(memory_space=pl.ANY)] * 4
        args += list(pieces)
    out_specs.append(pl.BlockSpec((total, 3 * LANES), lambda i, w: (0, i)))
    out_shape.append(((total, 3 * LANES * len(pairs)), BF16))
    return call(
        functools.partial(attend_back_kernel, score_scale=HD ** (-0.5), first=pairs, last=last),
        (len(pairs),), in_specs, out_specs, out_shape,
        [
            pltpu.VMEM((total, LANES), BF16),
            pltpu.VMEM((total, model), BF16),
            pltpu.VMEM((total, LANES), BF16),
            pltpu.VMEM((LANES, total), F32),
            pltpu.VMEM((total, LANES), F32),
            pltpu.VMEM((total, LANES), F32),
            pltpu.VMEM((model, 3 * LANES), BF16),
            pltpu.VMEM((2, width, LANES), BF16),
            pltpu.VMEM((width, total), BF16),
            pltpu.VMEM((width, total), BF16),
            pltpu.VMEM((total, LANES), F32),
            pltpu.VMEM((total, LANES), F32),
            pltpu.VMEM((model, total), BF16),
            pltpu.SemaphoreType.DMA((11,)),
        ],
        SMALL, aliases, mib=26,
    )(where, *args)


def stage_one_kernel(
    where_ref, up_keep, up_got, down_keep, down_got, up_sent, up_kept, down_sent, down_kept
):
    side, row = where_ref[SIDE], where_ref[ROW]
    unit = up_keep.shape[0] // 8
    for one in range(4):
        to = slice(one * unit, (one + 1) * unit)
        for out, mine in ((up_sent, 1 - side), (up_kept, side)):
            span = pl.ds(pl.multiple_of((2 * one + mine) * unit, unit), unit)
            out[to, :] = added(up_keep, up_got, span).astype(BF16)
    size = down_keep.shape[1] // 2
    for place, block in enumerate((1 - row, row)):
        for out, mine in ((down_sent, 1 - row), (down_kept, row)):
            span = pl.ds(pl.multiple_of(mine * size, size), size)
            out[block] = added(down_keep.at[place], down_got.at[place], span).astype(BF16)


def stage_one_call(where, up_keep, up_got, down_keep, down_got):
    rows, width = up_keep.shape
    _, size, lanes = down_keep.shape
    return stage_call(
        stage_one_kernel, where, (up_keep, up_got, down_keep, down_got),
        [((rows // 2, width), BF16)] * 2 + [((2, size // 2, lanes), BF16)] * 2,
    )


def added(one, two, span):
    return one[span, :].astype(F32) + two[span, :].astype(F32)


def stage_two_kernel(where_ref, up_kept, up_got, down_kept, down_got, sent, kept):
    unit = kept.shape[1] // 2
    size, lanes = down_kept.shape[1] // 2, down_kept.shape[2]
    low = where_ref[HIGH] % 2
    for high in range(2):
        for out, which in ((sent, 1 - low), (kept, low)):
            span = pl.ds(pl.multiple_of((2 * high + which) * unit, unit), unit)
            out[high, :unit, :] = added(up_kept, up_got, span).astype(BF16)
            for fold in range(size // unit):
                span = pl.ds(pl.multiple_of(which * size + fold * unit, unit), unit)
                values = added(down_kept.at[high], down_got.at[high], span)
                out[high, unit:, fold * lanes : (fold + 1) * lanes] = values.astype(BF16)


def halve_kernel(where_ref, before, got, sent, kept):
    high = where_ref[HIGH] // 2
    for out, which in ((sent, 1 - high), (kept, high)):
        out[...] = (before[which].astype(F32) + got[which].astype(F32)).astype(out.dtype)


def halve_call(where, before, got):
    shape = before.shape[1:]
    return stage_call(halve_kernel, where, (before, got), [(shape, BF16), (shape, F32)])


def stage_call(kernel, where, inputs, out_shape, mib=8):
    return call(
        kernel, (1,), [whole(one.shape) for one in inputs], [whole(shape) for shape, _ in out_shape],
        out_shape, [], SMALL, mib=mib,
    )(where, *inputs)


def stage_two_call(where, up_kept, up_got, down_kept, down_got):
    rows, width = up_kept.shape
    part = (2, rows // 2, width)
    return stage_call(
        stage_two_kernel, where, (up_kept, up_got, down_kept, down_got), [(part, BF16)] * 2
    )


def feed_sum_kernel(where_ref, own, got, up, down):
    unit, lanes = up.shape[0], down.shape[1]
    summed = own[...] + got[...].astype(F32)
    up[...] = summed[:unit]
    for fold in range(up.shape[1] // lanes):
        values = summed[unit:, fold * lanes : (fold + 1) * lanes]
        down[fold * unit : (fold + 1) * unit, :] = values.astype(BF16)


def feed_sum_call(where, own, got, lanes):
    rows, width = own.shape
    unit = rows // 2
    return stage_call(
        feed_sum_kernel, where, (own, got), [((unit, width), F32), ((unit * width // lanes, lanes), BF16)]
    )


def stage_three_kernel(where_ref, *refs):
    first_keep, first_got, second_keep, second_got, sums, sums_got = refs[:6]
    first_sent, first_kept, second_sent, second_kept = refs[6:]
    side, row = where_ref[SIDE], where_ref[ROW]
    unit = first_sent.shape[0] // 2
    for keep, got, mine, sent, kept in (
        (first_keep, first_got, row, first_sent, first_kept),
        (second_keep, second_got, side, second_sent, second_kept),
    ):
        for high in range(2):
            to = slice(high * unit, (high + 1) * unit)
            for out, which in ((sent, 1 - mine), (kept, mine)):
                span = pl.ds(pl.multiple_of((2 * high + which) * unit, unit), unit)
                out[to, :] = added(keep, got, span).astype(out.dtype)
    summed = sums[...] + sums_got[...]
    width = summed.shape[1]
    for out in (second_sent, second_kept):
        out[2 * unit :, :] = jnp.zeros_like(out[2 * unit :, :])
        out[2 * unit :, :width] = summed.astype(out.dtype)


def stage_three_call(where, first_keep, first_got, second_keep, second_got, sums, sums_got):
    rows, lanes = first_keep.shape[0] // 2, first_keep.shape[1]
    more = sums.shape[0]
    return stage_call(
        stage_three_kernel, where, (first_keep, first_got, second_keep, second_got, sums, sums_got),
        [
            ((rows, lanes), BF16), ((rows, lanes), F32),
            ((rows + more, lanes), BF16), ((rows + more, lanes), F32),
        ],
    )


def stage_four_kernel(where_ref, first_kept, first_got, second_kept, second_got, sent0, sent1, kept):
    rows = first_kept.shape[0]
    unit = rows // 2
    low = where_ref[HIGH] % 2
    sums = added(second_kept, second_got, slice(rows, None))
    for which, (before, got) in enumerate(((first_kept, first_got), (second_kept, second_got))):

        @pl.when(low == which)
        def _():
            kept[:rows, :] = added(before, got, slice(0, rows))

        @pl.when(low != which)
        def _():
            sent0[...] = added(before, got, slice(0, unit)).astype(BF16)
            sent1[:unit, :] = added(before, got, slice(unit, rows)).astype(BF16)

    kept[rows:, :] = sums
    sent1[unit:, :] = sums.astype(BF16)


def stage_four_call(where, first_kept, first_got, second_kept, second_got):
    rows, lanes = first_kept.shape
    more = second_kept.shape[0] - rows
    return stage_call(
        stage_four_kernel, where, (first_kept, first_got, second_kept, second_got),
        [((rows // 2, lanes), BF16), ((rows // 2 + more, lanes), BF16), ((rows + more, lanes), F32)],
    )


def halve_rows_kernel(where_ref, before, got0, got1, sent, kept):
    unit = got0.shape[0]
    high = where_ref[HIGH] // 2
    for which, got in enumerate((got0, got1)):
        values = before[which * unit : (which + 1) * unit, :] + got[:unit, :].astype(F32)

        @pl.when(high == which)
        def _():
            kept[:unit, :] = values

        @pl.when(high != which)
        def _():
            sent[:unit, :] = values.astype(BF16)

    sums = before[2 * unit :, :] + got1[unit:, :].astype(F32)
    kept[unit:, :] = sums
    sent[unit:, :] = sums.astype(BF16)


def halve_rows_call(where, before, got0, got1):
    shape = got1.shape
    return stage_call(halve_rows_kernel, where, (before, got0, got1), [(shape, BF16), (shape, F32)])


def stage_five_kernel(where_ref, own, got, sent, mine, *, pairs):
    summed = own[...] + got[...].astype(F32)
    width = mine.shape[1]
    unit = own.shape[0] - 8
    group = width // 4
    blocks = ([], [])
    for part in range(4):
        starts = [(4 * pair + part) * LANES for pair in range(pairs)]
        columns = jnp.concatenate([summed[:unit, at : at + LANES] for at in starts], axis=1)
        blocks[0].append(columns[:, :group])
        blocks[1].append(columns[:, group:])
    for row in range(2):

        @pl.when(where_ref[ROW] == row)
        def _():
            mine[:unit, :] = jnp.concatenate(blocks[row], axis=1)
            sent[:unit, :] = jnp.concatenate(blocks[1 - row], axis=1).astype(BF16)

    mine[unit:, :] = summed[unit:, :width]
    sent[unit:, :] = summed[unit:, :width].astype(BF16)


def stage_five_call(where, own, got, pairs):
    rows, lanes = own.shape
    shape = (rows, lanes // pairs // LANES * HD * pairs)
    return stage_call(
        functools.partial(stage_five_kernel, pairs=pairs), where, (own, got), [(shape, BF16), (shape, F32)]
    )


def stage_six_kernel(where_ref, mine, other, down_got, *outs):
    weights, sums, down = outs[:4], outs[4:8], outs[8]
    unit = mine.shape[0] - 8
    group = weights[0].shape[1]
    row = where_ref[ROW]
    for ref, place in ((mine, row), (other, 1 - row)):
        span = pl.ds(pl.multiple_of(place * unit, unit), unit)
        for part, out in enumerate(weights):
            out[span, :] = ref[:unit, part * group : (part + 1) * group].astype(F32)
    summed = added(mine, other, slice(unit, None))
    for which, out in enumerate(sums):
        out[...] = summed[which : which + 1, :].reshape(out.shape)
    down[...] = down_got[...].astype(F32)


def stage_six_call(where, mine, other, down_got):
    rows, width = mine.shape
    unit, group = rows - 8, width // 4
    rows, lanes = down_got.shape
    return stage_call(
        stage_six_kernel, where, (mine, other, down_got),
        [((2 * unit, group), F32)] * 4 + [((width,), F32)] * 4 + [((rows, lanes), F32)],
    )


def tokens_grad_kernel(
    where_ref,
    keep_ref, recv_ref, back_ref, *refs
):
    *got_refs, grad_res_ref, gain_ref, keep_out_ref, send_out_ref, sums_ref = refs
    step = pl.program_id(0)
    values = jnp.where(step == 0, recv_ref[...], keep_ref[...]).astype(F32)
    normal, inverse = normalize(values)
    back = back_ref[...] + by_step(got_refs, step)
    gains = jnp.sum(back * normal, axis=0, keepdims=True)
    shifts = jnp.sum(back, axis=0, keepdims=True)
    grad = (grad_res_ref[...].astype(F32) + norm_back(back, row_vector(gain_ref), normal, inverse)).astype(BF16)

    add_sums(sums_ref, step, 0, gains, shifts)

    @pl.when(step == 0)
    def _():
        send_out_ref[...] = grad

    @pl.when(step == 1)
    def _():
        keep_out_ref[0] = grad


def tokens_grad_call(where, keep, recv, back, got, grad_res, gain):
    rows, width = keep.shape
    row = pl.BlockSpec((rows, width), lambda i, w: (1 - i, 0))
    return call(
        tokens_grad_kernel,
        (2,),
        [whole((rows, width))] * 2 + [row] + [whole(one.shape) for one in got] + [row, whole((width,))],
        [
            pl.BlockSpec((1, rows, width), lambda i, w: (w[ROW], 0, 0)),
            whole((rows, width)),
            whole((8, width)),
        ],
        [((2, rows, width), BF16), ((rows, width), BF16), ((8, width), F32)],
        [],
        SMALL, mib=8,
    )(where, keep, recv, back, *got, grad_res, gain)


def local(
    tokens, gain_one, shift_one, w_query, w_key, w_value, w_out, gain_two, shift_two, w_up, w_down,
    cotangent, lengths,
):
    row_count, piece, width = tokens.shape
    n_dp = lax.axis_size("dp")
    n_seq = lax.axis_size("seq")
    count = n_dp // 4
    place = lax.axis_index("seq")
    core, row = place % 2, place // 2
    data = lax.axis_index("dp")
    high = data // count
    side = (data // (count // 2)) % 2
    total = n_seq * piece
    group = width // n_seq

    tok_send, tokens = together(pick(tokens, 1 - row), tokens)
    tok_recv = swap(tok_send, "seq", 2)
    tok_keep = pick(tokens, row)
    tok_keep_o = swap(tok_keep, "seq", 1)
    cot_keep = pick(cotangent, row)
    cot_recv = swap(pick(cotangent, 1 - row), "seq", 2)

    where = jnp.stack(
        [
            core, row, side, pick(lengths, row),
            2 * row + core, 2 * (1 - row) + core, 2 * row + 1 - core, 2 * (1 - row) + 1 - core,
            high,
        ]
    ).astype(jnp.int32)
    tables = tuple(jnp.asarray(table) for table in rotary_tables(total))
    out_blocks = w_out.reshape(n_seq, group, width)

    qkv, normed_t, w_qkv = project_call(
        0, where, tok_keep, tok_keep_o, gain_one, shift_one, (w_query, w_key, w_value), tables, ()
    )
    tok_recv, qkv, normed_t = together(tok_recv, qkv, normed_t)
    tok_recv_o = swap(tok_recv, "seq", 1)
    qkv, normed_t = project_call(
        1, where, tok_recv, tok_recv_o, gain_one, shift_one, (w_qkv,), tables, (qkv, normed_t)
    )
    ctx_m, ctx_o, ctx_t, lse = attend_call(where, qkv)
    cot_keep_o = swap(cot_keep, "seq", 1)
    ctx_m, ctx_o, ctx_t, cot_recv, cot_keep_o = together(ctx_m, ctx_o, ctx_t, cot_recv, cot_keep_o)
    cotangents = (cot_keep, cot_recv, cot_keep_o, swap(cot_recv, "seq", 1))
    ctx_got = swap(ctx_o, "seq", 1)
    residual, normed_two = residual_call(
        where, tok_keep, tok_recv, ctx_m, ctx_got, out_blocks, gain_two, shift_two
    )
    normed_two_o = swap(normed_two, "seq", 1)
    ctx_got_t = swap(ctx_t, "seq", 1)
    up_send, up_keep, down_send, down_keep, active, back_m, back_o = feed_call(
        where, normed_two, normed_two_o, cotangents, w_up, w_down
    )
    up_got = swap(up_send, "seq", 2)
    down_got = swap(down_send, "dp", count // 2)
    back_got = swap(back_o, "seq", 1)
    grad_low, sums_two = middle_call(where, residual, back_m, back_got, cot_keep, cot_recv, gain_two)
    grad_low_o = swap(grad_low, "seq", 1)

    block_rows = width // n_dp

    pairs = qkv.shape[1] // (3 * LANES)

    def upper(up, down):
        bit = count // 4
        up = up.reshape(4, count // 2, block_rows, width).astype(F32)
        down = down.reshape(4, group, -1).astype(F32)
        while bit > 0:
            mine = (data // bit) % 2
            size, lanes = up.shape[1] // 2, down.shape[2] // 2
            sent = lax.dynamic_slice_in_dim(up, (1 - mine) * size, size, 1).astype(BF16)
            up = lax.dynamic_slice_in_dim(up, mine * size, size, 1) + swap(sent, "dp", bit)
            sent = lax.dynamic_slice_in_dim(down, (1 - mine) * lanes, lanes, 2).astype(BF16)
            down = lax.dynamic_slice_in_dim(down, mine * lanes, lanes, 2) + swap(sent, "dp", bit)
            bit //= 2
        up = up.reshape(4, block_rows, width)
        folds = width // down.shape[2]
        size = group // folds
        down = jnp.concatenate([down[:, k * size : (k + 1) * size] for k in range(folds)], axis=2)
        both = jnp.concatenate([up, down], axis=1).astype(BF16)
        both = both.reshape((2, 2) + both.shape[1:])
        return pick(both, 1 - high % 2, 1), pick(both, high % 2, 1)

    def halved(before, got):
        if count == 2:
            return halve_call(where, before, got)
        both = before.astype(F32) + got.astype(F32)
        return pick(both, 1 - high // 2).astype(BF16), pick(both, high // 2)

    def feed_sums(own, got):
        lanes = w_down.shape[0] // n_dp
        if count == 2:
            return feed_sum_call(where, own, got, lanes)
        own = own + got.astype(F32)
        up, down = own[:block_rows], own[block_rows:].astype(BF16)
        down = jnp.concatenate([down[:, k * lanes : (k + 1) * lanes] for k in range(width // lanes)])
        return up, down

    def exchanged(values):
        perm = []
        for d in range(n_dp):
            for s in range(n_seq):
                second_bit = (d // count) % 2
                to_d = d + (s % 2 - second_bit) * count
                to_s = s - s % 2 + second_bit
                perm.append((d * n_seq + s, to_d * n_seq + to_s))
        return lax.ppermute(values, ("dp", "seq"), perm)

    inner = count // 2
    attention = (where, qkv, ctx_t, ctx_got_t, grad_low, grad_low_o, w_out, lse, tables, normed_t)
    *first_pieces, early = attend_back_call(tuple(range(pairs - 1)), *attention)
    active, early = together(active, early)
    out_m, *out_o = feed_out_call(where, active, w_down)
    up_got, down_got, early, out_o = together(up_got, down_got, early, out_o)
    up_sent, up_kept, down_sent, down_kept = stage_one_call(where, up_keep, up_got, down_keep, down_got)
    up_sent, down_sent, early = together(up_sent, down_sent, early)
    up_got2 = swap(up_sent, "dp", inner)
    down_got2 = swap(down_sent, "seq", 2)
    *pieces, late = attend_back_call((pairs - 1,), *attention, first_pieces)
    pieces, late = together(pieces, late)
    last_got = (swap(pieces[0], "dp", inner), swap(pieces[2], "seq", 2))
    normed_m, *normed_o = normed_grad_call(where, early, late, w_qkv)
    normed_o, up_got2, down_got2 = together(normed_o, up_got2, down_got2)
    normed_got = [swap(one, "seq", 1) for one in normed_o]
    if count == 2:
        feed_sent, feed_kept = stage_two_call(where, up_kept, up_got2, down_kept, down_got2)
    else:
        feed_sent, feed_kept = upper(
            up_kept.astype(F32) + up_got2.astype(F32), down_kept.astype(F32) + down_got2.astype(F32)
        )
    feed_sent, normed_m = together(feed_sent, normed_m)
    feed_got = swap(feed_sent, "dp", count)
    tok_buf, tok_send, sums_one = tokens_grad_call(
        where, tok_keep, tok_recv, normed_m, normed_got, grad_low, gain_one
    )

    sums = sums_one + sums_two
    sums_got = swap(sums, "seq", 1)
    if count == 2:
        last_got, tok_send, sums_got = together(last_got, tok_send, sums_got)
        sent_first, kept_first, sent_second, kept_second = stage_three_call(
            where, pieces[1], last_got[0], pieces[3], last_got[1], sums, sums_got
        )
        sent_first, sent_second, tok_send = together(sent_first, sent_second, tok_send)
        got_first = swap(sent_first, "seq", 2)
        got_second = swap(sent_second, "dp", inner)
        feed_sent, feed_own = halved(feed_kept, feed_got)
        feed_got = swap(feed_sent, "dp", 2 * count)
        tok_back = swap(tok_send, "seq", 2)
        out_got = [swap(one, "seq", 1) for one in out_o]
        got_first, got_second, feed_sent = together(got_first, got_second, feed_sent)
        *sent, kept = stage_four_call(where, kept_first, got_first, kept_second, got_second)
        got = [swap(one, "dp", count) for one in sent]
        out_got, feed_got = together(out_got, feed_got)
        out_send, out_buf = output_call(where, residual, out_m, out_got)
        got, out_send = together(got, out_send)
        sent, kept = halve_rows_call(where, kept, *got)
        sent, out_send = together(sent, out_send)
        got = swap(sent, "dp", 2 * count)
        out_back = swap(out_send, "seq", 2)
        grad_up, grad_down = feed_sums(feed_own, feed_got)
        grad_down = exchanged(grad_down)
        got, tok_back, out_back = together(got, tok_back, out_back)
        sent, mine = stage_five_call(where, kept, got, pairs)
        other = swap(sent, "seq", 2)
        *ordered, sums0, sums1, sums2, sums3, grad_down = stage_six_call(where, mine, other, grad_down)
        sums, grad_down = (sums0, sums1, sums2, sums3), grad_down.T
    else:
        piece0, piece1, piece2, piece3 = pieces
        shape = (2, 2, width // 16, -1)
        sides = jnp.stack([piece0, piece1]).reshape((2,) + shape)
        sides = jnp.stack([pick(sides, jnp.where(side == k, 1, 0)) for k in (0, 1)], 1)
        halves = jnp.stack([piece2, piece3]).reshape((2,) + shape)
        halves = jnp.stack([pick(halves, jnp.where(row == k, 1, 0)) for k in (0, 1)], 2)
        summed = jnp.stack([sides, halves], 1).reshape(width, pairs, 4, LANES).transpose(0, 2, 1, 3)
        summed = summed.reshape(width, 4, 2, group)
        other = swap(pick(summed, 1 - row, 2), "seq", 2).astype(F32)
        summed = (pick(summed, row, 2).astype(F32) + other).astype(BF16).reshape(width, -1)
        ordered = lax.psum_scatter(summed, "dp", scatter_dimension=0, tiled=True).astype(F32)
        tok_back = swap(tok_send, "seq", 2)
        out_got = [swap(one, "seq", 1) for one in out_o]
        out_send, out_buf = output_call(where, residual, out_m, out_got)
        out_back = swap(out_send, "seq", 2)
        feed_sent, feed_own = halved(feed_kept, feed_got)
        grad_up, grad_down = feed_sums(feed_own, swap(feed_sent, "dp", 2 * count))
        grad_down = exchanged(grad_down).astype(F32).T
        sums = sums + sums_got
        sums = sums + swap(sums, "seq", 2)
        bit = 1
        while bit < n_dp:
            sums = sums + swap(sums, "dp", bit)
            bit *= 2
        ordered = [ordered[:, k * group : (k + 1) * group] for k in range(4)]

    output = lax.dynamic_update_slice(out_buf, out_back[None], (1 - row, 0, 0))
    grad_tokens = lax.dynamic_update_slice(tok_buf, tok_back[None], (1 - row, 0, 0))
    return (
        output,
        grad_tokens,
        sums[0],
        sums[1],
        ordered[0],
        ordered[1],
        ordered[2],
        ordered[3],
        sums[2],
        sums[3],
        grad_up,
        grad_down,
    )


def solution(mesh):
    tokens = P("dp", "seq", None)
    weights = P("dp", "seq")
    return jax.shard_map(
        local,
        mesh=mesh,
        in_specs=(tokens,) + (P(),) * 10 + (tokens, P("dp")),
        out_specs=(tokens, tokens, P(), P(), weights, weights, weights, weights, P(), P(), weights, weights),
        check_vma=False,
    )
```
